32 devices in a mesh: seq: 4 (over y, x), chan: 8 (over z, core).
Axes of the slice: x: 2, y: 2, z: 4, core: 2. Of those that a mesh axis runs over, the one named last changes fastest.
Arguments:
- residual: bfloat16 [16384, 2048], P(('seq', 'chan')), may hold values from -6 to 6
- cotangent: bfloat16 [16384, 2048], P(('seq', 'chan')), may hold values from -6 to 6
- resets: int32 [16384], P('seq'), may hold values 0 or 1
- branch_weights: bfloat16 [2048, 2, 2560], P(None, None, 'chan'), may hold values from -0.125 to 0.125
- gate_blocks: bfloat16 [2, 16, 160, 160], P(None, 'chan'), may hold values from -0.5 to 0.5
- mixer_weights: bfloat16 [2560, 2048], P('chan'), may hold values from -0.3125 to 0.3125
- expand_weights: bfloat16 [2048, 2, 6144], P(None, None, 'chan'), may hold values from -0.125 to 0.125
- shrink_weights: bfloat16 [6144, 2048], P('chan'), may hold values from -0.109375 to 0.109375
- branch_state: float32 [4, 2048, 2, 2560], P(None, 'seq', None, 'chan'), as said below
- gate_state: float32 [4, 2, 16, 160, 160], P(None, None, 'chan', 'seq'), as said below
- mixer_state: float32 [4, 2560, 2048], P(None, 'chan', 'seq'), as said below
- expand_state: float32 [4, 2048, 2, 6144], P(None, 'seq', None, 'chan'), as said below
- shrink_state: float32 [4, 6144, 2048], P(None, 'chan', 'seq'), as said below
- channel_state: float32 [4, 8, 2560], P(None, None, 'chan'), as said below
- gains_state: float32 [4, 2, 2048], replicated, as said below
Outputs:
- output: bfloat16 [16384, 2048], P(('seq', 'chan'))
- residual_grad: float32 [16384, 2048], P(('seq', 'chan'))
- branch_grad: float32 [2048, 2, 2560], P('seq', None, 'chan')
- gate_grad: float32 [2, 16, 160, 160], P(None, 'chan', 'seq')
- mixer_grad: float32 [2560, 2048], P('chan', 'seq')
- expand_grad: float32 [2048, 2, 6144], P('seq', None, 'chan')
- shrink_grad: float32 [6144, 2048], P('chan', 'seq')
- channel_grad: float32 [8, 2560], P(None, 'chan')
- gains_grad: float32 [2, 2048], replicated
- grad_norm: float32 [], replicated
- branch_new: float32 [4, 2048, 2, 2560], P(None, 'seq', None, 'chan')
- gate_new: float32 [4, 2, 16, 160, 160], P(None, None, 'chan', 'seq')
- mixer_new: float32 [4, 2560, 2048], P(None, 'chan', 'seq')
- expand_new: float32 [4, 2048, 2, 6144], P(None, 'seq', None, 'chan')
- shrink_new: float32 [4, 6144, 2048], P(None, 'chan', 'seq')
- channel_new: float32 [2, 8, 2560], P(None, None, 'chan')
- channel_moments: float32 [2, 8, 2560], P(None, None, 'chan')
- gains_new: float32 [4, 2, 2048], replicated
- branch_copy: bfloat16 [2048, 2, 2560], P('seq', None, 'chan')
- gate_copy: bfloat16 [2, 16, 160, 160], P(None, 'chan', 'seq')
- mixer_copy: bfloat16 [2560, 2048], P('chan', 'seq')
- expand_copy: bfloat16 [2048, 2, 6144], P('seq', None, 'chan')
- shrink_copy: bfloat16 [6144, 2048], P('chan', 'seq')
The draws below stay inside these ranges and needn't reach their ends.
Inputs may be any that keep to these rules, and one draw needn't show every extreme that they name: `branch_state`: index 0 holds master weights, 1 first moments, 2 second moments (positive), 3 the weight average. `gate_state`: index 0 holds master weights, 1 first moments, 2 second moments (positive), 3 the weight average. `mixer_state`: index 0 holds master weights, 1 first moments, 2 second moments (positive), 3 the weight average. `expand_state`: index 0 holds master weights, 1 first moments, 2 second moments (positive), 3 the weight average. `shrink_state`: index 0 holds master weights, 1 first moments, 2 second moments (positive), 3 the weight average. `channel_state`: index 0 holds master values, 1 first moments, 2 second moments (positive), 3 the average; the decay parameter row is negative. `gains_state`: index 0 holds the gains' offsets from 1, 1 first moments, 2 second moments (positive), 3 the average.
All inputs are finite; a program needn't handle non-finite values. No bound on the sum of `resets` on one device may be relied on, other than what follows from the above.
Results may differ from the reference program's by a relative error of at most 0.02.
Values may be sent and summed in bfloat16 or wider, within the bound.
No kernel may reach another device: no remote copies, remote signals or barrier semaphores. Data moves between devices by JAX's collectives and lax.ppermute only.
A program may use at most 384 MiB of HBM per device.

```python
import math
import jax
import jax.numpy as jnp
from jax import lax

D = 2048
H = 16
BW = 160
W = 2560
F = 6144
CONV = 4
SEQ_LEN = 2048
SEQS = 2
STEP = 10
TOKENS = 16384
PARAMS = 54321152
N_SEQ = 4


def noise_draw(key, shape):
    return jax.random.normal(key, shape, jnp.float32)


def state_from_master(key, master, spread, grad_size):
    parts = jax.random.split(key, 3)
    shape = master.shape
    first = 0.11 * grad_size * noise_draw(parts[0], shape)
    second = 0.05 / 0.95 * grad_size * grad_size * jax.random.uniform(parts[1], shape, jnp.float32, 1.0, 4.0)
    average = master + 0.2 * spread * noise_draw(parts[2], shape)
    return jnp.stack([master, first, second, average])


def matrix_state(key, shape, spread, grad_size):
    parts = jax.random.split(jax.random.fold_in(key, 11), 2)
    master = spread * noise_draw(parts[0], shape)
    return state_from_master(parts[1], master, spread, grad_size)


def draw_branch_state(key, part):
    return matrix_state(key, (D, 2, W), D ** (-0.5), 0.35)


def draw_gate_state(key, part):
    return matrix_state(key, (2, H, BW, BW), BW ** (-0.5), 0.67)


def draw_mixer_state(key, part):
    return matrix_state(key, (W, D), W ** (-0.5), 0.34)


def draw_expand_state(key, part):
    return matrix_state(key, (D, 2, F), D ** (-0.5), 0.35)


def draw_shrink_state(key, part):
    return matrix_state(key, (F, D), F ** (-0.5), 0.27)


def draw_channel_state(key, part):
    parts = jax.random.split(jax.random.fold_in(key, 23), 6)
    taps = 0.5 * noise_draw(parts[0], (CONV, W))
    conv_bias = 0.3 * noise_draw(parts[1], (1, W))
    gate_bias = 0.5 * noise_draw(parts[2], (1, W))
    input_bias = 0.5 * noise_draw(parts[3], (1, W))
    lru_param = jax.random.uniform(parts[4], (1, W), jnp.float32, -7.0, -3.5)
    master = jnp.concatenate([taps, conv_bias, gate_bias, input_bias, lru_param], axis=0)
    grad_sizes = jnp.concatenate([jnp.full((CONV + 3, 1), 1.0, jnp.float32), jnp.full((1, 1), 0.02, jnp.float32)], axis=0)
    return state_from_master(parts[5], master, 0.5, grad_sizes)


def draw_gains_state(key, part):
    parts = jax.random.split(jax.random.fold_in(key, 37), 2)
    master = 0.3 * noise_draw(parts[0], (2, D))
    grad_sizes = jnp.concatenate([jnp.full((1, 1), 1.2, jnp.float32), jnp.full((1, 1), 0.7, jnp.float32)], axis=0)
    return state_from_master(parts[1], master, 0.3, grad_sizes)


def with_ends(array, key, smallest, high):
    place = [jax.random.randint(jax.random.fold_in(key, axis), (), 0, length) for axis, length in enumerate(array.shape)]
    longest = array.shape.index(max(array.shape))
    next_to = place[:longest] + [(place[longest] + 1) % array.shape[longest]] + place[longest + 1:]
    return array.at[tuple(place)].set(smallest).at[tuple(next_to)].set(high)


def steps_of(rng, dims, cuts, least, top_value):
    def one(dim, shards_of):
        heights = jax.random.uniform(jax.random.fold_in(jax.random.fold_in(rng, 6), dim), (shards_of,), jnp.float32, least / len(cuts), top_value / len(cuts))
        return jnp.repeat(jnp.exp(heights), dims[dim] // shards_of).reshape((-1,) + (1,) * (len(dims) - dim - 1))

    loudness = one(*cuts[0])
    for cut in cuts[1:]:
        loudness = loudness * one(*cut)
    return loudness


def noise(key, extent, scale, reach, cuts=(), dtype=jnp.bfloat16):
    values = jax.random.normal(key, extent, jnp.float32) * scale
    if len(cuts) > 0:
        values = steps_of(key, extent, cuts, -0.22, 0.18) * values
    return jnp.clip(values, min=-reach, max=reach).astype(dtype)


def setup_inputs(seed: int = 0) -> dict:
    keys = jax.random.split(jax.random.key(seed), 16)
    residual = noise(keys[0], (TOKENS, D), 1.0, 6.0, ((0, 32),))
    cotangent = noise(keys[1], (TOKENS, D), 1.0, 6.0, ((0, 32),))
    resets = with_ends((jax.random.randint(keys[2], (TOKENS,), 0, 512) < 1).astype(jnp.int32), jax.random.fold_in(keys[2], 1), 0, 1)
    branch_weights = noise(keys[3], (D, 2, W), D ** -0.5, 0.125, ((2, 8),))
    gate_blocks = noise(keys[4], (2, H, BW, BW), BW ** -0.5, 0.5, ((1, 8),))
    mixer_weights = noise(keys[5], (W, D), (W // 8) ** -0.5, 0.3125, ((0, 8),))
    expand_weights = noise(keys[6], (D, 2, F), D ** -0.5, 0.125, ((2, 8),))
    shrink_weights = noise(keys[7], (F, D), (F // 2) ** -0.5, 0.109375, ((0, 8),))
    branch_state = draw_branch_state(jax.random.fold_in(keys[15], 71), 0)
    gate_state = draw_gate_state(jax.random.fold_in(keys[15], 71), 0)
    mixer_state = draw_mixer_state(jax.random.fold_in(keys[15], 71), 0)
    expand_state = draw_expand_state(jax.random.fold_in(keys[15], 71), 0)
    shrink_state = draw_shrink_state(jax.random.fold_in(keys[15], 71), 0)
    channel_state = draw_channel_state(jax.random.fold_in(keys[15], 71), 0)
    gains_state = draw_gains_state(jax.random.fold_in(keys[15], 71), 0)
    return dict(residual=residual, cotangent=cotangent, resets=resets, branch_weights=branch_weights, gate_blocks=gate_blocks, mixer_weights=mixer_weights, expand_weights=expand_weights, shrink_weights=shrink_weights, branch_state=branch_state, gate_state=gate_state, mixer_state=mixer_state, expand_state=expand_state, shrink_state=shrink_state, channel_state=channel_state, gains_state=gains_state)


norm_eps = 1e-06
lru_scale = 8.0
clip_rms = 0.4
beta_one = 0.9
beta_two = 0.95
adam_eps = 1e-08
weight_decay = 0.1
ema_keep = 0.99
rate_matrix = 0.02
rate_gate = 0.1
rate_channel = 1.0
rate_gains = 0.5
highest = lax.Precision.HIGHEST

@jax.custom_vjp
def low(v):
    return lax.optimization_barrier(v.astype(jnp.bfloat16)).astype(jnp.float32)

@jax.custom_vjp
def low_back(v):
    return v

def low_keep(v):
    return (low(v), None)

def low_pass(kept, grad):
    return (grad,)

def back_keep(v):
    return (v, None)

def back_low(kept, grad):
    return (low(grad),)
low.defvjp(low_keep, low_pass)
low_back.defvjp(back_keep, back_low)

def shifted(values, offset):
    if offset == 0:
        return values
    length = values.shape[1]
    return jnp.pad(values, ((0, 0), (offset, 0), (0, 0)))[:, :length, :]

def doc_positions(flag_block):
    step_index = lax.broadcasted_iota(jnp.int32, flag_block.shape, 1)
    starting = jnp.logical_or(flag_block == 1, step_index == 0)
    latest = lax.cummax(jnp.where(starting, step_index, 0), axis=1)
    return (starting, step_index - latest)

def forward(weights, row_block, flag_block):
    branch_w, gate_w, mixer_w, expand_w, shrink_w, channel, gains = weights
    starting, inside = doc_positions(flag_block)
    retain_mask = (1.0 - starting.astype(jnp.float32))[:, :, None]
    scale_one = lax.rsqrt(lax.optimization_barrier(jnp.mean(row_block * row_block, axis=-1, keepdims=True)) + norm_eps)
    normed_one = low(row_block * scale_one * (1.0 + gains[0]))
    projected = jnp.einsum('rd,dbw->rbw', normed_one, branch_w, precision=highest)
    gate_branch = low_back(projected[:, 0, :])
    recur_input = low_back(projected[:, 1, :]).reshape(SEQS, SEQ_LEN, W)
    convolved = channel[CONV] + jnp.zeros((SEQS, SEQ_LEN, W), jnp.float32)
    for offset in range(CONV):
        valid = (inside >= offset).astype(jnp.float32)[:, :, None]
        convolved = convolved + channel[offset] * shifted(recur_input, offset) * valid
    conv_low = low(convolved)
    blocked = conv_low.reshape(SEQS, SEQ_LEN, H, BW)
    gate_pre = low_back(jnp.einsum('slhi,hij->slhj', blocked, gate_w[0], precision=highest).reshape(SEQS, SEQ_LEN, W) + channel[CONV + 1])
    input_pre = low_back(jnp.einsum('slhi,hij->slhj', blocked, gate_w[1], precision=highest).reshape(SEQS, SEQ_LEN, W) + channel[CONV + 2])
    recur_gate = jax.nn.sigmoid(gate_pre)
    input_gate = jax.nn.sigmoid(input_pre)
    log_decay = -lru_scale * jax.nn.softplus(channel[CONV + 3]) * recur_gate
    decay_rate = jnp.exp(log_decay)
    norm_term = jnp.sqrt(-jnp.expm1(2.0 * log_decay))
    coeff_term = decay_rate * retain_mask
    drive_term = norm_term * input_gate * conv_low

    def advance(hidden_state, inputs_now):
        new_state = inputs_now[0] * hidden_state + inputs_now[1]
        return (new_state, new_state)
    final_state, states = lax.scan(advance, jnp.zeros((SEQS, W), jnp.float32), (jnp.moveaxis(coeff_term, 1, 0), jnp.moveaxis(drive_term, 1, 0)))
    hidden = jnp.moveaxis(states, 0, 1)
    mixed = low((jax.nn.gelu(gate_branch).reshape(SEQS, SEQ_LEN, W) * hidden).reshape(SEQS * SEQ_LEN, W))
    mixer_out = low_back(jnp.dot(mixed, mixer_w, precision=highest))
    middle = row_block + mixer_out
    scale_two = lax.rsqrt(lax.optimization_barrier(jnp.mean(middle * middle, axis=-1, keepdims=True)) + norm_eps)
    normed_two = low(middle * scale_two * (1.0 + gains[1]))
    expanded = jnp.einsum('rd,dbf->rbf', normed_two, expand_w, precision=highest)
    gate_part = low_back(expanded[:, 0, :])
    up_part = low_back(expanded[:, 1, :])
    product = low(jax.nn.gelu(gate_part) * up_part)
    return middle + jnp.dot(product, shrink_w, precision=highest)

def adam(old_state, gradient, factor, step_rate, decay_use):
    clipped = gradient * factor
    moment_one = beta_one * old_state[1] + (1.0 - beta_one) * clipped
    moment_two = beta_two * old_state[2] + (1.0 - beta_two) * clipped * clipped
    first_hat = moment_one / (1.0 - beta_one ** STEP)
    second_hat = moment_two / (1.0 - beta_two ** STEP)
    master = old_state[0] - step_rate * (first_hat / (jnp.sqrt(second_hat) + adam_eps) + decay_use * old_state[0])
    average = ema_keep * old_state[3] + (1.0 - ema_keep) * master
    return (jnp.stack([master, moment_one, moment_two, average]), master)

def add_pair(former, latter):
    return former + latter

def reference(residual, cotangent, resets, branch_weights, gate_blocks, mixer_weights, expand_weights, shrink_weights, branch_state, gate_state, mixer_state, expand_state, shrink_state, channel_state, gains_state):
    weights = (branch_weights.astype(jnp.float32), gate_blocks.astype(jnp.float32), mixer_weights.astype(jnp.float32), expand_weights.astype(jnp.float32), shrink_weights.astype(jnp.float32), channel_state[0], gains_state[0])
    group_rows = SEQS * SEQ_LEN
    rows_all = residual.astype(jnp.float32).reshape(N_SEQ, group_rows, D)
    backs_all = cotangent.astype(jnp.float32).reshape(N_SEQ, group_rows, D)
    flags_all = resets.reshape(N_SEQ, SEQS, SEQ_LEN)

    def group_step(totals, inputs_now):
        row_block, back_block, flag_block = inputs_now

        def local_forward(params, values):
            return forward(params, values, flag_block)
        result, pullback = jax.vjp(local_forward, weights, row_block)
        weight_grads, row_grads = pullback(back_block)
        return (jax.tree.map(add_pair, totals, weight_grads), (result, row_grads))
    initial = jax.tree.map(jnp.zeros_like, weights)
    totals, (results, row_grads) = lax.scan(group_step, initial, (rows_all, backs_all, flags_all))
    output = results.reshape(TOKENS, D).astype(jnp.bfloat16)
    residual_grad = row_grads.reshape(TOKENS, D)
    branch_grad, gate_grad, mixer_grad, expand_grad, shrink_grad, channel_grad, gains_grad = totals
    squares = jnp.zeros((), jnp.float32)
    for entry in totals:
        squares = squares + jnp.sum(entry * entry)
    grad_norm = jnp.sqrt(squares)
    clip_limit = clip_rms * math.sqrt(PARAMS)
    factor = jnp.minimum(1.0, clip_limit / (grad_norm + 1e-06))
    branch_new, branch_master = adam(branch_state, branch_grad, factor, rate_matrix, weight_decay)
    gate_new, gate_master = adam(gate_state, gate_grad, factor, rate_gate, weight_decay)
    mixer_new, mixer_master = adam(mixer_state, mixer_grad, factor, rate_matrix, weight_decay)
    expand_new, expand_master = adam(expand_state, expand_grad, factor, rate_matrix, weight_decay)
    shrink_new, shrink_master = adam(shrink_state, shrink_grad, factor, rate_matrix, weight_decay)
    channel_full, channel_master = adam(channel_state, channel_grad, factor, rate_channel, 0.0)
    gains_new, gains_master = adam(gains_state, gains_grad, factor, rate_gains, 0.0)
    channel_new = jnp.stack([channel_full[0], channel_full[3]])
    channel_moments = channel_full[1:3]
    return (output, residual_grad, branch_grad, gate_grad, mixer_grad, expand_grad, shrink_grad, channel_grad, gains_grad, grad_norm, branch_new, gate_new, mixer_new, expand_new, shrink_new, channel_new, channel_moments, gains_new, branch_master.astype(jnp.bfloat16), gate_master.astype(jnp.bfloat16), mixer_master.astype(jnp.bfloat16), expand_master.astype(jnp.bfloat16), shrink_master.astype(jnp.bfloat16))
```

```python
import math

import jax
import jax.numpy as jnp
from jax import lax
from jax.experimental import pallas as pl
from jax.experimental.pallas import tpu as pltpu
from jax.sharding import PartitionSpec as P

CONV = 4
SEQ_LEN = 2048
SEQS = 2
STEP = 10
PARAMS = 54321152


norm_eps = 1e-06
lru_scale = 8.0
clip_rms = 0.4
beta_one = 0.9
beta_two = 0.95
adam_eps = 1e-08
weight_decay = 0.1
ema_keep = 0.99
rate_matrix = 0.02
rate_gate = 0.1
rate_channel = 1.0
rate_gains = 0.5
SUB = 8
TILE = 16
GELU_SCALE = math.sqrt(2.0 / math.pi)
GELU_CUBE = 0.044715


def contract_rows(left_mat, right_mat):
    return lax.dot_general(
        left_mat, right_mat, (((0,), (0,)), ((), ())), preferred_element_type=jnp.float32
    )


def contract_cols(left_mat, right_mat):
    return lax.dot_general(
        left_mat, right_mat, (((1,), (1,)), ((), ())), preferred_element_type=jnp.float32
    )


def contract(left_mat, right_mat):
    return jnp.dot(left_mat, right_mat, preferred_element_type=jnp.float32)


def norm_back(values, scale, gain, upstream):
    scaled = gain * upstream
    return scale * scaled - values * scale * scale * scale * jnp.mean(
        scaled * values, axis=-1, keepdims=True
    )


def adam(old_state, gradient, factor, step_rate, decay_use):
    clipped = gradient * factor
    moment_one = beta_one * old_state[1] + (1.0 - beta_one) * clipped
    moment_two = beta_two * old_state[2] + (1.0 - beta_two) * clipped * clipped
    first_hat = moment_one / (1.0 - beta_one**STEP)
    second_hat = moment_two / (1.0 - beta_two**STEP)
    master = old_state[0] - step_rate * (
        first_hat / (jnp.sqrt(second_hat) + adam_eps) + decay_use * old_state[0]
    )
    average = ema_keep * old_state[3] + (1.0 - ema_keep) * master
    return (jnp.stack([master, moment_one, moment_two, average]), master)


def gelu_parts(values):
    square = values * values
    turn = jnp.tanh(GELU_SCALE * values * (1.0 + GELU_CUBE * square))
    half = 0.5 * (1.0 + turn)
    slope = half + 0.5 * values * (1.0 - turn * turn) * (
        GELU_SCALE * (1.0 + 3.0 * GELU_CUBE * square)
    )
    return values * half, slope


def decay_parts(log_decay):
    decay = jnp.exp(log_decay)
    z = 2.0 * log_decay
    series = 1.0 + z * (1.0 / 7.0)
    for order in (6.0, 5.0, 4.0, 3.0, 2.0):
        series = 1.0 + z * (1.0 / order) * series
    return decay, jnp.where(z > -0.35, -z * series, 1.0 - decay * decay)


def roll_down(values, offset):
    return pltpu.roll(values, offset, 0)


def roll_up(values, offset):
    return pltpu.roll(values, SUB - offset, 0)


def lru_forward_kernel(
    place_ref,
    gate_ref,
    recur_ref,
    mask_ref,
    rate_w_ref,
    input_w_ref,
    par_ref,
    mixed_ref,
    hidden_ref,
    conv_ref,
    rate_ref,
    admit_ref,
    rate_pre,
    input_pre,
    tail,
    state,
):
    block, width = gate_ref.shape

    @pl.when(pl.program_id(0) == 0)
    def _():
        tail[...] = jnp.zeros_like(tail)
        state[...] = jnp.zeros_like(state)

    row = lax.broadcasted_iota(jnp.int32, (SUB, width), 0)

    def convolve(step, before):
        base = pl.multiple_of(step * TILE, TILE)
        halves = []
        for half in range(2):
            rows = pl.ds(base + half * SUB, SUB)
            now = recur_ref[rows, :]
            masks = mask_ref[rows, :]
            total = par_ref[CONV : CONV + 1, :] + par_ref[0:1, :] * now
            for offset in range(1, CONV):
                moved = jnp.where(
                    row < offset, roll_down(before, offset), roll_down(now, offset)
                )
                total = total + par_ref[offset : offset + 1, :] * (
                    moved * masks[:, offset - 1 : offset]
                )
            halves.append(total)
            before = now
        conv_ref[pl.ds(base, TILE), :] = jnp.concatenate(halves, axis=0).astype(jnp.bfloat16)
        return before

    tail[...] = lax.fori_loop(0, block // TILE, convolve, tail[...])
    low = conv_ref[...]
    rate_pre[...] = contract(low, rate_w_ref[...])
    input_pre[...] = contract(low, input_w_ref[...])

    def advance(step, carry):
        base = pl.multiple_of(step * TILE, TILE)
        conv = conv_ref[pl.ds(base, TILE), :].astype(jnp.float32)
        halves = []
        for half in range(2):
            rows = pl.ds(base + half * SUB, SUB)
            rate = jax.nn.sigmoid(rate_pre[rows, :] + par_ref[CONV + 1 : CONV + 2, :])
            admit = jax.nn.sigmoid(input_pre[rows, :] + par_ref[CONV + 2 : CONV + 3, :])
            decay, rest = decay_parts(par_ref[CONV + 3 : CONV + 4, :] * rate)
            coeff = decay * mask_ref[rows, 0:1]
            drive = jnp.sqrt(rest) * admit * conv[half * SUB : (half + 1) * SUB, :]
            for offset in (1, 2, 4):
                inner = row >= offset
                drive = drive + coeff * jnp.where(inner, roll_down(drive, offset), 0.0)
                coeff = coeff * jnp.where(inner, roll_down(coeff, offset), 1.0)
            hidden = drive + coeff * carry
            carry = jnp.broadcast_to(hidden[SUB - 1 : SUB, :], hidden.shape)
            hidden_ref[rows, :] = hidden
            rate_ref[rows, :] = rate
            admit_ref[rows, :] = admit
            branch = gate_ref[rows, :]
            turn = jnp.tanh(GELU_SCALE * branch * (1.0 + GELU_CUBE * branch * branch))
            halves.append(0.5 * branch * (1.0 + turn) * hidden)
        mixed_ref[pl.ds(base, TILE), :] = jnp.concatenate(halves, axis=0).astype(jnp.bfloat16)
        return carry

    state[...] = lax.fori_loop(0, block // TILE, advance, state[...])


def lru_backward_kernel(
    place_ref,
    upstream_ref,
    gate_ref,
    recur_ref,
    hidden_ref,
    before_ref,
    conv_ref,
    rate_ref,
    admit_ref,
    mask_ref,
    rate_w_ref,
    input_w_ref,
    par_ref,
    gate_back_ref,
    recur_back_ref,
    rate_grad_ref,
    input_grad_ref,
    sums_ref,
    rate_low,
    input_low,
    conv_back,
    state,
    ahead,
):
    block, width = gate_ref.shape
    steps = block // TILE

    @pl.when(pl.program_id(0) == 0)
    def _():
        state[...] = jnp.zeros_like(state)
        ahead[...] = jnp.zeros_like(ahead)
        sums_ref[...] = jnp.zeros_like(sums_ref)
        rate_grad_ref[...] = jnp.zeros_like(rate_grad_ref)
        input_grad_ref[...] = jnp.zeros_like(input_grad_ref)

    row = lax.broadcasted_iota(jnp.int32, (SUB, width), 0)

    def retreat(step, carry):
        carried_next, coeff_next = carry
        index = steps - 1 - step
        base = pl.multiple_of(index * TILE, TILE)
        conv_tile = conv_ref[pl.ds(base, TILE), :].astype(jnp.float32)
        halves = [None, None, None]
        lows = [[None, None] for _ in range(3)]
        edge = pl.multiple_of(jnp.maximum(base - SUB, 0), SUB)
        earlier = jnp.where(index == 0, before_ref[...], hidden_ref[pl.ds(edge, SUB), :])
        for half in (1, 0):
            rows = pl.ds(base + half * SUB, SUB)
            conv = conv_tile[half * SUB : (half + 1) * SUB, :]
            rate = rate_ref[rows, :]
            admit = admit_ref[rows, :]
            speed = par_ref[CONV + 3 : CONV + 4, :]
            decay, rest = decay_parts(speed * rate)
            inverse = lax.rsqrt(rest)
            norm = rest * inverse
            coeff = decay * mask_ref[rows, 0:1]
            act, slope = gelu_parts(gate_ref[rows, :])
            upstream = upstream_ref[rows, :]
            hidden = hidden_ref[rows, :]
            carried = upstream * act
            chain = jnp.where(row == SUB - 1, coeff_next, roll_up(coeff, 1))
            for offset in (1, 2, 4):
                inner = row < SUB - offset
                carried = carried + chain * jnp.where(inner, roll_up(carried, offset), 0.0)
                chain = chain * jnp.where(inner, roll_up(chain, offset), 1.0)
            carried = carried + chain * carried_next
            carried_next = jnp.broadcast_to(carried[0:1, :], carried.shape)
            coeff_next = jnp.broadcast_to(coeff[0:1, :], coeff.shape)
            if half == 1:
                last = hidden_ref[pl.ds(base, SUB), :]
            else:
                last = earlier
            previous = jnp.where(row == 0, roll_down(last, 1), roll_down(hidden, 1))
            log_grad = carried * (
                previous * coeff - admit * conv * (decay * decay) * inverse
            )
            rate_back = log_grad * speed * rate * (1.0 - rate)
            drive = carried * norm
            direct = drive * admit
            input_back = drive * conv * admit * (1.0 - admit)
            conv_back[rows, :] = direct
            lows[0][half] = upstream * hidden * slope
            lows[1][half] = rate_back
            lows[2][half] = input_back
            sums_ref[5] += rate_back
            sums_ref[6] += input_back
            sums_ref[7] += log_grad * rate
        tile = pl.ds(base, TILE)
        gate_back_ref[tile, :] = jnp.concatenate(lows[0], axis=0).astype(jnp.bfloat16)
        rate_low[tile, :] = jnp.concatenate(lows[1], axis=0).astype(jnp.bfloat16)
        input_low[tile, :] = jnp.concatenate(lows[2], axis=0).astype(jnp.bfloat16)
        return carried_next, coeff_next

    carried_next, coeff_next = lax.fori_loop(0, steps, retreat, (state[0], state[1]))
    state[0] = carried_next
    state[1] = coeff_next
    low = conv_ref[...]
    rate_back_low = rate_low[...]
    input_back_low = input_low[...]
    rate_grad_ref[...] += contract_rows(low, rate_back_low)
    input_grad_ref[...] += contract_rows(low, input_back_low)
    conv_back[...] += contract_cols(rate_back_low, rate_w_ref[...]) + contract_cols(
        input_back_low, input_w_ref[...]
    )

    def unconvolve(step, carry):
        base = pl.multiple_of((steps - 1 - step) * TILE, TILE)
        halves = [None, None]
        nexts = list(carry)
        for half in (1, 0):
            rows = pl.ds(base + half * SUB, SUB)
            grad = conv_back[rows, :]
            now = recur_ref[rows, :]
            masks = mask_ref[rows, :]
            sums_ref[0] += grad * now
            sums_ref[CONV] += grad
            total = par_ref[0:1, :] * grad
            for offset in range(1, CONV):
                kept = grad * masks[:, offset - 1 : offset]
                moved = jnp.where(
                    row < SUB - offset, roll_up(kept, offset), roll_up(nexts[offset - 1], offset)
                )
                nexts[offset - 1] = kept
                sums_ref[offset] += moved * now
                total = total + par_ref[offset : offset + 1, :] * moved
            halves[half] = total
        recur_back_ref[pl.ds(base, TILE), :] = jnp.concatenate(halves, axis=0).astype(jnp.bfloat16)
        return tuple(nexts)

    nexts = lax.fori_loop(0, steps, unconvolve, tuple(ahead[k] for k in range(CONV - 1)))
    for k in range(CONV - 1):
        ahead[k] = nexts[k]


def lru_sizes(rows, width, piece):
    block = min(256, piece)
    return block, rows // block, piece // block


def lru_forward(place, gate_branch, recur_input, masks, rate_w, input_w, params, piece):
    rows, width = gate_branch.shape
    block, count, per = lru_sizes(rows, width, piece)

    def there(i, place_ref):
        return (((i // per) ^ place_ref[0]) * per + i % per, 0)

    def here(i, place_ref):
        return (i, 0)

    def fixed(i, place_ref):
        return (0, 0)

    tall = lambda where: pl.BlockSpec((block, width), where)
    square = pl.BlockSpec((width, width), fixed)
    return pl.pallas_call(
        lru_forward_kernel,
        grid_spec=pltpu.PrefetchScalarGridSpec(
            num_scalar_prefetch=1,
            grid=(count,),
            in_specs=[
                tall(there),
                tall(there),
                pl.BlockSpec((block, SUB), here),
                square,
                square,
                pl.BlockSpec((2 * CONV, width), fixed),
            ],
            out_specs=[tall(there), tall(here), tall(here), tall(here), tall(here)],
            scratch_shapes=[
                pltpu.VMEM((block, width), jnp.float32),
                pltpu.VMEM((block, width), jnp.float32),
                pltpu.VMEM((SUB, width), jnp.float32),
                pltpu.VMEM((SUB, width), jnp.float32),
            ],
        ),
        out_shape=[
            jax.ShapeDtypeStruct((rows, width), jnp.bfloat16),
            jax.ShapeDtypeStruct((rows, width), jnp.float32),
            jax.ShapeDtypeStruct((rows, width), jnp.bfloat16),
            jax.ShapeDtypeStruct((rows, width), jnp.float32),
            jax.ShapeDtypeStruct((rows, width), jnp.float32),
        ],
        compiler_params=pltpu.CompilerParams(
            dimension_semantics=("arbitrary",), vmem_limit_bytes=48 * 2**20
        ),
        cost_estimate=pl.CostEstimate(
            flops=4 * rows * width * width,
            bytes_accessed=26 * rows * width,
            transcendentals=6 * rows * width,
        ),
        name="lru_forward",
    )(place, gate_branch, recur_input, masks, rate_w, input_w, params)


def lru_backward(
    place, upstream, gate_branch, recur_input, hidden, conv, rate, admit, masks, rate_w, input_w,
    params, piece,
):
    rows, width = gate_branch.shape
    block, count, per = lru_sizes(rows, width, piece)

    def there(i, place_ref):
        t = count - 1 - i
        return (((t // per) ^ place_ref[0]) * per + t % per, 0)

    def here(i, place_ref):
        return (count - 1 - i, 0)

    def before(i, place_ref):
        return (jnp.maximum((count - 1 - i) * (block // SUB) - 1, 0), 0)

    def fixed(i, place_ref):
        return (0, 0)

    tall = lambda where: pl.BlockSpec((block, width), where)
    square = pl.BlockSpec((width, width), fixed)
    return pl.pallas_call(
        lru_backward_kernel,
        grid_spec=pltpu.PrefetchScalarGridSpec(
            num_scalar_prefetch=1,
            grid=(count,),
            in_specs=[
                tall(there),
                tall(there),
                tall(there),
                tall(here),
                pl.BlockSpec((SUB, width), before),
                tall(here),
                tall(here),
                tall(here),
                pl.BlockSpec((block, SUB), here),
                square,
                square,
                pl.BlockSpec((2 * CONV, width), fixed),
            ],
            out_specs=[
                tall(there),
                tall(there),
                square,
                square,
                pl.BlockSpec((2 * CONV, SUB, width), lambda i, place_ref: (0, 0, 0)),
            ],
            scratch_shapes=[
                pltpu.VMEM((block, width), jnp.bfloat16),
                pltpu.VMEM((block, width), jnp.bfloat16),
                pltpu.VMEM((block, width), jnp.float32),
                pltpu.VMEM((2, SUB, width), jnp.float32),
                pltpu.VMEM((CONV - 1, SUB, width), jnp.float32),
            ],
        ),
        out_shape=[
            jax.ShapeDtypeStruct((rows, width), jnp.bfloat16),
            jax.ShapeDtypeStruct((rows, width), jnp.bfloat16),
            jax.ShapeDtypeStruct((width, width), jnp.float32),
            jax.ShapeDtypeStruct((width, width), jnp.float32),
            jax.ShapeDtypeStruct((2 * CONV, SUB, width), jnp.float32),
        ],
        compiler_params=pltpu.CompilerParams(
            dimension_semantics=("arbitrary",), vmem_limit_bytes=48 * 2**20
        ),
        cost_estimate=pl.CostEstimate(
            flops=8 * rows * width * width,
            bytes_accessed=30 * rows * width,
            transcendentals=6 * rows * width,
        ),
        name="lru_backward",
    )(
        place, upstream, gate_branch, recur_input, hidden, hidden, conv, rate, admit, masks,
        rate_w, input_w, params,
    )


def swap(values, axis, bit):
    return lax.ppermute(
        values, axis, [(i, i ^ bit) for i in range(lax.axis_size(axis))]
    )


def bits_of(size):
    return [1 << k for k in reversed(range(size.bit_length() - 1))]


def gather_rows(own, size):
    blocks = {0: own}
    for bit in bits_of(size):
        blocks.update({m | bit: swap(block, "chan", bit) for m, block in list(blocks.items())})
    return jnp.concatenate([blocks[m] for m in range(size)], axis=0)


def scatter_rows(partial, size):
    rows = partial.shape[0] // size
    blocks = {m: partial[m * rows : (m + 1) * rows] for m in range(size)}
    for bit in reversed(bits_of(size)):
        blocks = {
            m: block.astype(jnp.float32)
            + swap(blocks[m | bit].astype(jnp.bfloat16), "chan", bit).astype(jnp.float32)
            for m, block in blocks.items()
            if not m & bit
        }
    return blocks[0]


def block_diagonal(blocks):
    count, size, _ = blocks.shape
    return jnp.concatenate(
        [jnp.pad(blocks[k], ((0, 0), (k * size, (count - 1 - k) * size))) for k in range(count)],
        axis=0,
    )


def diagonal_blocks(matrix, count):
    size = matrix.shape[0] // count
    return jnp.stack(
        [matrix[k * size : (k + 1) * size, k * size : (k + 1) * size] for k in range(count)]
    )


def local(
    residual,
    cotangent,
    resets,
    branch_weights,
    gate_blocks,
    mixer_weights,
    expand_weights,
    shrink_weights,
    branch_state,
    gate_state,
    mixer_state,
    expand_state,
    shrink_state,
    channel_state,
    gains_state,
):
    seq_count = lax.axis_size("seq")
    group = lax.axis_size("chan") // SEQS
    seq_place = lax.axis_index("seq")
    chan_place = lax.axis_index("chan")
    place = (chan_place % group).astype(jnp.int32).reshape(1)
    width = residual.shape[1]
    piece = residual.shape[0]
    chan_width = branch_weights.shape[2]
    hidden_width = expand_weights.shape[2]
    block_count = gate_blocks.shape[1]

    def partner(values):
        return swap(values, "chan", group)

    def fetch(matrix):
        rows = matrix.shape[0] // seq_count
        part = lax.dynamic_slice_in_dim(matrix, seq_place * rows, rows, axis=0)
        return lax.all_gather(partner(part), "seq", axis=0, tiled=True)

    gains = gains_state[0]
    gain_first = 1.0 + gains[0]
    gain_second = 1.0 + gains[1]
    rows_float = residual.astype(jnp.float32)
    scale_one = lax.rsqrt(jnp.mean(rows_float * rows_float, axis=-1, keepdims=True) + norm_eps)
    normed_one = (rows_float * scale_one * gain_first).astype(jnp.bfloat16)
    normed_all = gather_rows(normed_one, group)

    own_branch = branch_weights.transpose(1, 2, 0)
    other_branch = fetch(own_branch.reshape(2 * chan_width, width)).reshape(own_branch.shape)
    branch_full = jnp.concatenate([own_branch, other_branch], axis=1)
    gate_full = jnp.concatenate([gate_blocks, partner(gate_blocks)], axis=1)
    rate_w = block_diagonal(gate_full[0])
    input_w = block_diagonal(gate_full[1])
    channel = channel_state[0]
    channel_full = jnp.concatenate([channel, partner(channel)], axis=1)
    speed = -lru_scale * jax.nn.softplus(channel_full[CONV + 3 :])
    params = jnp.concatenate([channel_full[: CONV + 3], speed], axis=0)
    mixer_full = jnp.concatenate([mixer_weights, fetch(mixer_weights)], axis=0)
    own_expand = expand_weights.reshape(width, 2 * hidden_width)
    other_expand = fetch(own_expand)
    expand_full = jnp.concatenate(
        [
            own_expand[:, :hidden_width],
            other_expand[:, :hidden_width],
            own_expand[:, hidden_width:],
            other_expand[:, hidden_width:],
        ],
        axis=1,
    )
    shrink_full = jnp.concatenate([shrink_weights, fetch(shrink_weights)], axis=0)
    pair_width = 2 * hidden_width

    flags = lax.dynamic_index_in_dim(
        resets.reshape(SEQS, SEQ_LEN), chan_place // group, axis=0, keepdims=False
    )
    stays = jnp.where(jnp.arange(SEQ_LEN) == 0, 0.0, 1.0 - (flags == 1).astype(jnp.float32))
    within = [stays]
    for offset in range(1, CONV - 1):
        within.append(within[-1] * jnp.pad(stays, (offset, 0))[:SEQ_LEN])
    masks = jnp.stack(within + [stays] * (SUB - len(within)), axis=1)

    gate_branch = contract_cols(normed_all, branch_full[0])
    recur_input = contract_cols(normed_all, branch_full[1])
    mixed, hidden, conv_low, rate, admit = lru_forward(
        place, gate_branch, recur_input, masks, rate_w, input_w, params, piece
    )
    middle = rows_float + scatter_rows(contract(mixed, mixer_full).astype(jnp.bfloat16), group)
    scale_two = lax.rsqrt(jnp.mean(middle * middle, axis=-1, keepdims=True) + norm_eps)
    normed_two = (middle * scale_two * gain_second).astype(jnp.bfloat16)
    normed_mlp = gather_rows(normed_two, group)
    back_all = gather_rows(cotangent, group)
    expanded = contract(normed_mlp, expand_full)
    up_part = expanded[:, pair_width:]
    act_part, slope_part = gelu_parts(expanded[:, :pair_width])
    product_low = (act_part * up_part).astype(jnp.bfloat16)
    product_grad = contract_cols(back_all, shrink_full)
    gate_grad_low = (product_grad * up_part * slope_part).astype(jnp.bfloat16)
    up_grad_low = (product_grad * act_part).astype(jnp.bfloat16)
    expand_back = jnp.concatenate([gate_grad_low, up_grad_low], axis=1)
    normed_two_grad = scatter_rows(
        contract_cols(expand_back, expand_full).astype(jnp.bfloat16), group
    )
    output = (
        middle + scatter_rows(contract(product_low, shrink_full).astype(jnp.bfloat16), group)
    ).astype(jnp.bfloat16)
    gain_two = jnp.sum(normed_two_grad * middle * scale_two, axis=0)
    back_float = cotangent.astype(jnp.float32)
    middle_grad = back_float + norm_back(middle, scale_two, gain_second, normed_two_grad)
    branch_back = gather_rows(middle_grad.astype(jnp.bfloat16), group)

    def reduce_seq(matrix):
        return lax.psum_scatter(
            matrix.astype(jnp.bfloat16), "seq", scatter_dimension=0, tiled=True
        )

    shrink_part = reduce_seq(contract_rows(back_all, product_low))
    expand_part = reduce_seq(contract_rows(normed_mlp, expand_back))

    mixed_grad = contract_cols(branch_back, mixer_full)
    gate_back, recur_back, rate_w_grad, input_w_grad, sums = lru_backward(
        place, mixed_grad, gate_branch, recur_input, hidden, conv_low, rate, admit, masks,
        rate_w, input_w, params, piece,
    )
    branch_back_low = jnp.concatenate([gate_back, recur_back], axis=1)
    branch_part = reduce_seq(contract_rows(normed_all, branch_back_low))
    mixer_part = reduce_seq(contract_rows(branch_back, mixed))
    normed_one_grad = scatter_rows(
        contract(branch_back_low, branch_full.reshape(4 * chan_width, width)).astype(jnp.bfloat16),
        group,
    )
    gain_one = jnp.sum(normed_one_grad * rows_float * scale_one, axis=0)
    residual_grad = middle_grad + norm_back(rows_float, scale_one, gain_first, normed_one_grad)
    gains_grad = lax.psum(jnp.stack([gain_one, gain_two]), ("seq", "chan"))

    channel_pair = jnp.sum(sums, axis=1)
    channel_pair = jnp.concatenate(
        [
            channel_pair[: CONV + 3],
            channel_pair[CONV + 3 :] * -lru_scale * jax.nn.sigmoid(channel_full[CONV + 3 :]),
        ],
        axis=0,
    )
    channel_grad = lax.psum(
        channel_pair[:, :chan_width] + partner(channel_pair[:, chan_width:]), "seq"
    )
    block_size = gate_blocks.shape[2]
    gate_pair = jnp.stack(
        [
            diagonal_blocks(rate_w_grad, 2 * block_count),
            diagonal_blocks(input_w_grad, 2 * block_count),
        ]
    )
    gate_part = lax.psum_scatter(
        gate_pair.astype(jnp.bfloat16), "seq", scatter_dimension=2, tiled=True
    )

    def settle(part, pieces, each):
        mine = [part[:, 2 * k * each : (2 * k + 1) * each] for k in range(pieces)]
        theirs = [part[:, (2 * k + 1) * each : (2 * k + 2) * each] for k in range(pieces)]
        mine = jnp.concatenate(mine, axis=1).astype(jnp.float32)
        return mine + partner(jnp.concatenate(theirs, axis=1)).astype(jnp.float32)

    shrink_grad = settle(shrink_part, 1, hidden_width).T
    expand_grad = settle(expand_part, 2, hidden_width).reshape(-1, 2, hidden_width)
    mixer_grad = settle(mixer_part, 1, chan_width).T
    branch_grad = settle(branch_part, 2, chan_width).reshape(-1, 2, chan_width)
    gate_grad = gate_part[:, :block_count].astype(jnp.float32) + partner(
        gate_part[:, block_count:]
    ).astype(jnp.float32)
    grad_shards = (branch_grad, gate_grad, mixer_grad, expand_grad, shrink_grad)
    own_squares = sum((jnp.sum(shard_grad * shard_grad) for shard_grad in grad_shards))
    own_squares = own_squares + jnp.where(
        seq_place == 0, jnp.sum(channel_grad * channel_grad), 0.0
    )
    total_squares = lax.psum(own_squares, ("seq", "chan"))
    grad_norm = jnp.sqrt(total_squares + jnp.sum(gains_grad * gains_grad))
    clip_limit = clip_rms * math.sqrt(PARAMS)
    factor = jnp.minimum(1.0, clip_limit / (grad_norm + 1e-06))
    branch_new, branch_master = adam(branch_state, branch_grad, factor, rate_matrix, weight_decay)
    gate_new, gate_master = adam(gate_state, gate_grad, factor, rate_gate, weight_decay)
    mixer_new, mixer_master = adam(mixer_state, mixer_grad, factor, rate_matrix, weight_decay)
    expand_new, expand_master = adam(expand_state, expand_grad, factor, rate_matrix, weight_decay)
    shrink_new, shrink_master = adam(shrink_state, shrink_grad, factor, rate_matrix, weight_decay)
    channel_all, _ = adam(channel_state, channel_grad, factor, rate_channel, 0.0)
    gains_new, _ = adam(gains_state, gains_grad, factor, rate_gains, 0.0)
    channel_new = jnp.stack([channel_all[0], channel_all[3]])
    channel_moments = channel_all[1:3]
    return (
        output,
        residual_grad,
        branch_grad,
        gate_grad,
        mixer_grad,
        expand_grad,
        shrink_grad,
        channel_grad,
        gains_grad,
        grad_norm,
        branch_new,
        gate_new,
        mixer_new,
        expand_new,
        shrink_new,
        channel_new,
        channel_moments,
        gains_new,
        branch_master.astype(jnp.bfloat16),
        gate_master.astype(jnp.bfloat16),
        mixer_master.astype(jnp.bfloat16),
        expand_master.astype(jnp.bfloat16),
        shrink_master.astype(jnp.bfloat16),
    )


def solution(mesh):
    in_specs = (
        P(("seq", "chan"), None),
        P(("seq", "chan"), None),
        P("seq"),
        P(None, None, "chan"),
        P(None, "chan", None, None),
        P("chan", None),
        P(None, None, "chan"),
        P("chan", None),
        P(None, "seq", None, "chan"),
        P(None, None, "chan", "seq", None),
        P(None, "chan", "seq"),
        P(None, "seq", None, "chan"),
        P(None, "chan", "seq"),
        P(None, None, "chan"),
        P(),
    )
    out_specs = (
        P(("seq", "chan"), None),
        P(("seq", "chan"), None),
        P("seq", None, "chan"),
        P(None, "chan", "seq", None),
        P("chan", "seq"),
        P("seq", None, "chan"),
        P("chan", "seq"),
        P(None, "chan"),
        P(),
        P(),
        P(None, "seq", None, "chan"),
        P(None, None, "chan", "seq", None),
        P(None, "chan", "seq"),
        P(None, "seq", None, "chan"),
        P(None, "chan", "seq"),
        P(None, None, "chan"),
        P(None, None, "chan"),
        P(),
        P("seq", None, "chan"),
        P(None, "chan", "seq", None),
        P("chan", "seq"),
        P("seq", None, "chan"),
        P("chan", "seq"),
    )
    return jax.shard_map(local, mesh=mesh, in_specs=in_specs, out_specs=out_specs, check_vma=False)
```

```python
import math

import jax
import jax.numpy as jnp
from jax import lax
from jax.experimental import pallas as pl
from jax.experimental.pallas import tpu as pltpu
from jax.sharding import PartitionSpec as P

CONV = 4
SEQ_LEN = 2048
SEQS = 2
STEP = 10
PARAMS = 54321152


norm_eps = 1e-06
lru_scale = 8.0
clip_rms = 0.4
beta_one = 0.9
beta_two = 0.95
adam_eps = 1e-08
weight_decay = 0.1
ema_keep = 0.99
rate_matrix = 0.02
rate_gate = 0.1
rate_channel = 1.0
rate_gains = 0.5
SUB = 8
TILE = 16
GELU_SCALE = math.sqrt(2.0 / math.pi)
GELU_CUBE = 0.044715


def contract_rows(left_mat, right_mat):
    return lax.dot_general(
        left_mat, right_mat, (((0,), (0,)), ((), ())), preferred_element_type=jnp.float32
    )


def contract_cols(left_mat, right_mat):
    return lax.dot_general(
        left_mat, right_mat, (((1,), (1,)), ((), ())), preferred_element_type=jnp.float32
    )


def contract(left_mat, right_mat):
    return jnp.dot(left_mat, right_mat, preferred_element_type=jnp.float32)


def norm_back(values, scale, gain, upstream):
    scaled = gain * upstream
    return scale * scaled - values * scale * scale * scale * jnp.mean(
        scaled * values, axis=-1, keepdims=True
    )


def adam(old_state, gradient, factor, step_rate, decay_use):
    clipped = gradient * factor
    moment_one = beta_one * old_state[1] + (1.0 - beta_one) * clipped
    moment_two = beta_two * old_state[2] + (1.0 - beta_two) * clipped * clipped
    first_hat = moment_one / (1.0 - beta_one**STEP)
    second_hat = moment_two / (1.0 - beta_two**STEP)
    master = old_state[0] - step_rate * (
        first_hat / (jnp.sqrt(second_hat) + adam_eps) + decay_use * old_state[0]
    )
    average = ema_keep * old_state[3] + (1.0 - ema_keep) * master
    return (jnp.stack([master, moment_one, moment_two, average]), master)


def gelu_parts(values):
    square = values * values
    turn = jnp.tanh(GELU_SCALE * values * (1.0 + GELU_CUBE * square))
    half = 0.5 * (1.0 + turn)
    slope = half + 0.5 * values * (1.0 - turn * turn) * (
        GELU_SCALE * (1.0 + 3.0 * GELU_CUBE * square)
    )
    return values * half, slope


def decay_parts(log_decay):
    decay = jnp.exp(log_decay)
    z = 2.0 * log_decay
    series = 1.0 + z * (1.0 / 7.0)
    for order in (6.0, 5.0, 4.0, 3.0, 2.0):
        series = 1.0 + z * (1.0 / order) * series
    return decay, jnp.where(z > -0.35, -z * series, 1.0 - decay * decay)


def roll_down(values, offset):
    return pltpu.roll(values, offset, 0)


def roll_up(values, offset):
    return pltpu.roll(values, SUB - offset, 0)


def lru_forward_kernel(
    place_ref,
    normed_ref,
    gate_w_ref,
    recur_w_ref,
    mask_ref,
    rate_w_ref,
    input_w_ref,
    par_ref,
    mixed_ref,
    gate_ref,
    recur_ref,
    hidden_ref,
    conv_ref,
    rate_ref,
    admit_ref,
    rate_pre,
    input_pre,
    tail,
    state,
):
    block, width = gate_ref.shape

    @pl.when(pl.program_id(0) == 0)
    def _():
        tail[...] = jnp.zeros_like(tail)
        state[...] = jnp.zeros_like(state)

    normed = normed_ref[...]
    recur_ref[...] = contract_cols(normed, recur_w_ref[...])
    gate_ref[...] = contract_cols(normed, gate_w_ref[...])
    row = lax.broadcasted_iota(jnp.int32, (SUB, width), 0)

    def convolve(step, before):
        base = pl.multiple_of(step * TILE, TILE)
        halves = []
        for half in range(2):
            rows = pl.ds(base + half * SUB, SUB)
            now = recur_ref[rows, :]
            masks = mask_ref[rows, :]
            total = par_ref[CONV : CONV + 1, :] + par_ref[0:1, :] * now
            for offset in range(1, CONV):
                moved = jnp.where(
                    row < offset, roll_down(before, offset), roll_down(now, offset)
                )
                total = total + par_ref[offset : offset + 1, :] * (
                    moved * masks[:, offset - 1 : offset]
                )
            halves.append(total)
            before = now
        conv_ref[pl.ds(base, TILE), :] = jnp.concatenate(halves, axis=0).astype(jnp.bfloat16)
        return before

    tail[...] = lax.fori_loop(0, block // TILE, convolve, tail[...])
    low = conv_ref[...]
    rate_pre[...] = contract(low, rate_w_ref[...])
    input_pre[...] = contract(low, input_w_ref[...])

    def advance(step, carry):
        base = pl.multiple_of(step * TILE, TILE)
        conv = conv_ref[pl.ds(base, TILE), :].astype(jnp.float32)
        halves = []
        for half in range(2):
            rows = pl.ds(base + half * SUB, SUB)
            rate = jax.nn.sigmoid(rate_pre[rows, :] + par_ref[CONV + 1 : CONV + 2, :])
            admit = jax.nn.sigmoid(input_pre[rows, :] + par_ref[CONV + 2 : CONV + 3, :])
            decay, rest = decay_parts(par_ref[CONV + 3 : CONV + 4, :] * rate)
            coeff = decay * mask_ref[rows, 0:1]
            drive = jnp.sqrt(rest) * admit * conv[half * SUB : (half + 1) * SUB, :]
            for offset in (1, 2, 4):
                inner = row >= offset
                drive = drive + coeff * jnp.where(inner, roll_down(drive, offset), 0.0)
                coeff = coeff * jnp.where(inner, roll_down(coeff, offset), 1.0)
            hidden = drive + coeff * carry
            carry = jnp.broadcast_to(hidden[SUB - 1 : SUB, :], hidden.shape)
            hidden_ref[rows, :] = hidden
            rate_ref[rows, :] = rate
            admit_ref[rows, :] = admit
            branch = gate_ref[rows, :]
            turn = jnp.tanh(GELU_SCALE * branch * (1.0 + GELU_CUBE * branch * branch))
            halves.append(0.5 * branch * (1.0 + turn) * hidden)
        mixed_ref[pl.ds(base, TILE), :] = jnp.concatenate(halves, axis=0).astype(jnp.bfloat16)
        return carry

    state[...] = lax.fori_loop(0, block // TILE, advance, state[...])


def lru_backward_kernel(
    place_ref,
    back_ref,
    mixer_ref,
    gate_ref,
    recur_ref,
    hidden_ref,
    before_ref,
    conv_ref,
    rate_ref,
    admit_ref,
    mask_ref,
    rate_w_ref,
    input_w_ref,
    par_ref,
    gate_back_ref,
    recur_back_ref,
    rate_grad_ref,
    input_grad_ref,
    sums_ref,
    upstream_ref,
    rate_low,
    input_low,
    conv_back,
    state,
    ahead,
):
    block, width = gate_ref.shape
    steps = block // TILE

    @pl.when(pl.program_id(0) == 0)
    def _():
        state[...] = jnp.zeros_like(state)
        ahead[...] = jnp.zeros_like(ahead)
        sums_ref[...] = jnp.zeros_like(sums_ref)
        rate_grad_ref[...] = jnp.zeros_like(rate_grad_ref)
        input_grad_ref[...] = jnp.zeros_like(input_grad_ref)

    upstream_ref[...] = contract_cols(back_ref[...], mixer_ref[...])
    row = lax.broadcasted_iota(jnp.int32, (SUB, width), 0)

    def retreat(step, carry):
        carried_next, coeff_next = carry
        index = steps - 1 - step
        base = pl.multiple_of(index * TILE, TILE)
        conv_tile = conv_ref[pl.ds(base, TILE), :].astype(jnp.float32)
        halves = [None, None, None]
        lows = [[None, None] for _ in range(3)]
        edge = pl.multiple_of(jnp.maximum(base - SUB, 0), SUB)
        earlier = jnp.where(index == 0, before_ref[...], hidden_ref[pl.ds(edge, SUB), :])
        for half in (1, 0):
            rows = pl.ds(base + half * SUB, SUB)
            conv = conv_tile[half * SUB : (half + 1) * SUB, :]
            rate = rate_ref[rows, :]
            admit = admit_ref[rows, :]
            speed = par_ref[CONV + 3 : CONV + 4, :]
            decay, rest = decay_parts(speed * rate)
            inverse = lax.rsqrt(rest)
            norm = rest * inverse
            coeff = decay * mask_ref[rows, 0:1]
            act, slope = gelu_parts(gate_ref[rows, :])
            upstream = upstream_ref[rows, :]
            hidden = hidden_ref[rows, :]
            carried = upstream * act
            chain = jnp.where(row == SUB - 1, coeff_next, roll_up(coeff, 1))
            for offset in (1, 2, 4):
                inner = row < SUB - offset
                carried = carried + chain * jnp.where(inner, roll_up(carried, offset), 0.0)
                chain = chain * jnp.where(inner, roll_up(chain, offset), 1.0)
            carried = carried + chain * carried_next
            carried_next = jnp.broadcast_to(carried[0:1, :], carried.shape)
            coeff_next = jnp.broadcast_to(coeff[0:1, :], coeff.shape)
            if half == 1:
                last = hidden_ref[pl.ds(base, SUB), :]
            else:
                last = earlier
            previous = jnp.where(row == 0, roll_down(last, 1), roll_down(hidden, 1))
            log_grad = carried * (
                previous * coeff - admit * conv * (decay * decay) * inverse
            )
            rate_back = log_grad * speed * rate * (1.0 - rate)
            drive = carried * norm
            direct = drive * admit
            input_back = drive * conv * admit * (1.0 - admit)
            conv_back[rows, :] = direct
            lows[0][half] = upstream * hidden * slope
            lows[1][half] = rate_back
            lows[2][half] = input_back
            sums_ref[5] += rate_back
            sums_ref[6] += input_back
            sums_ref[7] += log_grad * rate
        tile = pl.ds(base, TILE)
        gate_back_ref[tile, :] = jnp.concatenate(lows[0], axis=0).astype(jnp.bfloat16)
        rate_low[tile, :] = jnp.concatenate(lows[1], axis=0).astype(jnp.bfloat16)
        input_low[tile, :] = jnp.concatenate(lows[2], axis=0).astype(jnp.bfloat16)
        return carried_next, coeff_next

    carried_next, coeff_next = lax.fori_loop(0, steps, retreat, (state[0], state[1]))
    state[0] = carried_next
    state[1] = coeff_next
    low = conv_ref[...]
    rate_back_low = rate_low[...]
    input_back_low = input_low[...]
    rate_grad_ref[...] += contract_rows(low, rate_back_low)
    input_grad_ref[...] += contract_rows(low, input_back_low)
    conv_back[...] += contract_cols(rate_back_low, rate_w_ref[...]) + contract_cols(
        input_back_low, input_w_ref[...]
    )

    def unconvolve(step, carry):
        base = pl.multiple_of((steps - 1 - step) * TILE, TILE)
        halves = [None, None]
        nexts = list(carry)
        for half in (1, 0):
            rows = pl.ds(base + half * SUB, SUB)
            grad = conv_back[rows, :]
            now = recur_ref[rows, :]
            masks = mask_ref[rows, :]
            sums_ref[0] += grad * now
            sums_ref[CONV] += grad
            total = par_ref[0:1, :] * grad
            for offset in range(1, CONV):
                kept = grad * masks[:, offset - 1 : offset]
                moved = jnp.where(
                    row < SUB - offset, roll_up(kept, offset), roll_up(nexts[offset - 1], offset)
                )
                nexts[offset - 1] = kept
                sums_ref[offset] += moved * now
                total = total + par_ref[offset : offset + 1, :] * moved
            halves[half] = total
        recur_back_ref[pl.ds(base, TILE), :] = jnp.concatenate(halves, axis=0).astype(jnp.bfloat16)
        return tuple(nexts)

    nexts = lax.fori_loop(0, steps, unconvolve, tuple(ahead[k] for k in range(CONV - 1)))
    for k in range(CONV - 1):
        ahead[k] = nexts[k]


def lru_sizes(rows, width, piece):
    block = min(256, piece)
    return block, rows // block, piece // block


def lru_forward(place, normed, gate_w, recur_w, masks, rate_w, input_w, params, piece):
    rows, depth = normed.shape
    width = gate_w.shape[0]
    block, count, per = lru_sizes(rows, width, piece)

    def there(i, place_ref):
        return (((i // per) ^ place_ref[0]) * per + i % per, 0)

    def here(i, place_ref):
        return (i, 0)

    def fixed(i, place_ref):
        return (0, 0)

    tall = lambda where: pl.BlockSpec((block, width), where)
    square = pl.BlockSpec((width, width), fixed)
    flat = pl.BlockSpec((width, depth), fixed)
    floats = jax.ShapeDtypeStruct((rows, width), jnp.float32)
    lows = jax.ShapeDtypeStruct((rows, width), jnp.bfloat16)
    return pl.pallas_call(
        lru_forward_kernel,
        grid_spec=pltpu.PrefetchScalarGridSpec(
            num_scalar_prefetch=1,
            grid=(count,),
            in_specs=[
                pl.BlockSpec((block, depth), there),
                flat,
                flat,
                pl.BlockSpec((block, SUB), here),
                square,
                square,
                pl.BlockSpec((2 * CONV, width), fixed),
            ],
            out_specs=[tall(there)] + [tall(here)] * 6,
            scratch_shapes=[
                pltpu.VMEM((block, width), jnp.float32),
                pltpu.VMEM((block, width), jnp.float32),
                pltpu.VMEM((SUB, width), jnp.float32),
                pltpu.VMEM((SUB, width), jnp.float32),
            ],
        ),
        out_shape=[lows, floats, floats, floats, lows, floats, floats],
        compiler_params=pltpu.CompilerParams(
            dimension_semantics=("arbitrary",), vmem_limit_bytes=48 * 2**20
        ),
        cost_estimate=pl.CostEstimate(
            flops=4 * rows * width * (width + depth),
            bytes_accessed=26 * rows * width + 2 * rows * depth,
            transcendentals=6 * rows * width,
        ),
        name="lru_forward",
    )(place, normed, gate_w, recur_w, masks, rate_w, input_w, params)


def lru_backward(
    place, back, mixer, gate_branch, recur_input, hidden, conv, rate, admit, masks, rate_w,
    input_w, params, piece,
):
    rows, depth = back.shape
    width = gate_branch.shape[1]
    block, count, per = lru_sizes(rows, width, piece)

    def there(i, place_ref):
        t = count - 1 - i
        return (((t // per) ^ place_ref[0]) * per + t % per, 0)

    def here(i, place_ref):
        return (count - 1 - i, 0)

    def before(i, place_ref):
        return (jnp.maximum((count - 1 - i) * (block // SUB) - 1, 0), 0)

    def fixed(i, place_ref):
        return (0, 0)

    tall = lambda where: pl.BlockSpec((block, width), where)
    square = pl.BlockSpec((width, width), fixed)
    return pl.pallas_call(
        lru_backward_kernel,
        grid_spec=pltpu.PrefetchScalarGridSpec(
            num_scalar_prefetch=1,
            grid=(count,),
            in_specs=[
                pl.BlockSpec((block, depth), there),
                pl.BlockSpec((width, depth), fixed),
                tall(here),
                tall(here),
                tall(here),
                pl.BlockSpec((SUB, width), before),
                tall(here),
                tall(here),
                tall(here),
                pl.BlockSpec((block, SUB), here),
                square,
                square,
                pl.BlockSpec((2 * CONV, width), fixed),
            ],
            out_specs=[
                tall(there),
                tall(there),
                square,
                square,
                pl.BlockSpec((2 * CONV, SUB, width), lambda i, place_ref: (0, 0, 0)),
            ],
            scratch_shapes=[
                pltpu.VMEM((block, width), jnp.float32),
                pltpu.VMEM((block, width), jnp.bfloat16),
                pltpu.VMEM((block, width), jnp.bfloat16),
                pltpu.VMEM((block, width), jnp.float32),
                pltpu.VMEM((2, SUB, width), jnp.float32),
                pltpu.VMEM((CONV - 1, SUB, width), jnp.float32),
            ],
        ),
        out_shape=[
            jax.ShapeDtypeStruct((rows, width), jnp.bfloat16),
            jax.ShapeDtypeStruct((rows, width), jnp.bfloat16),
            jax.ShapeDtypeStruct((width, width), jnp.float32),
            jax.ShapeDtypeStruct((width, width), jnp.float32),
            jax.ShapeDtypeStruct((2 * CONV, SUB, width), jnp.float32),
        ],
        compiler_params=pltpu.CompilerParams(
            dimension_semantics=("arbitrary",), vmem_limit_bytes=48 * 2**20
        ),
        cost_estimate=pl.CostEstimate(
            flops=8 * rows * width * width + 2 * rows * width * depth,
            bytes_accessed=30 * rows * width + 2 * rows * depth,
            transcendentals=6 * rows * width,
        ),
        name="lru_backward",
    )(
        place, back, mixer, gate_branch, recur_input, hidden, hidden, conv, rate, admit, masks,
        rate_w, input_w, params,
    )


def adam_kernel(step_rate, decay_use, factor_ref, state_ref, grad_ref, new_ref, copy_ref):
    clipped = grad_ref[...] * factor_ref[0, 0]
    master = state_ref[0]
    moment_one = beta_one * state_ref[1] + (1.0 - beta_one) * clipped
    moment_two = beta_two * state_ref[2] + (1.0 - beta_two) * clipped * clipped
    first_hat = moment_one * (1.0 / (1.0 - beta_one**STEP))
    second_hat = moment_two * (1.0 / (1.0 - beta_two**STEP))
    master = master - step_rate * (
        first_hat / (jnp.sqrt(second_hat) + adam_eps) + decay_use * master
    )
    new_ref[0] = master
    new_ref[1] = moment_one
    new_ref[2] = moment_two
    new_ref[3] = ema_keep * state_ref[3] + (1.0 - ema_keep) * master
    copy_ref[...] = master.astype(jnp.bfloat16)


def adam_matrix(state, gradient, factor, step_rate, decay_use):
    rows, rest = gradient.shape[0], gradient.shape[1:]
    goal = max(16, 2**16 // math.prod(rest))
    fits = [b for b in range(16, rows + 1, 16) if rows % b == 0 and (b <= goal or b == 16)]
    block = max(fits, default=rows)
    zeros = (0,) * len(rest)
    wide = pl.BlockSpec((4, block) + rest, lambda i: (0, i) + zeros)
    narrow = pl.BlockSpec((block,) + rest, lambda i: (i,) + zeros)
    return pl.pallas_call(
        lambda *refs: adam_kernel(step_rate, decay_use, *refs),
        grid=(rows // block,),
        in_specs=[pl.BlockSpec(memory_space=pltpu.SMEM), wide, narrow],
        out_specs=[wide, narrow],
        out_shape=[
            jax.ShapeDtypeStruct(state.shape, jnp.float32),
            jax.ShapeDtypeStruct(gradient.shape, jnp.bfloat16),
        ],
        compiler_params=pltpu.CompilerParams(
            dimension_semantics=("arbitrary",), vmem_limit_bytes=48 * 2**20
        ),
        cost_estimate=pl.CostEstimate(
            flops=20 * gradient.size, bytes_accessed=38 * gradient.size, transcendentals=0
        ),
        name="adam",
    )(factor.reshape(1, 1), state, gradient)


def swap(values, axis, bit):
    return lax.ppermute(
        values, axis, [(i, i ^ bit) for i in range(lax.axis_size(axis))]
    )


def bits_of(size):
    return [1 << k for k in reversed(range(size.bit_length() - 1))]


def later(values, *others):
    return lax.optimization_barrier((values,) + others)[0]


def tree_sum(terms):
    while len(terms) > 1:
        terms = [left + right for left, right in zip(terms[::2], terms[1::2])]
    return terms[0]


def sum_over_all(values):
    values = values + swap(values, "chan", 1)
    for axis, step in (("chan", 2), ("seq", 1)):
        others = range(step, lax.axis_size(axis), step)
        values = tree_sum([values] + [swap(values, axis, other) for other in others])
    return values


def sum_by_steps(values, axes):
    for axis in axes:
        for bit in bits_of(lax.axis_size(axis)):
            values = values + swap(values, axis, bit)
    return values


def both(*values):
    return lax.optimization_barrier(values)


def gather_blocks(own, size):
    blocks = {0: own}
    for bit in bits_of(size):
        blocks.update({m | bit: swap(block, "chan", bit) for m, block in list(blocks.items())})
    return [blocks[m] for m in range(size)]


def lay_rows(blocks, room=1):
    rows = room * sum(block.shape[0] for block in blocks)
    return lay_more(jnp.zeros((rows,) + blocks[0].shape[1:], blocks[0].dtype), blocks, 0)


def lay_more(whole, blocks, start=None):
    if start is None:
        start = whole.shape[0] - sum(block.shape[0] for block in blocks)
    for block in blocks:
        whole = lax.dynamic_update_slice_in_dim(whole, block, start, axis=0)
        start += block.shape[0]
    return whole


def split_rows(mat, piece):
    return [mat[k * piece : (k + 1) * piece] for k in range(mat.shape[0] // piece)]


def scatter_near(partial, piece):
    blocks = dict(enumerate(split_rows(partial, piece)))
    came = []
    for bit in reversed(bits_of(len(blocks))):
        inward = {m: swap(blocks[m | bit], "chan", bit) for m in blocks if not m & bit}
        came += inward.values()
        blocks = {
            m: (blocks[m].astype(jnp.float32) + block.astype(jnp.float32)).astype(jnp.bfloat16)
            for m, block in inward.items()
        }
    return blocks[0], came


def rows_far(parts):
    return [part[part.shape[0] // 2 :] for part in parts]


def rows_near(parts):
    return [part[: part.shape[0] // 2] for part in parts]


def scatter_start(product, parts, size, piece):
    far = product(*rows_far(parts)).astype(jnp.bfloat16)
    total, came = scatter_near(far, piece)
    return swap(total, "chan", size // 2), came, far


def scatter_end(arrived, near, piece):
    total, _ = scatter_near(near, piece)
    return total.astype(jnp.float32) + arrived.astype(jnp.float32)


def block_diagonal(blocks):
    count, size, _ = blocks.shape
    return jnp.concatenate(
        [jnp.pad(blocks[k], ((0, 0), (k * size, (count - 1 - k) * size))) for k in range(count)],
        axis=0,
    )


def diagonal_blocks(matrix, count):
    size = matrix.shape[0] // count
    return jnp.stack(
        [matrix[k * size : (k + 1) * size, k * size : (k + 1) * size] for k in range(count)]
    )


def local(
    residual,
    cotangent,
    resets,
    branch_weights,
    gate_blocks,
    mixer_weights,
    expand_weights,
    shrink_weights,
    branch_state,
    gate_state,
    mixer_state,
    expand_state,
    shrink_state,
    channel_state,
    gains_state,
):
    seq_count = lax.axis_size("seq")
    group = lax.axis_size("chan") // SEQS
    seq_place = lax.axis_index("seq")
    chan_place = lax.axis_index("chan")
    place = (chan_place % group).astype(jnp.int32).reshape(1)
    width = residual.shape[1]
    piece = residual.shape[0]
    chan_width = branch_weights.shape[2]
    hidden_width = expand_weights.shape[2]
    block_count = gate_blocks.shape[1]

    def partner(values):
        return swap(values, "chan", group)

    def fetch_part(matrix):
        rows = matrix.shape[0] // seq_count
        return partner(lax.dynamic_slice_in_dim(matrix, seq_place * rows, rows, axis=0))

    def share(part):
        return lax.all_gather(part, "seq", axis=0, tiled=True)

    gains = gains_state[0]
    gain_first = 1.0 + gains[0]
    gain_second = 1.0 + gains[1]
    rows_float = residual.astype(jnp.float32)
    scale_one = lax.rsqrt(jnp.mean(rows_float * rows_float, axis=-1, keepdims=True) + norm_eps)
    normed_one = (rows_float * scale_one * gain_first).astype(jnp.bfloat16)
    side = group // 2
    own_branch = branch_weights.transpose(1, 2, 0)
    first_part = fetch_part(
        later(
            jnp.concatenate([own_branch.reshape(2 * chan_width, width), mixer_weights], axis=0),
            normed_one,
        )
    )
    half = piece // 2
    normed_top, first_part = both(swap(normed_one[:half], "chan", side), first_part)
    others = share(first_part)
    other_branch = others[: 2 * chan_width].reshape(own_branch.shape)
    other_mixer = others[2 * chan_width :]
    branch_full = jnp.concatenate([own_branch, other_branch], axis=1)
    normed_end = swap(later(normed_one, normed_top)[half:], "chan", side)
    normed_far = gather_blocks(jnp.concatenate([normed_top, normed_end], axis=0), side)
    normed_all = lay_rows(gather_blocks(normed_one, side) + normed_far)
    back_far = swap(later(cotangent, normed_end), "chan", side)
    own_expand = expand_weights.reshape(width, 2 * hidden_width)
    expand_part = fetch_part(later(own_expand, normed_end))
    shrink_part = fetch_part(later(shrink_weights, normed_end))
    pair_width = 2 * hidden_width

    gate_full = jnp.concatenate([gate_blocks, partner(gate_blocks)], axis=1)
    rate_w = block_diagonal(gate_full[0])
    input_w = block_diagonal(gate_full[1])
    channel = channel_state[0]
    channel_full = jnp.concatenate([channel, partner(channel)], axis=1)
    speed = -lru_scale * jax.nn.softplus(channel_full[CONV + 3 :])
    params = jnp.concatenate([channel_full[: CONV + 3], speed], axis=0)

    flags = lax.dynamic_index_in_dim(
        resets.reshape(SEQS, SEQ_LEN), chan_place // group, axis=0, keepdims=False
    )
    stays = jnp.where(jnp.arange(SEQ_LEN) == 0, 0.0, 1.0 - (flags == 1).astype(jnp.float32))
    within = [stays]
    for offset in range(1, CONV - 1):
        within.append(within[-1] * jnp.pad(stays, (offset, 0))[:SEQ_LEN])
    masks = jnp.stack(within + [stays] * (SUB - len(within)), axis=1)

    mixed, gate_branch, recur_input, hidden, conv_low, rate, admit = lru_forward(
        place, normed_all, branch_full[0], branch_full[1], masks, rate_w, input_w, params, piece
    )
    mixed, back_far, expand_part = both(mixed, back_far, expand_part)
    mixer_full = jnp.concatenate([mixer_weights, other_mixer], axis=0)
    back_all = lay_rows(gather_blocks(cotangent, side) + gather_blocks(back_far, side))
    other_expand = share(expand_part)
    expand_full = jnp.concatenate(
        [
            own_expand[:, :hidden_width],
            other_expand[:, :hidden_width],
            own_expand[:, hidden_width:],
            other_expand[:, hidden_width:],
        ],
        axis=1,
    )
    through_mixer = lambda left: contract(left, mixer_full)
    arrived, came, _ = scatter_start(through_mixer, [mixed], group, piece)
    near = through_mixer(*rows_near([later(mixed, *came)])).astype(jnp.bfloat16)
    arrived, shrink_part = both(arrived, shrink_part)
    middle = rows_float + scatter_end(arrived, near, piece)
    scale_two = lax.rsqrt(jnp.mean(middle * middle, axis=-1, keepdims=True) + norm_eps)
    normed_two = (middle * scale_two * gain_second).astype(jnp.bfloat16)
    shrink_full = lay_rows([shrink_weights, share(later(shrink_part, other_expand))])
    mlp_near = lay_rows(gather_blocks(normed_two, side), 2)
    mlp_far, mlp_near, back_all, expand_full = both(
        swap(normed_two, "chan", side), mlp_near, back_all, expand_full
    )
    normed_mlp = lay_more(mlp_near, gather_blocks(mlp_far, side))
    expanded = contract(normed_mlp, expand_full)
    product_grad = contract_cols(back_all, shrink_full)
    up_part = expanded[:, pair_width:]
    act_part, slope_part = gelu_parts(expanded[:, :pair_width])
    product_low = (act_part * up_part).astype(jnp.bfloat16)
    gate_grad_low = (product_grad * up_part * slope_part).astype(jnp.bfloat16)
    up_grad_low = (product_grad * act_part).astype(jnp.bfloat16)
    def reduce_seq(matrix):
        return lax.psum_scatter(
            matrix.astype(jnp.bfloat16), "seq", scatter_dimension=0, tiled=True
        )

    def through_expand(*grads):
        return contract_cols(jnp.concatenate(grads, axis=1), expand_full)

    def through_shrink(left):
        return contract(left, shrink_full)

    arrived, came, _ = scatter_start(through_expand, [gate_grad_low, up_grad_low], group, piece)
    gate_grad_low, up_grad_low, product_low, *_ = both(
        gate_grad_low, up_grad_low, product_low, *came
    )
    expand_local = contract_rows(
        normed_mlp, jnp.concatenate([gate_grad_low, up_grad_low], axis=1)
    ).astype(jnp.bfloat16)
    arrived, expand_local, gate_grad_low = both(arrived, expand_local, gate_grad_low)
    near = through_expand(*rows_near([gate_grad_low, up_grad_low])).astype(jnp.bfloat16)
    expand_sum = reduce_seq(expand_local)
    normed_two_grad = scatter_end(arrived, near, piece)
    back_float = cotangent.astype(jnp.float32)
    middle_grad = back_float + norm_back(middle, scale_two, gain_second, normed_two_grad)
    middle_low = middle_grad.astype(jnp.bfloat16)
    product_low = later(product_low, middle_low)
    shrink_local = contract_rows(back_all, product_low).astype(jnp.bfloat16)
    middle_near = lay_rows(gather_blocks(middle_low, side), 2)
    product_low = later(product_low, shrink_local)
    out_arrived, _, out_far = scatter_start(through_shrink, [product_low], group, piece)
    out_near = through_shrink(*rows_near([later(product_low, out_far)])).astype(jnp.bfloat16)
    middle_far, shrink_local, middle_near, out_near = both(
        swap(middle_low, "chan", side), shrink_local, middle_near, out_near
    )
    shrink_sum = reduce_seq(shrink_local)
    branch_back = lay_more(middle_near, gather_blocks(middle_far, side))
    gain_two = jnp.sum(normed_two_grad * middle * scale_two, axis=0)

    def settle(part, pieces, each):
        mine = [part[:, 2 * k * each : (2 * k + 1) * each] for k in range(pieces)]
        theirs = [part[:, (2 * k + 1) * each : (2 * k + 2) * each] for k in range(pieces)]
        return jnp.concatenate(mine, axis=1), partner(jnp.concatenate(theirs, axis=1))

    def total(pair):
        return pair[0].astype(jnp.float32) + pair[1].astype(jnp.float32)

    mixer_local = contract_rows(branch_back, mixed).astype(jnp.bfloat16)
    mixer_sum = reduce_seq(mixer_local)
    expand_pair = settle(expand_sum, 2, hidden_width)
    gate_back, recur_back, rate_w_grad, input_w_grad, sums = lru_backward(
        place, later(branch_back, mixer_local), mixer_full, gate_branch, recur_input, hidden,
        conv_low, rate, admit, masks, rate_w, input_w, params, piece,
    )
    gate_back, out_arrived, expand_theirs = both(gate_back, out_arrived, expand_pair[1])
    expand_pair = (expand_pair[0], expand_theirs)
    branch_back_low = jnp.concatenate([gate_back, recur_back], axis=1)
    branch_local = contract_rows(normed_all, branch_back_low).astype(jnp.bfloat16)
    branch_sum = reduce_seq(branch_local)
    through_branch = lambda left: contract(left, branch_full.reshape(4 * chan_width, width))
    branch_back_low = later(branch_back_low, branch_local)
    arrived, came, far = scatter_start(through_branch, [branch_back_low], group, piece)
    branch_back_low, *_ = both(branch_back_low, *came)
    shrink_pair = settle(later(shrink_sum, far), 1, hidden_width)
    near = through_branch(*rows_near([branch_back_low])).astype(jnp.bfloat16)
    mixer_pair = settle(later(mixer_sum, near), 1, chan_width)
    rate_w_grad, input_w_grad, sums = (
        later(rate_w_grad, far), later(input_w_grad, far), later(sums, far)
    )
    block_size = gate_blocks.shape[2]
    gate_pair = jnp.stack(
        [
            diagonal_blocks(rate_w_grad, 2 * block_count),
            diagonal_blocks(input_w_grad, 2 * block_count),
        ]
    )
    gate_pair = gate_pair.reshape(
        2, 2 * block_count, seq_count, block_size // seq_count, block_size
    )

    def gate_rows(other):
        rows = lax.dynamic_index_in_dim(gate_pair, seq_place ^ other, axis=2, keepdims=False)
        return swap(rows.astype(jnp.bfloat16), "seq", other).astype(jnp.float32) if other else rows

    gate_part = sum(gate_rows(other) for other in range(seq_count))
    gate_theirs = partner(gate_part[:, block_count:].astype(jnp.bfloat16))
    branch_sum, near, arrived, gate_theirs, shrink_theirs, mixer_theirs = both(
        branch_sum, near, arrived, gate_theirs, shrink_pair[1], mixer_pair[1]
    )
    mixer_pair = (mixer_pair[0], mixer_theirs)
    shrink_pair = (shrink_pair[0], shrink_theirs)
    output = (middle + scatter_end(out_arrived, out_near, piece)).astype(jnp.bfloat16)
    normed_one_grad = scatter_end(arrived, near, piece)
    gain_one = jnp.sum(normed_one_grad * rows_float * scale_one, axis=0)
    residual_grad = middle_grad + norm_back(rows_float, scale_one, gain_first, normed_one_grad)
    gains_grad = sum_by_steps(jnp.stack([gain_one, gain_two]), ("seq", "chan"))

    channel_pair = jnp.sum(sums, axis=1)
    channel_pair = jnp.concatenate(
        [
            channel_pair[: CONV + 3],
            channel_pair[CONV + 3 :] * -lru_scale * jax.nn.sigmoid(channel_full[CONV + 3 :]),
        ],
        axis=0,
    )
    channel_grad = sum_by_steps(
        channel_pair[:, :chan_width] + partner(channel_pair[:, chan_width:]), ("seq",)
    )
    shrink_grad = total(shrink_pair).T
    expand_grad = lax.optimization_barrier(
        total(expand_pair).reshape(-1, 2, hidden_width)
    )
    mixer_grad = total(mixer_pair).T
    branch_grad = total(settle(branch_sum, 2, chan_width)).reshape(-1, 2, chan_width)
    gate_grad = gate_part[:, :block_count] + gate_theirs.astype(jnp.float32)
    grad_shards = (branch_grad, gate_grad, mixer_grad, expand_grad, shrink_grad)
    own_squares = sum((jnp.sum(shard_grad * shard_grad) for shard_grad in grad_shards))
    own_squares = own_squares + jnp.where(
        seq_place == 0, jnp.sum(channel_grad * channel_grad), 0.0
    )
    total_squares = sum_over_all(own_squares.reshape(1))[0]
    grad_norm = jnp.sqrt(total_squares + jnp.sum(gains_grad * gains_grad))
    clip_limit = clip_rms * math.sqrt(PARAMS)
    factor = jnp.minimum(1.0, clip_limit / (grad_norm + 1e-06))
    part_rows = width // seq_count

    def rows_of_branch(values):
        return jnp.moveaxis(values, -3, -1).reshape(values.shape[:-3] + (2 * chan_width, part_rows))

    def branch_of_rows(values):
        return jnp.moveaxis(values.reshape(values.shape[:-2] + (2, chan_width, part_rows)), -1, -3)

    branch_new, branch_copy = map(
        branch_of_rows,
        adam_matrix(
            rows_of_branch(branch_state), rows_of_branch(branch_grad), factor, rate_matrix,
            weight_decay,
        ),
    )
    gate_rows_state = gate_state.reshape(4, -1, block_size)
    gate_new, gate_copy = adam_matrix(
        gate_rows_state, gate_grad.reshape(-1, block_size), factor, rate_gate, weight_decay
    )
    gate_new, gate_copy = gate_new.reshape(gate_state.shape), gate_copy.reshape(gate_grad.shape)
    mixer_new, mixer_copy = adam_matrix(mixer_state, mixer_grad, factor, rate_matrix, weight_decay)
    expand_new, expand_copy = adam_matrix(
        expand_state, expand_grad, factor, rate_matrix, weight_decay
    )
    shrink_new, shrink_copy = adam_matrix(
        shrink_state, shrink_grad, factor, rate_matrix, weight_decay
    )
    channel_all, _ = adam(channel_state, channel_grad, factor, rate_channel, 0.0)
    gains_new, _ = adam(gains_state, gains_grad, factor, rate_gains, 0.0)
    channel_new = jnp.stack([channel_all[0], channel_all[3]])
    channel_moments = channel_all[1:3]
    return (
        output,
        residual_grad,
        branch_grad,
        gate_grad,
        mixer_grad,
        expand_grad,
        shrink_grad,
        channel_grad,
        gains_grad,
        grad_norm,
        branch_new,
        gate_new,
        mixer_new,
        expand_new,
        shrink_new,
        channel_new,
        channel_moments,
        gains_new,
        branch_copy,
        gate_copy,
        mixer_copy,
        expand_copy,
        shrink_copy,
    )


def solution(mesh):
    in_specs = (
        P(("seq", "chan"), None),
        P(("seq", "chan"), None),
        P("seq"),
        P(None, None, "chan"),
        P(None, "chan", None, None),
        P("chan", None),
        P(None, None, "chan"),
        P("chan", None),
        P(None, "seq", None, "chan"),
        P(None, None, "chan", "seq", None),
        P(None, "chan", "seq"),
        P(None, "seq", None, "chan"),
        P(None, "chan", "seq"),
        P(None, None, "chan"),
        P(),
    )
    out_specs = (
        P(("seq", "chan"), None),
        P(("seq", "chan"), None),
        P("seq", None, "chan"),
        P(None, "chan", "seq", None),
        P("chan", "seq"),
        P("seq", None, "chan"),
        P("chan", "seq"),
        P(None, "chan"),
        P(),
        P(),
        P(None, "seq", None, "chan"),
        P(None, None, "chan", "seq", None),
        P(None, "chan", "seq"),
        P(None, "seq", None, "chan"),
        P(None, "chan", "seq"),
        P(None, None, "chan"),
        P(None, None, "chan"),
        P(),
        P("seq", None, "chan"),
        P(None, "chan", "seq", None),
        P("chan", "seq"),
        P("seq", None, "chan"),
        P("chan", "seq"),
    )
    return jax.shard_map(local, mesh=mesh, in_specs=in_specs, out_specs=out_specs, check_vma=False)
```

```python
import math

import jax
import jax.numpy as jnp
from jax import lax
from jax.experimental import pallas as pl
from jax.experimental.pallas import tpu as pltpu
from jax.sharding import PartitionSpec as P

CONV = 4
SEQ_LEN = 2048
SEQS = 2
STEP = 10
PARAMS = 54321152


norm_eps = 1e-06
lru_scale = 8.0
clip_rms = 0.4
beta_one = 0.9
beta_two = 0.95
adam_eps = 1e-08
weight_decay = 0.1
ema_keep = 0.99
rate_matrix = 0.02
rate_gate = 0.1
rate_channel = 1.0
rate_gains = 0.5
SUB = 8
TILE = 64
PARTS = TILE // SUB
GELU_SCALE = math.sqrt(2.0 / math.pi)
GELU_CUBE = 0.044715


def contract_rows(left_mat, right_mat):
    return lax.dot_general(
        left_mat, right_mat, (((0,), (0,)), ((), ())), preferred_element_type=jnp.float32
    )


def contract_cols(left_mat, right_mat):
    return lax.dot_general(
        left_mat, right_mat, (((1,), (1,)), ((), ())), preferred_element_type=jnp.float32
    )


def contract(left_mat, right_mat):
    return jnp.dot(left_mat, right_mat, preferred_element_type=jnp.float32)


def norm_back(values, scale, gain, upstream):
    scaled = gain * upstream
    return scale * scaled - values * scale * scale * scale * jnp.mean(
        scaled * values, axis=-1, keepdims=True
    )


def adam(old_state, gradient, factor, step_rate, decay_use):
    clipped = gradient * factor
    moment_one = beta_one * old_state[1] + (1.0 - beta_one) * clipped
    moment_two = beta_two * old_state[2] + (1.0 - beta_two) * clipped * clipped
    first_hat = moment_one / (1.0 - beta_one**STEP)
    second_hat = moment_two / (1.0 - beta_two**STEP)
    master = old_state[0] - step_rate * (
        first_hat / (jnp.sqrt(second_hat) + adam_eps) + decay_use * old_state[0]
    )
    average = ema_keep * old_state[3] + (1.0 - ema_keep) * master
    return (jnp.stack([master, moment_one, moment_two, average]), master)


def gelu_parts(values):
    square = values * values
    turn = jnp.tanh(GELU_SCALE * values * (1.0 + GELU_CUBE * square))
    half = 0.5 * (1.0 + turn)
    slope = half + 0.5 * values * (1.0 - turn * turn) * (
        GELU_SCALE * (1.0 + 3.0 * GELU_CUBE * square)
    )
    return values * half, slope


def decay_parts(log_decay):
    decay = jnp.exp(log_decay)
    z = 2.0 * log_decay
    series = 1.0 + z * (1.0 / 7.0)
    for order in (6.0, 5.0, 4.0, 3.0, 2.0):
        series = 1.0 + z * (1.0 / order) * series
    return decay, jnp.where(z > -0.35, -z * series, 1.0 - decay * decay)


def roll_down(values, offset):
    return pltpu.roll(values, offset, 0)


def roll_up(values, offset):
    return pltpu.roll(values, SUB - offset, 0)


def lru_forward_kernel(
    place_ref,
    normed_ref,
    gate_w_ref,
    recur_w_ref,
    mask_ref,
    rate_w_ref,
    input_w_ref,
    par_ref,
    mixed_ref,
    gate_ref,
    recur_ref,
    hidden_ref,
    conv_ref,
    rate_ref,
    admit_ref,
    rate_pre,
    input_pre,
    tail,
    state,
):
    block, width = gate_ref.shape

    @pl.when(pl.program_id(0) == 0)
    def _():
        tail[...] = jnp.zeros_like(tail)
        state[...] = jnp.zeros_like(state)

    normed = normed_ref[...]
    recur_ref[...] = contract_cols(normed, recur_w_ref[...])
    gate_ref[...] = contract_cols(normed, gate_w_ref[...])
    row = lax.broadcasted_iota(jnp.int32, (SUB, width), 0)

    def convolve(step, before):
        base = pl.multiple_of(step * TILE, TILE)
        halves = []
        for half in range(PARTS):
            rows = pl.ds(base + half * SUB, SUB)
            now = recur_ref[rows, :]
            masks = mask_ref[rows, :]
            total = par_ref[CONV : CONV + 1, :] + par_ref[0:1, :] * now
            for offset in range(1, CONV):
                moved = jnp.where(
                    row < offset, roll_down(before, offset), roll_down(now, offset)
                )
                total = total + par_ref[offset : offset + 1, :] * (
                    moved * masks[:, offset - 1 : offset]
                )
            halves.append(total)
            before = now
        conv_ref[pl.ds(base, TILE), :] = jnp.concatenate(halves, axis=0).astype(jnp.bfloat16)
        return before

    tail[...] = lax.fori_loop(0, block // TILE, convolve, tail[...])
    low = conv_ref[...]
    rate_pre[...] = contract(low, rate_w_ref[...])
    input_pre[...] = contract(low, input_w_ref[...])

    def advance(step, carry):
        base = pl.multiple_of(step * TILE, TILE)
        conv = conv_ref[pl.ds(base, TILE), :].astype(jnp.float32)
        halves = []
        for half in range(PARTS):
            rows = pl.ds(base + half * SUB, SUB)
            rate = jax.nn.sigmoid(rate_pre[rows, :] + par_ref[CONV + 1 : CONV + 2, :])
            admit = jax.nn.sigmoid(input_pre[rows, :] + par_ref[CONV + 2 : CONV + 3, :])
            decay, rest = decay_parts(par_ref[CONV + 3 : CONV + 4, :] * rate)
            coeff = decay * mask_ref[rows, 0:1]
            drive = jnp.sqrt(rest) * admit * conv[half * SUB : (half + 1) * SUB, :]
            for offset in (1, 2, 4):
                inner = row >= offset
                drive = drive + coeff * jnp.where(inner, roll_down(drive, offset), 0.0)
                coeff = coeff * jnp.where(inner, roll_down(coeff, offset), 1.0)
            hidden = drive + coeff * carry
            carry = jnp.broadcast_to(hidden[SUB - 1 : SUB, :], hidden.shape)
            hidden_ref[rows, :] = hidden
            rate_ref[rows, :] = rate
            admit_ref[rows, :] = admit
            branch = gate_ref[rows, :]
            turn = jnp.tanh(GELU_SCALE * branch * (1.0 + GELU_CUBE * branch * branch))
            halves.append(0.5 * branch * (1.0 + turn) * hidden)
        mixed_ref[pl.ds(base, TILE), :] = jnp.concatenate(halves, axis=0).astype(jnp.bfloat16)
        return carry

    state[...] = lax.fori_loop(0, block // TILE, advance, state[...])


def lru_backward_kernel(
    place_ref,
    back_ref,
    mixer_ref,
    gate_ref,
    recur_ref,
    hidden_ref,
    before_ref,
    conv_ref,
    rate_ref,
    admit_ref,
    mask_ref,
    rate_w_ref,
    input_w_ref,
    par_ref,
    gate_back_ref,
    recur_back_ref,
    rate_grad_ref,
    input_grad_ref,
    sums_ref,
    upstream_ref,
    rate_low,
    input_low,
    conv_back,
    state,
    ahead,
):
    block, width = gate_ref.shape
    steps = block // TILE

    @pl.when(pl.program_id(0) == 0)
    def _():
        state[...] = jnp.zeros_like(state)
        ahead[...] = jnp.zeros_like(ahead)
        sums_ref[...] = jnp.zeros_like(sums_ref)
        rate_grad_ref[...] = jnp.zeros_like(rate_grad_ref)
        input_grad_ref[...] = jnp.zeros_like(input_grad_ref)

    upstream_ref[...] = contract_cols(back_ref[...], mixer_ref[...])
    row = lax.broadcasted_iota(jnp.int32, (SUB, width), 0)

    def retreat(step, carry):
        carried_next, coeff_next = carry
        index = steps - 1 - step
        base = pl.multiple_of(index * TILE, TILE)
        conv_tile = conv_ref[pl.ds(base, TILE), :].astype(jnp.float32)
        lows = [[None] * PARTS for _ in range(3)]
        edge = pl.multiple_of(jnp.maximum(base - SUB, 0), SUB)
        earlier = jnp.where(index == 0, before_ref[...], hidden_ref[pl.ds(edge, SUB), :])
        for half in reversed(range(PARTS)):
            rows = pl.ds(base + half * SUB, SUB)
            conv = conv_tile[half * SUB : (half + 1) * SUB, :]
            rate = rate_ref[rows, :]
            admit = admit_ref[rows, :]
            speed = par_ref[CONV + 3 : CONV + 4, :]
            decay, rest = decay_parts(speed * rate)
            inverse = lax.rsqrt(rest)
            norm = rest * inverse
            coeff = decay * mask_ref[rows, 0:1]
            act, slope = gelu_parts(gate_ref[rows, :])
            upstream = upstream_ref[rows, :]
            hidden = hidden_ref[rows, :]
            carried = upstream * act
            chain = jnp.where(row == SUB - 1, coeff_next, roll_up(coeff, 1))
            for offset in (1, 2, 4):
                inner = row < SUB - offset
                carried = carried + chain * jnp.where(inner, roll_up(carried, offset), 0.0)
                chain = chain * jnp.where(inner, roll_up(chain, offset), 1.0)
            carried = carried + chain * carried_next
            carried_next = jnp.broadcast_to(carried[0:1, :], carried.shape)
            coeff_next = jnp.broadcast_to(coeff[0:1, :], coeff.shape)
            if half:
                last = hidden_ref[pl.ds(base + (half - 1) * SUB, SUB), :]
            else:
                last = earlier
            previous = jnp.where(row == 0, roll_down(last, 1), roll_down(hidden, 1))
            log_grad = carried * (
                previous * coeff - admit * conv * (decay * decay) * inverse
            )
            rate_back = log_grad * speed * rate * (1.0 - rate)
            drive = carried * norm
            direct = drive * admit
            input_back = drive * conv * admit * (1.0 - admit)
            conv_back[rows, :] = direct
            lows[0][half] = upstream * hidden * slope
            lows[1][half] = rate_back
            lows[2][half] = input_back
            sums_ref[5] += rate_back
            sums_ref[6] += input_back
            sums_ref[7] += log_grad * rate
        tile = pl.ds(base, TILE)
        gate_back_ref[tile, :] = jnp.concatenate(lows[0], axis=0).astype(jnp.bfloat16)
        rate_low[tile, :] = jnp.concatenate(lows[1], axis=0).astype(jnp.bfloat16)
        input_low[tile, :] = jnp.concatenate(lows[2], axis=0).astype(jnp.bfloat16)
        return carried_next, coeff_next

    carried_next, coeff_next = lax.fori_loop(0, steps, retreat, (state[0], state[1]))
    state[0] = carried_next
    state[1] = coeff_next
    low = conv_ref[...]
    rate_back_low = rate_low[...]
    input_back_low = input_low[...]
    rate_grad_ref[...] += contract_rows(low, rate_back_low)
    input_grad_ref[...] += contract_rows(low, input_back_low)
    conv_back[...] += contract_cols(rate_back_low, rate_w_ref[...]) + contract_cols(
        input_back_low, input_w_ref[...]
    )

    def unconvolve(step, carry):
        base = pl.multiple_of((steps - 1 - step) * TILE, TILE)
        halves = [None] * PARTS
        nexts = list(carry)
        for half in reversed(range(PARTS)):
            rows = pl.ds(base + half * SUB, SUB)
            grad = conv_back[rows, :]
            now = recur_ref[rows, :]
            masks = mask_ref[rows, :]
            sums_ref[0] += grad * now
            sums_ref[CONV] += grad
            total = par_ref[0:1, :] * grad
            for offset in range(1, CONV):
                kept = grad * masks[:, offset - 1 : offset]
                moved = jnp.where(
                    row < SUB - offset, roll_up(kept, offset), roll_up(nexts[offset - 1], offset)
                )
                nexts[offset - 1] = kept
                sums_ref[offset] += moved * now
                total = total + par_ref[offset : offset + 1, :] * moved
            halves[half] = total
        recur_back_ref[pl.ds(base, TILE), :] = jnp.concatenate(halves, axis=0).astype(jnp.bfloat16)
        return tuple(nexts)

    nexts = lax.fori_loop(0, steps, unconvolve, tuple(ahead[k] for k in range(CONV - 1)))
    for k in range(CONV - 1):
        ahead[k] = nexts[k]


def lru_sizes(rows, width, piece):
    block = min(256, piece)
    return block, rows // block, piece // block


def lru_forward(place, normed, gate_w, recur_w, masks, rate_w, input_w, params, piece):
    rows, depth = normed.shape
    width = gate_w.shape[0]
    block, count, per = lru_sizes(rows, width, piece)

    def there(i, place_ref):
        return (((i // per) ^ place_ref[0]) * per + i % per, 0)

    def here(i, place_ref):
        return (i, 0)

    def fixed(i, place_ref):
        return (0, 0)

    tall = lambda where: pl.BlockSpec((block, width), where)
    square = pl.BlockSpec((width, width), fixed)
    flat = pl.BlockSpec((width, depth), fixed)
    floats = jax.ShapeDtypeStruct((rows, width), jnp.float32)
    lows = jax.ShapeDtypeStruct((rows, width), jnp.bfloat16)
    return pl.pallas_call(
        lru_forward_kernel,
        grid_spec=pltpu.PrefetchScalarGridSpec(
            num_scalar_prefetch=1,
            grid=(count,),
            in_specs=[
                pl.BlockSpec((block, depth), there),
                flat,
                flat,
                pl.BlockSpec((block, SUB), here),
                square,
                square,
                pl.BlockSpec((2 * CONV, width), fixed),
            ],
            out_specs=[tall(there)] + [tall(here)] * 6,
            scratch_shapes=[
                pltpu.VMEM((block, width), jnp.float32),
                pltpu.VMEM((block, width), jnp.float32),
                pltpu.VMEM((SUB, width), jnp.float32),
                pltpu.VMEM((SUB, width), jnp.float32),
            ],
        ),
        out_shape=[lows, floats, floats, floats, lows, floats, floats],
        compiler_params=pltpu.CompilerParams(
            dimension_semantics=("arbitrary",), vmem_limit_bytes=48 * 2**20
        ),
        cost_estimate=pl.CostEstimate(
            flops=4 * rows * width * (width + depth),
            bytes_accessed=26 * rows * width + 2 * rows * depth,
            transcendentals=6 * rows * width,
        ),
        name="lru_forward",
    )(place, normed, gate_w, recur_w, masks, rate_w, input_w, params)


def lru_backward(
    place, back, mixer, gate_branch, recur_input, hidden, conv, rate, admit, masks, rate_w,
    input_w, params, piece,
):
    rows, depth = back.shape
    width = gate_branch.shape[1]
    block, count, per = lru_sizes(rows, width, piece)

    def there(i, place_ref):
        t = count - 1 - i
        return (((t // per) ^ place_ref[0]) * per + t % per, 0)

    def here(i, place_ref):
        return (count - 1 - i, 0)

    def before(i, place_ref):
        return (jnp.maximum((count - 1 - i) * (block // SUB) - 1, 0), 0)

    def fixed(i, place_ref):
        return (0, 0)

    tall = lambda where: pl.BlockSpec((block, width), where)
    square = pl.BlockSpec((width, width), fixed)
    return pl.pallas_call(
        lru_backward_kernel,
        grid_spec=pltpu.PrefetchScalarGridSpec(
            num_scalar_prefetch=1,
            grid=(count,),
            in_specs=[
                pl.BlockSpec((block, depth), there),
                pl.BlockSpec((width, depth), fixed),
                tall(here),
                tall(here),
                tall(here),
                pl.BlockSpec((SUB, width), before),
                tall(here),
                tall(here),
                tall(here),
                pl.BlockSpec((block, SUB), here),
                square,
                square,
                pl.BlockSpec((2 * CONV, width), fixed),
            ],
            out_specs=[
                tall(there),
                tall(there),
                square,
                square,
                pl.BlockSpec((2 * CONV, SUB, width), lambda i, place_ref: (0, 0, 0)),
            ],
            scratch_shapes=[
                pltpu.VMEM((block, width), jnp.float32),
                pltpu.VMEM((block, width), jnp.bfloat16),
                pltpu.VMEM((block, width), jnp.bfloat16),
                pltpu.VMEM((block, width), jnp.float32),
                pltpu.VMEM((2, SUB, width), jnp.float32),
                pltpu.VMEM((CONV - 1, SUB, width), jnp.float32),
            ],
        ),
        out_shape=[
            jax.ShapeDtypeStruct((rows, width), jnp.bfloat16),
            jax.ShapeDtypeStruct((rows, width), jnp.bfloat16),
            jax.ShapeDtypeStruct((width, width), jnp.float32),
            jax.ShapeDtypeStruct((width, width), jnp.float32),
            jax.ShapeDtypeStruct((2 * CONV, SUB, width), jnp.float32),
        ],
        compiler_params=pltpu.CompilerParams(
            dimension_semantics=("arbitrary",), vmem_limit_bytes=48 * 2**20
        ),
        cost_estimate=pl.CostEstimate(
            flops=8 * rows * width * width + 2 * rows * width * depth,
            bytes_accessed=30 * rows * width + 2 * rows * depth,
            transcendentals=6 * rows * width,
        ),
        name="lru_backward",
    )(
        place, back, mixer, gate_branch, recur_input, hidden, hidden, conv, rate, admit, masks,
        rate_w, input_w, params,
    )


def adam_kernel(step_rate, decay_use, factor_ref, state_ref, grad_ref, new_ref, copy_ref):
    clipped = grad_ref[...] * factor_ref[0, 0]
    master = state_ref[0]
    moment_one = beta_one * state_ref[1] + (1.0 - beta_one) * clipped
    moment_two = beta_two * state_ref[2] + (1.0 - beta_two) * clipped * clipped
    first_hat = moment_one * (1.0 / (1.0 - beta_one**STEP))
    second_hat = moment_two * (1.0 / (1.0 - beta_two**STEP))
    master = master - step_rate * (
        first_hat / (jnp.sqrt(second_hat) + adam_eps) + decay_use * master
    )
    new_ref[0] = master
    new_ref[1] = moment_one
    new_ref[2] = moment_two
    new_ref[3] = ema_keep * state_ref[3] + (1.0 - ema_keep) * master
    copy_ref[...] = master.astype(jnp.bfloat16)


def adam_matrix(state, gradient, factor, step_rate, decay_use):
    rows, rest = gradient.shape[0], gradient.shape[1:]
    goal = max(16, 2**17 // math.prod(rest))
    fits = [b for b in range(16, rows + 1, 16) if rows % b == 0 and (b <= goal or b == 16)]
    block = max(fits, default=rows)
    zeros = (0,) * len(rest)
    wide = pl.BlockSpec((4, block) + rest, lambda i: (0, i) + zeros)
    narrow = pl.BlockSpec((block,) + rest, lambda i: (i,) + zeros)
    return pl.pallas_call(
        lambda *refs: adam_kernel(step_rate, decay_use, *refs),
        grid=(rows // block,),
        in_specs=[pl.BlockSpec(memory_space=pltpu.SMEM), wide, narrow],
        out_specs=[wide, narrow],
        out_shape=[
            jax.ShapeDtypeStruct(state.shape, jnp.float32),
            jax.ShapeDtypeStruct(gradient.shape, jnp.bfloat16),
        ],
        compiler_params=pltpu.CompilerParams(
            dimension_semantics=("arbitrary",), vmem_limit_bytes=48 * 2**20
        ),
        cost_estimate=pl.CostEstimate(
            flops=20 * gradient.size, bytes_accessed=38 * gradient.size, transcendentals=0
        ),
        name="adam",
    )(factor.reshape(1, 1), state, gradient)


def swap(values, axis, bit):
    return lax.ppermute(
        values, axis, [(i, i ^ bit) for i in range(lax.axis_size(axis))]
    )


def bits_of(size):
    return [1 << k for k in reversed(range(size.bit_length() - 1))]


def later(values, *others):
    return lax.optimization_barrier((values,) + others)[0]


def tree_sum(terms):
    while len(terms) > 1:
        terms = [left + right for left, right in zip(terms[::2], terms[1::2])]
    return terms[0]


def sum_over(values, axis, step=1):
    others = range(step, lax.axis_size(axis), step)
    return tree_sum([values] + [swap(values, axis, other) for other in others])


def both(*values):
    return lax.optimization_barrier(values)


def gather_blocks(own, size):
    blocks = {0: own}
    for bit in bits_of(size):
        blocks.update({m | bit: swap(block, "chan", bit) for m, block in list(blocks.items())})
    return [blocks[m] for m in range(size)]


def lay_rows(blocks, room=1):
    rows = room * sum(block.shape[0] for block in blocks)
    return lay_more(jnp.zeros((rows,) + blocks[0].shape[1:], blocks[0].dtype), blocks, 0)


def lay_more(whole, blocks, start=None):
    if start is None:
        start = whole.shape[0] - sum(block.shape[0] for block in blocks)
    for block in blocks:
        whole = lax.dynamic_update_slice_in_dim(whole, block, start, axis=0)
        start += block.shape[0]
    return whole


def split_rows(mat, piece):
    return [mat[k * piece : (k + 1) * piece] for k in range(mat.shape[0] // piece)]


def scatter_near(partial, piece):
    blocks = dict(enumerate(split_rows(partial, piece)))
    came = []
    for bit in reversed(bits_of(len(blocks))):
        inward = {m: swap(blocks[m | bit], "chan", bit) for m in blocks if not m & bit}
        came += inward.values()
        blocks = {
            m: (blocks[m].astype(jnp.float32) + block.astype(jnp.float32)).astype(jnp.bfloat16)
            for m, block in inward.items()
        }
    return blocks[0], came


def rows_far(parts):
    return [part[part.shape[0] // 2 :] for part in parts]


def rows_near(parts):
    return [part[: part.shape[0] // 2] for part in parts]


def scatter_start(product, parts, size, piece, first=0):
    far = product(*rows_far(parts)).astype(jnp.bfloat16)
    total, came = scatter_near(far, piece)
    if first:
        sent = [swap(rows, "chan", size // 2) for rows in (total[:first], total[first:])]
    else:
        sent = swap(total, "chan", size // 2)
    return sent, came, far


def scatter_end(arrived, near, piece):
    total, _ = scatter_near(near, piece)
    return total.astype(jnp.float32) + arrived.astype(jnp.float32)


def block_diagonal(blocks):
    count, size, _ = blocks.shape
    return jnp.concatenate(
        [jnp.pad(blocks[k], ((0, 0), (k * size, (count - 1 - k) * size))) for k in range(count)],
        axis=0,
    )


def diagonal_blocks(matrix, count):
    size = matrix.shape[0] // count
    return jnp.stack(
        [matrix[k * size : (k + 1) * size, k * size : (k + 1) * size] for k in range(count)]
    )


def local(
    residual,
    cotangent,
    resets,
    branch_weights,
    gate_blocks,
    mixer_weights,
    expand_weights,
    shrink_weights,
    branch_state,
    gate_state,
    mixer_state,
    expand_state,
    shrink_state,
    channel_state,
    gains_state,
):
    seq_count = lax.axis_size("seq")
    group = lax.axis_size("chan") // SEQS
    seq_place = lax.axis_index("seq")
    chan_place = lax.axis_index("chan")
    place = (chan_place % group).astype(jnp.int32).reshape(1)
    width = residual.shape[1]
    piece = residual.shape[0]
    chan_width = branch_weights.shape[2]
    hidden_width = expand_weights.shape[2]
    block_count = gate_blocks.shape[1]

    def partner(values):
        return swap(values, "chan", group)

    def fetch_part(matrix):
        rows = matrix.shape[0] // seq_count
        return partner(lax.dynamic_slice_in_dim(matrix, seq_place * rows, rows, axis=0))

    def share(part):
        return lax.all_gather(part, "seq", axis=0, tiled=True)

    gains = gains_state[0]
    gain_first = 1.0 + gains[0]
    gain_second = 1.0 + gains[1]
    rows_float = residual.astype(jnp.float32)
    scale_one = lax.rsqrt(jnp.mean(rows_float * rows_float, axis=-1, keepdims=True) + norm_eps)
    normed_one = (rows_float * scale_one * gain_first).astype(jnp.bfloat16)
    side = group // 2
    own_branch = branch_weights.transpose(1, 2, 0)
    first_part = fetch_part(
        later(
            jnp.concatenate([own_branch.reshape(2 * chan_width, width), mixer_weights], axis=0),
            normed_one,
        )
    )
    half = piece // 2
    own_expand = expand_weights.reshape(width, 2 * hidden_width)
    normed_near = lay_rows(gather_blocks(normed_one, side), 2)
    normed_top, first_part, own_expand, normed_near = both(
        swap(normed_one[:half], "chan", side), first_part, own_expand, normed_near
    )
    others = share(first_part)
    other_branch = others[: 2 * chan_width].reshape(own_branch.shape)
    other_mixer = others[2 * chan_width :]
    branch_full = jnp.concatenate([own_branch, other_branch], axis=1)
    normed_end = swap(later(normed_one, normed_top)[half:], "chan", side)
    normed_far = gather_blocks(jnp.concatenate([normed_top, normed_end], axis=0), side)
    normed_all = lay_more(normed_near, normed_far)
    back_far = swap(later(cotangent, normed_end), "chan", side)
    expand_part = fetch_part(later(own_expand, normed_end))
    shrink_part = fetch_part(later(shrink_weights, normed_end))
    pair_width = 2 * hidden_width

    gate_full = jnp.concatenate([gate_blocks, partner(gate_blocks)], axis=1)
    rate_w = block_diagonal(gate_full[0])
    input_w = block_diagonal(gate_full[1])
    channel = channel_state[0]
    channel_full = jnp.concatenate([channel, partner(channel)], axis=1)
    speed = -lru_scale * jax.nn.softplus(channel_full[CONV + 3 :])
    params = jnp.concatenate([channel_full[: CONV + 3], speed], axis=0)

    flags = lax.dynamic_index_in_dim(
        resets.reshape(SEQS, SEQ_LEN), chan_place // group, axis=0, keepdims=False
    )
    stays = jnp.where(jnp.arange(SEQ_LEN) == 0, 0.0, 1.0 - (flags == 1).astype(jnp.float32))
    within = [stays]
    for offset in range(1, CONV - 1):
        within.append(within[-1] * jnp.pad(stays, (offset, 0))[:SEQ_LEN])
    masks = jnp.stack(within + [stays] * (SUB - len(within)), axis=1)

    mixed, gate_branch, recur_input, hidden, conv_low, rate, admit = lru_forward(
        place, normed_all, branch_full[0], branch_full[1], masks, rate_w, input_w, params, piece
    )
    mixed, back_far, expand_part = both(mixed, back_far, expand_part)
    mixer_full = jnp.concatenate([mixer_weights, other_mixer], axis=0)
    back_all = lay_rows(gather_blocks(cotangent, side) + gather_blocks(back_far, side))
    other_expand = share(expand_part)
    expand_full = jnp.concatenate(
        [
            own_expand[:, :hidden_width],
            other_expand[:, :hidden_width],
            own_expand[:, hidden_width:],
            other_expand[:, hidden_width:],
        ],
        axis=1,
    )
    through_mixer = lambda left: contract(left, mixer_full)
    arrived, came, _ = scatter_start(through_mixer, [mixed], group, piece)
    near = through_mixer(*rows_near([later(mixed, *came)])).astype(jnp.bfloat16)
    arrived, shrink_part = both(arrived, shrink_part)
    middle = rows_float + scatter_end(arrived, near, piece)
    scale_two = lax.rsqrt(jnp.mean(middle * middle, axis=-1, keepdims=True) + norm_eps)
    normed_two = (middle * scale_two * gain_second).astype(jnp.bfloat16)
    shrink_full = lay_rows([shrink_weights, share(later(shrink_part, other_expand))])
    mlp_near = lay_rows(gather_blocks(normed_two, side), 2)
    mlp_far, mlp_near, back_all, expand_full = both(
        swap(normed_two, "chan", side), mlp_near, back_all, expand_full
    )
    normed_mlp = lay_more(mlp_near, gather_blocks(mlp_far, side))
    expanded = contract(normed_mlp, expand_full)
    product_grad = contract_cols(back_all, shrink_full)
    up_part = expanded[:, pair_width:]
    act_part, slope_part = gelu_parts(expanded[:, :pair_width])
    product_low = (act_part * up_part).astype(jnp.bfloat16)
    gate_grad_low = (product_grad * up_part * slope_part).astype(jnp.bfloat16)
    up_grad_low = (product_grad * act_part).astype(jnp.bfloat16)
    def reduce_seq(matrix):
        return lax.psum_scatter(
            matrix.astype(jnp.bfloat16), "seq", scatter_dimension=0, tiled=True
        )

    def through_expand(*grads):
        return contract_cols(jnp.concatenate(grads, axis=1), expand_full)

    def through_shrink(left):
        return contract(left, shrink_full)

    arrived, came, _ = scatter_start(through_expand, [gate_grad_low, up_grad_low], group, piece)
    gate_grad_low, up_grad_low, product_low, *_ = both(
        gate_grad_low, up_grad_low, product_low, *came
    )
    expand_local = contract_rows(
        normed_mlp, jnp.concatenate([gate_grad_low, up_grad_low], axis=1)
    ).astype(jnp.bfloat16)
    arrived, expand_local, gate_grad_low = both(arrived, expand_local, gate_grad_low)
    near = through_expand(*rows_near([gate_grad_low, up_grad_low])).astype(jnp.bfloat16)
    expand_sum = reduce_seq(expand_local)
    normed_two_grad = scatter_end(arrived, near, piece)
    back_float = cotangent.astype(jnp.float32)
    middle_grad = back_float + norm_back(middle, scale_two, gain_second, normed_two_grad)
    middle_low = middle_grad.astype(jnp.bfloat16)
    product_low = later(product_low, middle_low)
    shrink_local = contract_rows(back_all, product_low).astype(jnp.bfloat16)
    middle_near = lay_rows(gather_blocks(middle_low, side), 2)
    product_low = later(product_low, shrink_local)
    out_arrived, _, out_far = scatter_start(through_shrink, [product_low], group, piece)
    out_near = through_shrink(*rows_near([later(product_low, out_far)])).astype(jnp.bfloat16)
    middle_far, shrink_local, middle_near, out_near, mixer_full = both(
        swap(middle_low, "chan", side), shrink_local, middle_near, out_near, mixer_full
    )
    shrink_sum = reduce_seq(shrink_local)
    branch_back = lay_more(middle_near, gather_blocks(middle_far, side))
    gain_two = jnp.sum(normed_two_grad * middle * scale_two, axis=0)

    def settle(part, pieces, each):
        mine = [part[:, 2 * k * each : (2 * k + 1) * each] for k in range(pieces)]
        theirs = [part[:, (2 * k + 1) * each : (2 * k + 2) * each] for k in range(pieces)]
        return jnp.concatenate(mine, axis=1), partner(jnp.concatenate(theirs, axis=1))

    def total(pair):
        return pair[0].astype(jnp.float32) + pair[1].astype(jnp.float32)

    mixer_local = contract_rows(branch_back, mixed).astype(jnp.bfloat16)
    mixer_sum = reduce_seq(mixer_local)
    expand_pair = settle(expand_sum, 2, hidden_width)
    gate_back, recur_back, rate_w_grad, input_w_grad, sums = lru_backward(
        place, later(branch_back, mixer_local), mixer_full, gate_branch, recur_input, hidden,
        conv_low, rate, admit, masks, rate_w, input_w, params, piece,
    )
    gate_back, out_arrived, expand_theirs = both(gate_back, out_arrived, expand_pair[1])
    expand_pair = (expand_pair[0], expand_theirs)
    branch_back_low = jnp.concatenate([gate_back, recur_back], axis=1)
    through_branch = lambda left: contract(left, branch_full.reshape(4 * chan_width, width))
    branch_local = contract_rows(normed_all, branch_back_low).astype(jnp.bfloat16)
    branch_back_low = later(branch_back_low, branch_local)
    arrived, _, far = scatter_start(through_branch, [branch_back_low], group, piece, TILE)
    branch_back_low, arrived[0] = both(branch_back_low, arrived[0])
    arrived = jnp.concatenate(arrived, axis=0)
    block_size = gate_blocks.shape[2]
    part_rows = width // seq_count
    gate_pair = jnp.stack(
        [
            diagonal_blocks(rate_w_grad, 2 * block_count),
            diagonal_blocks(input_w_grad, 2 * block_count),
        ]
    ).astype(jnp.bfloat16)
    gate_parts = (2, 2, block_count, seq_count, block_size // seq_count, block_size)
    gate_pair = gate_pair.reshape(gate_parts).transpose(3, 1, 0, 2, 4, 5)
    gate_shape = gate_pair.shape[1:]
    gate_count = math.prod(gate_shape[:-1])
    gate_rows = jnp.pad(
        gate_pair.reshape(seq_count, gate_count, block_size),
        ((0, 0), (0, part_rows - gate_count), (0, 0)),
    ).reshape(width, block_size)
    branch_sum = reduce_seq(jnp.concatenate([branch_local, gate_rows], axis=1))
    shrink_pair = settle(later(shrink_sum, branch_local), 1, hidden_width)
    near = through_branch(*rows_near([branch_back_low])).astype(jnp.bfloat16)
    mixer_pair = settle(later(mixer_sum, near), 1, chan_width)
    sums = later(sums, branch_local)
    expand_grad = total(expand_pair).reshape(-1, 2, hidden_width)
    channel_pair = jnp.sum(sums, axis=1)
    channel_pair = jnp.concatenate(
        [
            channel_pair[: CONV + 3],
            channel_pair[CONV + 3 :] * -lru_scale * jax.nn.sigmoid(channel_full[CONV + 3 :]),
        ],
        axis=0,
    )
    channel_own = channel_pair[:, :chan_width] + partner(channel_pair[:, chan_width:])
    output = (middle + scatter_end(out_arrived, out_near, piece)).astype(jnp.bfloat16)
    normed_one_grad = scatter_end(arrived, near, piece)
    gain_one = jnp.sum(normed_one_grad * rows_float * scale_one, axis=0)
    residual_grad = middle_grad + norm_back(rows_float, scale_one, gain_first, normed_one_grad)
    (
        branch_sum, residual_grad, gain_one, gain_two, output, channel_own, shrink_theirs,
        mixer_theirs, expand_grad,
    ) = both(
        branch_sum, residual_grad, gain_one, gain_two, output, channel_own, shrink_pair[1],
        mixer_pair[1], expand_grad,
    )
    mixer_pair = (mixer_pair[0], mixer_theirs)
    shrink_pair = (shrink_pair[0], shrink_theirs)
    gate_part = branch_sum[:gate_count, 4 * chan_width :].reshape(gate_shape)
    gate_pair = (gate_part[0], partner(gate_part[1]))
    branch_pair = settle(branch_sum[:, : 4 * chan_width], 2, chan_width)
    shrink_grad = total(shrink_pair).T
    mixer_grad = total(mixer_pair).T
    branch_grad = total(branch_pair).reshape(-1, 2, chan_width)
    gate_grad = total(gate_pair)
    grad_shards = (branch_grad, gate_grad, mixer_grad, expand_grad, shrink_grad)
    own_squares = sum((jnp.sum(shard_grad * shard_grad) for shard_grad in grad_shards))
    lanes = 128
    packed = sum_over(
        jnp.concatenate(
            [
                gain_one,
                gain_two,
                jnp.full((lanes,), own_squares),
                channel_own.reshape(-1),
            ]
        ),
        "seq",
    )
    channel_grad = packed[2 * width + lanes :].reshape(channel_own.shape)
    packed = jnp.concatenate(
        [
            packed[: 2 * width],
            packed[2 * width : 2 * width + lanes] + jnp.sum(channel_grad * channel_grad),
        ]
    )
    packed = packed + swap(packed, "chan", 1)
    packed = sum_over(packed, "chan", 2)
    gains_grad = packed[: 2 * width].reshape(2, width)
    grad_norm = jnp.sqrt(packed[2 * width] + jnp.sum(gains_grad * gains_grad))
    clip_limit = clip_rms * math.sqrt(PARAMS)
    factor = jnp.minimum(1.0, clip_limit / (grad_norm + 1e-06))

    def rows_of_branch(values):
        return jnp.moveaxis(values, -3, -1).reshape(values.shape[:-3] + (2 * chan_width, part_rows))

    def branch_of_rows(values):
        return jnp.moveaxis(values.reshape(values.shape[:-2] + (2, chan_width, part_rows)), -1, -3)

    branch_new, branch_copy = map(
        branch_of_rows,
        adam_matrix(
            rows_of_branch(branch_state), rows_of_branch(branch_grad), factor, rate_matrix,
            weight_decay,
        ),
    )
    gate_rows_state = gate_state.reshape(4, -1, block_size)
    gate_new, gate_copy = adam_matrix(
        gate_rows_state, gate_grad.reshape(-1, block_size), factor, rate_gate, weight_decay
    )
    gate_new, gate_copy = gate_new.reshape(gate_state.shape), gate_copy.reshape(gate_grad.shape)
    mixer_new, mixer_copy = adam_matrix(mixer_state, mixer_grad, factor, rate_matrix, weight_decay)
    expand_new, expand_copy = adam_matrix(
        expand_state, expand_grad, factor, rate_matrix, weight_decay
    )
    shrink_new, shrink_copy = adam_matrix(
        shrink_state, shrink_grad, factor, rate_matrix, weight_decay
    )
    channel_all, _ = adam(channel_state, channel_grad, factor, rate_channel, 0.0)
    gains_new, _ = adam(gains_state, gains_grad, factor, rate_gains, 0.0)
    channel_new = jnp.stack([channel_all[0], channel_all[3]])
    channel_moments = channel_all[1:3]
    return (
        output,
        residual_grad,
        branch_grad,
        gate_grad,
        mixer_grad,
        expand_grad,
        shrink_grad,
        channel_grad,
        gains_grad,
        grad_norm,
        branch_new,
        gate_new,
        mixer_new,
        expand_new,
        shrink_new,
        channel_new,
        channel_moments,
        gains_new,
        branch_copy,
        gate_copy,
        mixer_copy,
        expand_copy,
        shrink_copy,
    )


def solution(mesh):
    in_specs = (
        P(("seq", "chan"), None),
        P(("seq", "chan"), None),
        P("seq"),
        P(None, None, "chan"),
        P(None, "chan", None, None),
        P("chan", None),
        P(None, None, "chan"),
        P("chan", None),
        P(None, "seq", None, "chan"),
        P(None, None, "chan", "seq", None),
        P(None, "chan", "seq"),
        P(None, "seq", None, "chan"),
        P(None, "chan", "seq"),
        P(None, None, "chan"),
        P(),
    )
    out_specs = (
        P(("seq", "chan"), None),
        P(("seq", "chan"), None),
        P("seq", None, "chan"),
        P(None, "chan", "seq", None),
        P("chan", "seq"),
        P("seq", None, "chan"),
        P("chan", "seq"),
        P(None, "chan"),
        P(),
        P(),
        P(None, "seq", None, "chan"),
        P(None, None, "chan", "seq", None),
        P(None, "chan", "seq"),
        P(None, "seq", None, "chan"),
        P(None, "chan", "seq"),
        P(None, None, "chan"),
        P(None, None, "chan"),
        P(),
        P("seq", None, "chan"),
        P(None, "chan", "seq", None),
        P("chan", "seq"),
        P("seq", None, "chan"),
        P("chan", "seq"),
    )
    return jax.shard_map(local, mesh=mesh, in_specs=in_specs, out_specs=out_specs, check_vma=False)
```

```python
import math

import jax
import jax.numpy as jnp
from jax import lax
from jax.experimental import pallas as pl
from jax.experimental.pallas import tpu as pltpu
from jax.sharding import PartitionSpec as P

CONV = 4
SEQ_LEN = 2048
SEQS = 2
STEP = 10
PARAMS = 54321152


norm_eps = 1e-06
lru_scale = 8.0
clip_rms = 0.4
beta_one = 0.9
beta_two = 0.95
adam_eps = 1e-08
weight_decay = 0.1
ema_keep = 0.99
rate_matrix = 0.02
rate_gate = 0.1
rate_channel = 1.0
rate_gains = 0.5
SUB = 8
TILE = 64
PARTS = TILE // SUB
GELU_SCALE = math.sqrt(2.0 / math.pi)
GELU_CUBE = 0.044715


def contract_rows(left_mat, right_mat):
    return lax.dot_general(
        left_mat, right_mat, (((0,), (0,)), ((), ())), preferred_element_type=jnp.float32
    )


def contract_cols(left_mat, right_mat):
    return lax.dot_general(
        left_mat, right_mat, (((1,), (1,)), ((), ())), preferred_element_type=jnp.float32
    )


def contract(left_mat, right_mat):
    return jnp.dot(left_mat, right_mat, preferred_element_type=jnp.float32)


def norm_back(values, scale, gain, upstream):
    scaled = gain * upstream
    return scale * scaled - values * scale * scale * scale * jnp.mean(
        scaled * values, axis=-1, keepdims=True
    )


def adam(old_state, gradient, factor, step_rate, decay_use):
    clipped = gradient * factor
    moment_one = beta_one * old_state[1] + (1.0 - beta_one) * clipped
    moment_two = beta_two * old_state[2] + (1.0 - beta_two) * clipped * clipped
    first_hat = moment_one / (1.0 - beta_one**STEP)
    second_hat = moment_two / (1.0 - beta_two**STEP)
    master = old_state[0] - step_rate * (
        first_hat / (jnp.sqrt(second_hat) + adam_eps) + decay_use * old_state[0]
    )
    average = ema_keep * old_state[3] + (1.0 - ema_keep) * master
    return (jnp.stack([master, moment_one, moment_two, average]), master)


def gelu_parts(values):
    square = values * values
    turn = jnp.tanh(GELU_SCALE * values * (1.0 + GELU_CUBE * square))
    half = 0.5 * (1.0 + turn)
    slope = half + 0.5 * values * (1.0 - turn * turn) * (
        GELU_SCALE * (1.0 + 3.0 * GELU_CUBE * square)
    )
    return values * half, slope


def decay_parts(log_decay):
    decay = jnp.exp(log_decay)
    z = 2.0 * log_decay
    series = 1.0 + z * (1.0 / 7.0)
    for order in (6.0, 5.0, 4.0, 3.0, 2.0):
        series = 1.0 + z * (1.0 / order) * series
    return decay, jnp.where(z > -0.35, -z * series, 1.0 - decay * decay)


def roll_down(values, offset):
    return pltpu.roll(values, offset, 0)


def roll_up(values, offset):
    return pltpu.roll(values, SUB - offset, 0)


def lru_forward_kernel(
    place_ref,
    normed_ref,
    gate_w_ref,
    recur_w_ref,
    mask_ref,
    rate_w_ref,
    input_w_ref,
    par_ref,
    mixed_ref,
    gate_ref,
    recur_ref,
    hidden_ref,
    conv_ref,
    rate_ref,
    admit_ref,
    rate_pre,
    input_pre,
    tail,
    state,
):
    block, width = gate_ref.shape

    @pl.when(pl.program_id(0) == 0)
    def _():
        tail[...] = jnp.zeros_like(tail)
        state[...] = jnp.zeros_like(state)

    normed = normed_ref[...]
    recur_ref[...] = contract_cols(normed, recur_w_ref[...])
    gate_ref[...] = contract_cols(normed, gate_w_ref[...])
    row = lax.broadcasted_iota(jnp.int32, (SUB, width), 0)

    def convolve(step, before):
        base = pl.multiple_of(step * TILE, TILE)
        halves = []
        for half in range(PARTS):
            rows = pl.ds(base + half * SUB, SUB)
            now = recur_ref[rows, :]
            masks = mask_ref[rows, :]
            total = par_ref[CONV : CONV + 1, :] + par_ref[0:1, :] * now
            for offset in range(1, CONV):
                moved = jnp.where(
                    row < offset, roll_down(before, offset), roll_down(now, offset)
                )
                total = total + par_ref[offset : offset + 1, :] * (
                    moved * masks[:, offset - 1 : offset]
                )
            halves.append(total)
            before = now
        conv_ref[pl.ds(base, TILE), :] = jnp.concatenate(halves, axis=0).astype(jnp.bfloat16)
        return before

    tail[...] = lax.fori_loop(0, block // TILE, convolve, tail[...])
    low = conv_ref[...]
    rate_pre[...] = contract(low, rate_w_ref[...])
    input_pre[...] = contract(low, input_w_ref[...])

    def advance(step, carry):
        base = pl.multiple_of(step * TILE, TILE)
        conv = conv_ref[pl.ds(base, TILE), :].astype(jnp.float32)
        halves = []
        for half in range(PARTS):
            rows = pl.ds(base + half * SUB, SUB)
            rate = jax.nn.sigmoid(rate_pre[rows, :] + par_ref[CONV + 1 : CONV + 2, :])
            admit = jax.nn.sigmoid(input_pre[rows, :] + par_ref[CONV + 2 : CONV + 3, :])
            decay, rest = decay_parts(par_ref[CONV + 3 : CONV + 4, :] * rate)
            coeff = decay * mask_ref[rows, 0:1]
            drive = jnp.sqrt(rest) * admit * conv[half * SUB : (half + 1) * SUB, :]
            for offset in (1, 2, 4):
                inner = row >= offset
                drive = drive + coeff * jnp.where(inner, roll_down(drive, offset), 0.0)
                coeff = coeff * jnp.where(inner, roll_down(coeff, offset), 1.0)
            hidden = drive + coeff * carry
            carry = jnp.broadcast_to(hidden[SUB - 1 : SUB, :], hidden.shape)
            hidden_ref[rows, :] = hidden
            rate_ref[rows, :] = rate
            admit_ref[rows, :] = admit
            branch = gate_ref[rows, :]
            turn = jnp.tanh(GELU_SCALE * branch * (1.0 + GELU_CUBE * branch * branch))
            halves.append(0.5 * branch * (1.0 + turn) * hidden)
        mixed_ref[pl.ds(base, TILE), :] = jnp.concatenate(halves, axis=0).astype(jnp.bfloat16)
        return carry

    state[...] = lax.fori_loop(0, block // TILE, advance, state[...])


def lru_backward_kernel(
    place_ref,
    back_ref,
    mixer_ref,
    gate_ref,
    recur_ref,
    hidden_ref,
    before_ref,
    conv_ref,
    rate_ref,
    admit_ref,
    mask_ref,
    rate_w_ref,
    input_w_ref,
    par_ref,
    gate_back_ref,
    recur_back_ref,
    rate_grad_ref,
    input_grad_ref,
    sums_ref,
    upstream_ref,
    rate_low,
    input_low,
    conv_back,
    state,
    ahead,
):
    block, width = gate_ref.shape
    steps = block // TILE

    @pl.when(pl.program_id(0) == 0)
    def _():
        state[...] = jnp.zeros_like(state)
        ahead[...] = jnp.zeros_like(ahead)
        sums_ref[...] = jnp.zeros_like(sums_ref)
        rate_grad_ref[...] = jnp.zeros_like(rate_grad_ref)
        input_grad_ref[...] = jnp.zeros_like(input_grad_ref)

    upstream_ref[...] = contract_cols(back_ref[...], mixer_ref[...])
    row = lax.broadcasted_iota(jnp.int32, (SUB, width), 0)

    def retreat(step, carry):
        carried_next, coeff_next = carry
        index = steps - 1 - step
        base = pl.multiple_of(index * TILE, TILE)
        conv_tile = conv_ref[pl.ds(base, TILE), :].astype(jnp.float32)
        lows = [[None] * PARTS for _ in range(3)]
        edge = pl.multiple_of(jnp.maximum(base - SUB, 0), SUB)
        earlier = jnp.where(index == 0, before_ref[...], hidden_ref[pl.ds(edge, SUB), :])
        for half in reversed(range(PARTS)):
            rows = pl.ds(base + half * SUB, SUB)
            conv = conv_tile[half * SUB : (half + 1) * SUB, :]
            rate = rate_ref[rows, :]
            admit = admit_ref[rows, :]
            speed = par_ref[CONV + 3 : CONV + 4, :]
            decay, rest = decay_parts(speed * rate)
            inverse = lax.rsqrt(rest)
            norm = rest * inverse
            coeff = decay * mask_ref[rows, 0:1]
            act, slope = gelu_parts(gate_ref[rows, :])
            upstream = upstream_ref[rows, :]
            hidden = hidden_ref[rows, :]
            carried = upstream * act
            chain = jnp.where(row == SUB - 1, coeff_next, roll_up(coeff, 1))
            for offset in (1, 2, 4):
                inner = row < SUB - offset
                carried = carried + chain * jnp.where(inner, roll_up(carried, offset), 0.0)
                chain = chain * jnp.where(inner, roll_up(chain, offset), 1.0)
            carried = carried + chain * carried_next
            carried_next = jnp.broadcast_to(carried[0:1, :], carried.shape)
            coeff_next = jnp.broadcast_to(coeff[0:1, :], coeff.shape)
            if half:
                last = hidden_ref[pl.ds(base + (half - 1) * SUB, SUB), :]
            else:
                last = earlier
            previous = jnp.where(row == 0, roll_down(last, 1), roll_down(hidden, 1))
            log_grad = carried * (
                previous * coeff - admit * conv * (decay * decay) * inverse
            )
            rate_back = log_grad * speed * rate * (1.0 - rate)
            drive = carried * norm
            direct = drive * admit
            input_back = drive * conv * admit * (1.0 - admit)
            conv_back[rows, :] = direct
            lows[0][half] = upstream * hidden * slope
            lows[1][half] = rate_back
            lows[2][half] = input_back
            sums_ref[5] += rate_back
            sums_ref[6] += input_back
            sums_ref[7] += log_grad * rate
        tile = pl.ds(base, TILE)
        gate_back_ref[tile, :] = jnp.concatenate(lows[0], axis=0).astype(jnp.bfloat16)
        rate_low[tile, :] = jnp.concatenate(lows[1], axis=0).astype(jnp.bfloat16)
        input_low[tile, :] = jnp.concatenate(lows[2], axis=0).astype(jnp.bfloat16)
        return carried_next, coeff_next

    carried_next, coeff_next = lax.fori_loop(0, steps, retreat, (state[0], state[1]))
    state[0] = carried_next
    state[1] = coeff_next
    low = conv_ref[...]
    rate_back_low = rate_low[...]
    input_back_low = input_low[...]
    rate_grad_ref[...] += contract_rows(low, rate_back_low)
    input_grad_ref[...] += contract_rows(low, input_back_low)
    conv_back[...] += contract_cols(rate_back_low, rate_w_ref[...]) + contract_cols(
        input_back_low, input_w_ref[...]
    )

    def unconvolve(step, carry):
        base = pl.multiple_of((steps - 1 - step) * TILE, TILE)
        halves = [None] * PARTS
        nexts = list(carry)
        for half in reversed(range(PARTS)):
            rows = pl.ds(base + half * SUB, SUB)
            grad = conv_back[rows, :]
            now = recur_ref[rows, :]
            masks = mask_ref[rows, :]
            sums_ref[0] += grad * now
            sums_ref[CONV] += grad
            total = par_ref[0:1, :] * grad
            for offset in range(1, CONV):
                kept = grad * masks[:, offset - 1 : offset]
                moved = jnp.where(
                    row < SUB - offset, roll_up(kept, offset), roll_up(nexts[offset - 1], offset)
                )
                nexts[offset - 1] = kept
                sums_ref[offset] += moved * now
                total = total + par_ref[offset : offset + 1, :] * moved
            halves[half] = total
        recur_back_ref[pl.ds(base, TILE), :] = jnp.concatenate(halves, axis=0).astype(jnp.bfloat16)
        return tuple(nexts)

    nexts = lax.fori_loop(0, steps, unconvolve, tuple(ahead[k] for k in range(CONV - 1)))
    for k in range(CONV - 1):
        ahead[k] = nexts[k]


def lru_sizes(rows, width, piece):
    block = min(256, piece)
    return block, rows // block, piece // block


def lru_forward(place, normed, gate_w, recur_w, masks, rate_w, input_w, params, piece):
    rows, depth = normed.shape
    width = gate_w.shape[0]
    block, count, per = lru_sizes(rows, width, piece)

    def there(i, place_ref):
        return (((i // per) ^ place_ref[0]) * per + i % per, 0)

    def here(i, place_ref):
        return (i, 0)

    def fixed(i, place_ref):
        return (0, 0)

    tall = lambda where: pl.BlockSpec((block, width), where)
    square = pl.BlockSpec((width, width), fixed)
    flat = pl.BlockSpec((width, depth), fixed)
    floats = jax.ShapeDtypeStruct((rows, width), jnp.float32)
    lows = jax.ShapeDtypeStruct((rows, width), jnp.bfloat16)
    return pl.pallas_call(
        lru_forward_kernel,
        grid_spec=pltpu.PrefetchScalarGridSpec(
            num_scalar_prefetch=1,
            grid=(count,),
            in_specs=[
                pl.BlockSpec((block, depth), there),
                flat,
                flat,
                pl.BlockSpec((block, SUB), here),
                square,
                square,
                pl.BlockSpec((2 * CONV, width), fixed),
            ],
            out_specs=[tall(there)] + [tall(here)] * 6,
            scratch_shapes=[
                pltpu.VMEM((block, width), jnp.float32),
                pltpu.VMEM((block, width), jnp.float32),
                pltpu.VMEM((SUB, width), jnp.float32),
                pltpu.VMEM((SUB, width), jnp.float32),
            ],
        ),
        out_shape=[lows, floats, floats, floats, lows, floats, floats],
        compiler_params=pltpu.CompilerParams(
            dimension_semantics=("arbitrary",), vmem_limit_bytes=48 * 2**20
        ),
        cost_estimate=pl.CostEstimate(
            flops=4 * rows * width * (width + depth),
            bytes_accessed=26 * rows * width + 2 * rows * depth,
            transcendentals=6 * rows * width,
        ),
        name="lru_forward",
    )(place, normed, gate_w, recur_w, masks, rate_w, input_w, params)


def lru_backward(
    place, back, mixer, gate_branch, recur_input, hidden, conv, rate, admit, masks, rate_w,
    input_w, params, piece,
):
    rows, depth = back.shape
    width = gate_branch.shape[1]
    block, count, per = lru_sizes(rows, width, piece)

    def there(i, place_ref):
        t = count - 1 - i
        return (((t // per) ^ place_ref[0]) * per + t % per, 0)

    def here(i, place_ref):
        return (count - 1 - i, 0)

    def before(i, place_ref):
        return (jnp.maximum((count - 1 - i) * (block // SUB) - 1, 0), 0)

    def fixed(i, place_ref):
        return (0, 0)

    tall = lambda where: pl.BlockSpec((block, width), where)
    square = pl.BlockSpec((width, width), fixed)
    return pl.pallas_call(
        lru_backward_kernel,
        grid_spec=pltpu.PrefetchScalarGridSpec(
            num_scalar_prefetch=1,
            grid=(count,),
            in_specs=[
                pl.BlockSpec((block, depth), there),
                pl.BlockSpec((width, depth), fixed),
                tall(here),
                tall(here),
                tall(here),
                pl.BlockSpec((SUB, width), before),
                tall(here),
                tall(here),
                tall(here),
                pl.BlockSpec((block, SUB), here),
                square,
                square,
                pl.BlockSpec((2 * CONV, width), fixed),
            ],
            out_specs=[
                tall(there),
                tall(there),
                square,
                square,
                pl.BlockSpec((2 * CONV, SUB, width), lambda i, place_ref: (0, 0, 0)),
            ],
            scratch_shapes=[
                pltpu.VMEM((block, width), jnp.float32),
                pltpu.VMEM((block, width), jnp.bfloat16),
                pltpu.VMEM((block, width), jnp.bfloat16),
                pltpu.VMEM((block, width), jnp.float32),
                pltpu.VMEM((2, SUB, width), jnp.float32),
                pltpu.VMEM((CONV - 1, SUB, width), jnp.float32),
            ],
        ),
        out_shape=[
            jax.ShapeDtypeStruct((rows, width), jnp.bfloat16),
            jax.ShapeDtypeStruct((rows, width), jnp.bfloat16),
            jax.ShapeDtypeStruct((width, width), jnp.float32),
            jax.ShapeDtypeStruct((width, width), jnp.float32),
            jax.ShapeDtypeStruct((2 * CONV, SUB, width), jnp.float32),
        ],
        compiler_params=pltpu.CompilerParams(
            dimension_semantics=("arbitrary",), vmem_limit_bytes=48 * 2**20
        ),
        cost_estimate=pl.CostEstimate(
            flops=8 * rows * width * width + 2 * rows * width * depth,
            bytes_accessed=30 * rows * width + 2 * rows * depth,
            transcendentals=6 * rows * width,
        ),
        name="lru_backward",
    )(
        place, back, mixer, gate_branch, recur_input, hidden, hidden, conv, rate, admit, masks,
        rate_w, input_w, params,
    )


def adam_kernel(step_rate, decay_use, factor_ref, state_ref, grad_ref, new_ref, copy_ref):
    clipped = grad_ref[...] * factor_ref[0, 0]
    master = state_ref[0]
    moment_one = beta_one * state_ref[1] + (1.0 - beta_one) * clipped
    moment_two = beta_two * state_ref[2] + (1.0 - beta_two) * clipped * clipped
    first_hat = moment_one * (1.0 / (1.0 - beta_one**STEP))
    second_hat = moment_two * (1.0 / (1.0 - beta_two**STEP))
    master = master - step_rate * (
        first_hat / (jnp.sqrt(second_hat) + adam_eps) + decay_use * master
    )
    new_ref[0] = master
    new_ref[1] = moment_one
    new_ref[2] = moment_two
    new_ref[3] = ema_keep * state_ref[3] + (1.0 - ema_keep) * master
    copy_ref[...] = master.astype(jnp.bfloat16)


def adam_matrix(state, gradient, factor, step_rate, decay_use):
    rows, rest = gradient.shape[0], gradient.shape[1:]
    goal = max(16, 2**17 // math.prod(rest))
    fits = [b for b in range(16, rows + 1, 16) if rows % b == 0 and (b <= goal or b == 16)]
    block = max(fits, default=rows)
    zeros = (0,) * len(rest)
    wide = pl.BlockSpec((4, block) + rest, lambda i: (0, i) + zeros)
    narrow = pl.BlockSpec((block,) + rest, lambda i: (i,) + zeros)
    return pl.pallas_call(
        lambda *refs: adam_kernel(step_rate, decay_use, *refs),
        grid=(rows // block,),
        in_specs=[pl.BlockSpec(memory_space=pltpu.SMEM), wide, narrow],
        out_specs=[wide, narrow],
        out_shape=[
            jax.ShapeDtypeStruct(state.shape, jnp.float32),
            jax.ShapeDtypeStruct(gradient.shape, jnp.bfloat16),
        ],
        compiler_params=pltpu.CompilerParams(
            dimension_semantics=("arbitrary",), vmem_limit_bytes=48 * 2**20
        ),
        cost_estimate=pl.CostEstimate(
            flops=20 * gradient.size, bytes_accessed=38 * gradient.size, transcendentals=0
        ),
        name="adam",
    )(factor.reshape(1, 1), state, gradient)


def swap(values, axis, bit):
    return lax.ppermute(
        values, axis, [(i, i ^ bit) for i in range(lax.axis_size(axis))]
    )


def bits_of(size):
    return [1 << k for k in reversed(range(size.bit_length() - 1))]


def later(values, *others):
    return lax.optimization_barrier((values,) + others)[0]


def tree_sum(terms):
    while len(terms) > 1:
        terms = [left + right for left, right in zip(terms[::2], terms[1::2])]
    return terms[0]


def sum_over(values, axis, step=1):
    others = range(step, lax.axis_size(axis), step)
    return tree_sum([values] + [swap(values, axis, other) for other in others])


def both(*values):
    return lax.optimization_barrier(values)


def gather_blocks(own, size):
    blocks = {0: own}
    for bit in bits_of(size):
        blocks.update({m | bit: swap(block, "chan", bit) for m, block in list(blocks.items())})
    return [blocks[m] for m in range(size)]


def lay_rows(blocks, room=1):
    rows = room * sum(block.shape[0] for block in blocks)
    return lay_more(jnp.zeros((rows,) + blocks[0].shape[1:], blocks[0].dtype), blocks, 0)


def lay_more(whole, blocks, start=None):
    if start is None:
        start = whole.shape[0] - sum(block.shape[0] for block in blocks)
    for block in blocks:
        whole = lax.dynamic_update_slice_in_dim(whole, block, start, axis=0)
        start += block.shape[0]
    return whole


def split_rows(mat, piece):
    return [mat[k * piece : (k + 1) * piece] for k in range(mat.shape[0] // piece)]


def scatter_near(partial, piece):
    blocks = dict(enumerate(split_rows(partial, piece)))
    came = []
    for bit in reversed(bits_of(len(blocks))):
        inward = {m: swap(blocks[m | bit], "chan", bit) for m in blocks if not m & bit}
        came += inward.values()
        blocks = {
            m: (blocks[m].astype(jnp.float32) + block.astype(jnp.float32)).astype(jnp.bfloat16)
            for m, block in inward.items()
        }
    return blocks[0], came


def rows_far(parts):
    return [part[part.shape[0] // 2 :] for part in parts]


def rows_near(parts):
    return [part[: part.shape[0] // 2] for part in parts]


def scatter_start(product, parts, size, piece, first=0):
    far = product(*parts).astype(jnp.bfloat16)
    total, came = scatter_near(far, piece)
    if first:
        sent = [swap(rows, "chan", size // 2) for rows in (total[:first], total[first:])]
    else:
        sent = swap(total, "chan", size // 2)
    return sent, came, far


def scatter_end(arrived, near, piece):
    total, _ = scatter_near(near, piece)
    return total.astype(jnp.float32) + arrived.astype(jnp.float32)


def block_diagonal(blocks):
    count, size, _ = blocks.shape
    return jnp.concatenate(
        [jnp.pad(blocks[k], ((0, 0), (k * size, (count - 1 - k) * size))) for k in range(count)],
        axis=0,
    )


def diagonal_blocks(matrix, count):
    size = matrix.shape[0] // count
    return jnp.stack(
        [matrix[k * size : (k + 1) * size, k * size : (k + 1) * size] for k in range(count)]
    )


def local(
    residual,
    cotangent,
    resets,
    branch_weights,
    gate_blocks,
    mixer_weights,
    expand_weights,
    shrink_weights,
    branch_state,
    gate_state,
    mixer_state,
    expand_state,
    shrink_state,
    channel_state,
    gains_state,
):
    seq_count = lax.axis_size("seq")
    group = lax.axis_size("chan") // SEQS
    seq_place = lax.axis_index("seq")
    chan_place = lax.axis_index("chan")
    place = (chan_place % group).astype(jnp.int32).reshape(1)
    width = residual.shape[1]
    piece = residual.shape[0]
    chan_width = branch_weights.shape[2]
    hidden_width = expand_weights.shape[2]
    block_count = gate_blocks.shape[1]

    def partner(values):
        return swap(values, "chan", group)

    def fetch_part(matrix):
        rows = matrix.shape[0] // seq_count
        return partner(lax.dynamic_slice_in_dim(matrix, seq_place * rows, rows, axis=0))

    def share(part):
        return lax.all_gather(part, "seq", axis=0, tiled=True)

    gains = gains_state[0]
    gain_first = 1.0 + gains[0]
    gain_second = 1.0 + gains[1]
    rows_float = residual.astype(jnp.float32)
    scale_one = lax.rsqrt(jnp.mean(rows_float * rows_float, axis=-1, keepdims=True) + norm_eps)
    normed_one = (rows_float * scale_one * gain_first).astype(jnp.bfloat16)
    side = group // 2
    own_branch = branch_weights.transpose(1, 2, 0)
    first_part = fetch_part(
        later(
            jnp.concatenate([own_branch.reshape(2 * chan_width, width), mixer_weights], axis=0),
            normed_one,
        )
    )
    half = piece // 2
    own_expand = expand_weights.reshape(width, 2 * hidden_width)
    normed_near = lay_rows(gather_blocks(normed_one, side), 2)
    normed_top, first_part, own_expand, normed_near = both(
        swap(normed_one[:half], "chan", side), first_part, own_expand, normed_near
    )
    others = share(first_part)
    other_branch = others[: 2 * chan_width].reshape(own_branch.shape)
    other_mixer = others[2 * chan_width :]
    branch_full = jnp.concatenate([own_branch, other_branch], axis=1)
    normed_end = swap(later(normed_one, normed_top)[half:], "chan", side)
    normed_far = gather_blocks(jnp.concatenate([normed_top, normed_end], axis=0), side)
    normed_all = lay_more(normed_near, normed_far)
    back_far = swap(later(cotangent, normed_end), "chan", side)
    expand_part = fetch_part(later(own_expand, normed_end))
    shrink_part = fetch_part(later(shrink_weights, normed_end))
    pair_width = 2 * hidden_width

    gate_full = jnp.concatenate([gate_blocks, partner(gate_blocks)], axis=1)
    rate_w = block_diagonal(gate_full[0])
    input_w = block_diagonal(gate_full[1])
    channel = channel_state[0]
    channel_full = jnp.concatenate([channel, partner(channel)], axis=1)
    speed = -lru_scale * jax.nn.softplus(channel_full[CONV + 3 :])
    params = jnp.concatenate([channel_full[: CONV + 3], speed], axis=0)

    flags = lax.dynamic_index_in_dim(
        resets.reshape(SEQS, SEQ_LEN), chan_place // group, axis=0, keepdims=False
    )
    stays = jnp.where(jnp.arange(SEQ_LEN) == 0, 0.0, 1.0 - (flags == 1).astype(jnp.float32))
    within = [stays]
    for offset in range(1, CONV - 1):
        within.append(within[-1] * jnp.pad(stays, (offset, 0))[:SEQ_LEN])
    masks = jnp.stack(within + [stays] * (SUB - len(within)), axis=1)

    mixed, gate_branch, recur_input, hidden, conv_low, rate, admit = lru_forward(
        place, normed_all, branch_full[0], branch_full[1], masks, rate_w, input_w, params, piece
    )
    mixed, back_far, expand_part = both(mixed, back_far, expand_part)
    mixer_full = jnp.concatenate([mixer_weights, other_mixer], axis=0)
    back_halves = [lay_rows(gather_blocks(half_of, side)) for half_of in (cotangent, back_far)]
    other_expand = share(expand_part)
    expand_full = jnp.concatenate(
        [
            own_expand[:, :hidden_width],
            other_expand[:, :hidden_width],
            own_expand[:, hidden_width:],
            other_expand[:, hidden_width:],
        ],
        axis=1,
    )
    through_mixer = lambda left: contract(left, mixer_full)
    arrived, came, _ = scatter_start(through_mixer, rows_far([mixed]), group, piece)
    near = through_mixer(*rows_near([later(mixed, *came)])).astype(jnp.bfloat16)
    arrived, shrink_part = both(arrived, shrink_part)
    middle = rows_float + scatter_end(arrived, near, piece)
    scale_two = lax.rsqrt(jnp.mean(middle * middle, axis=-1, keepdims=True) + norm_eps)
    normed_two = (middle * scale_two * gain_second).astype(jnp.bfloat16)
    shrink_full = lay_rows([shrink_weights, share(later(shrink_part, other_expand))])
    mlp_near = lay_rows(gather_blocks(normed_two, side))
    mlp_far = swap(normed_two, "chan", side)

    def mlp(rows, backs):
        expanded = contract(rows, expand_full)
        up_part = expanded[:, pair_width:]
        act_part, slope_part = gelu_parts(expanded[:, :pair_width])
        product_grad = contract_cols(backs, shrink_full)
        return (
            (act_part * up_part).astype(jnp.bfloat16),
            (product_grad * up_part * slope_part).astype(jnp.bfloat16),
            (product_grad * act_part).astype(jnp.bfloat16),
        )

    product_near, gate_near, up_near = mlp(mlp_near, back_halves[0])
    mlp_far, product_near, gate_near, up_near = both(mlp_far, product_near, gate_near, up_near)
    mlp_far = lay_rows(gather_blocks(mlp_far, side))
    product_far, gate_far, up_far = mlp(mlp_far, back_halves[1])

    def reduce_seq(matrix):
        return lax.psum_scatter(
            matrix.astype(jnp.bfloat16), "seq", scatter_dimension=0, tiled=True
        )

    def through_expand(*grads):
        return contract_cols(jnp.concatenate(grads, axis=1), expand_full)

    def through_shrink(left):
        return contract(left, shrink_full)

    arrived, came, _ = scatter_start(through_expand, [gate_far, up_far], group, piece)
    gate_far, up_far, product_far, *_ = both(gate_far, up_far, product_far, *came)
    expand_back = jnp.concatenate(
        [
            jnp.concatenate([gate_near, up_near], axis=1),
            jnp.concatenate([gate_far, up_far], axis=1),
        ],
        axis=0,
    )
    normed_mlp = lay_rows([mlp_near, mlp_far])
    expand_local = contract_rows(normed_mlp, expand_back).astype(jnp.bfloat16)
    arrived, expand_local, gate_near, up_near = both(arrived, expand_local, gate_near, up_near)
    near = through_expand(gate_near, up_near).astype(jnp.bfloat16)
    expand_sum = reduce_seq(expand_local)
    normed_two_grad = scatter_end(arrived, near, piece)
    back_float = cotangent.astype(jnp.float32)
    middle_grad = back_float + norm_back(middle, scale_two, gain_second, normed_two_grad)
    middle_low = middle_grad.astype(jnp.bfloat16)
    product_near, product_far = later(product_near, middle_low), later(product_far, middle_low)
    back_all = lay_rows(back_halves)
    product_low = lay_rows([product_near, product_far])
    shrink_local = contract_rows(back_all, product_low).astype(jnp.bfloat16)
    middle_near = lay_rows(gather_blocks(middle_low, side), 2)
    product_far = later(product_far, shrink_local)
    out_arrived, _, out_far = scatter_start(through_shrink, [product_far], group, piece)
    out_near = through_shrink(later(product_near, out_far)).astype(jnp.bfloat16)
    middle_far, shrink_local, middle_near, out_near, mixer_full = both(
        swap(middle_low, "chan", side), shrink_local, middle_near, out_near, mixer_full
    )
    shrink_sum = reduce_seq(shrink_local)
    branch_back = lay_more(middle_near, gather_blocks(middle_far, side))
    gain_two = jnp.sum(normed_two_grad * middle * scale_two, axis=0)

    def settle(part, pieces, each):
        mine = [part[:, 2 * k * each : (2 * k + 1) * each] for k in range(pieces)]
        theirs = [part[:, (2 * k + 1) * each : (2 * k + 2) * each] for k in range(pieces)]
        return jnp.concatenate(mine, axis=1), partner(jnp.concatenate(theirs, axis=1))

    def total(pair):
        return pair[0].astype(jnp.float32) + pair[1].astype(jnp.float32)

    mixer_local = contract_rows(branch_back, mixed).astype(jnp.bfloat16)
    mixer_sum = reduce_seq(mixer_local)
    expand_pair = settle(expand_sum, 2, hidden_width)
    gate_back, recur_back, rate_w_grad, input_w_grad, sums = lru_backward(
        place, later(branch_back, mixer_local), mixer_full, gate_branch, recur_input, hidden,
        conv_low, rate, admit, masks, rate_w, input_w, params, piece,
    )
    gate_back, out_arrived, expand_theirs = both(gate_back, out_arrived, expand_pair[1])
    expand_pair = (expand_pair[0], expand_theirs)
    branch_back_low = jnp.concatenate([gate_back, recur_back], axis=1)
    through_branch = lambda left: contract(left, branch_full.reshape(4 * chan_width, width))
    branch_local = contract_rows(normed_all, branch_back_low).astype(jnp.bfloat16)
    branch_back_low = later(branch_back_low, branch_local)
    arrived, _, far = scatter_start(
        through_branch, rows_far([branch_back_low]), group, piece, TILE
    )
    branch_back_low, arrived[0] = both(branch_back_low, arrived[0])
    arrived = jnp.concatenate(arrived, axis=0)
    block_size = gate_blocks.shape[2]
    part_rows = width // seq_count
    gate_pair = jnp.stack(
        [
            diagonal_blocks(rate_w_grad, 2 * block_count),
            diagonal_blocks(input_w_grad, 2 * block_count),
        ]
    ).astype(jnp.bfloat16)
    gate_parts = (2, 2, block_count, seq_count, block_size // seq_count, block_size)
    gate_pair = gate_pair.reshape(gate_parts).transpose(3, 1, 0, 2, 4, 5)
    gate_shape = gate_pair.shape[1:]
    gate_count = math.prod(gate_shape[:-1])
    gate_rows = jnp.pad(
        gate_pair.reshape(seq_count, gate_count, block_size),
        ((0, 0), (0, part_rows - gate_count), (0, 0)),
    ).reshape(width, block_size)
    branch_sum = reduce_seq(jnp.concatenate([branch_local, gate_rows], axis=1))
    shrink_pair = settle(later(shrink_sum, branch_local), 1, hidden_width)
    near = through_branch(*rows_near([branch_back_low])).astype(jnp.bfloat16)
    mixer_pair = settle(later(mixer_sum, near), 1, chan_width)
    sums = later(sums, branch_local)
    expand_grad = total(expand_pair).reshape(-1, 2, hidden_width)
    channel_pair = jnp.sum(sums, axis=1)
    channel_pair = jnp.concatenate(
        [
            channel_pair[: CONV + 3],
            channel_pair[CONV + 3 :] * -lru_scale * jax.nn.sigmoid(channel_full[CONV + 3 :]),
        ],
        axis=0,
    )
    channel_own = channel_pair[:, :chan_width] + partner(channel_pair[:, chan_width:])
    output = (middle + scatter_end(out_arrived, out_near, piece)).astype(jnp.bfloat16)
    normed_one_grad = scatter_end(arrived, near, piece)
    gain_one = jnp.sum(normed_one_grad * rows_float * scale_one, axis=0)
    residual_grad = middle_grad + norm_back(rows_float, scale_one, gain_first, normed_one_grad)
    (
        branch_sum, residual_grad, gain_one, gain_two, output, channel_own, shrink_theirs,
        mixer_theirs, expand_grad,
    ) = both(
        branch_sum, residual_grad, gain_one, gain_two, output, channel_own, shrink_pair[1],
        mixer_pair[1], expand_grad,
    )
    mixer_pair = (mixer_pair[0], mixer_theirs)
    shrink_pair = (shrink_pair[0], shrink_theirs)
    gate_part = branch_sum[:gate_count, 4 * chan_width :].reshape(gate_shape)
    gate_pair = (gate_part[0], partner(gate_part[1]))
    branch_pair = settle(branch_sum[:, : 4 * chan_width], 2, chan_width)
    shrink_grad = total(shrink_pair).T
    mixer_grad = total(mixer_pair).T
    branch_grad = total(branch_pair).reshape(-1, 2, chan_width)
    gate_grad = total(gate_pair)
    grad_shards = (branch_grad, gate_grad, mixer_grad, expand_grad, shrink_grad)
    own_squares = sum((jnp.sum(shard_grad * shard_grad) for shard_grad in grad_shards))
    lanes = 128
    packed = sum_over(
        jnp.concatenate(
            [
                gain_one,
                gain_two,
                jnp.full((lanes,), own_squares),
                channel_own.reshape(-1),
            ]
        ),
        "seq",
    )
    channel_grad = packed[2 * width + lanes :].reshape(channel_own.shape)
    packed = jnp.concatenate(
        [
            packed[: 2 * width],
            packed[2 * width : 2 * width + lanes] + jnp.sum(channel_grad * channel_grad),
        ]
    )
    packed = packed + swap(packed, "chan", 1)
    packed = sum_over(packed, "chan", 2)
    gains_grad = packed[: 2 * width].reshape(2, width)
    grad_norm = jnp.sqrt(packed[2 * width] + jnp.sum(gains_grad * gains_grad))
    clip_limit = clip_rms * math.sqrt(PARAMS)
    factor = jnp.minimum(1.0, clip_limit / (grad_norm + 1e-06))

    def rows_of_branch(values):
        return jnp.moveaxis(values, -3, -1).reshape(values.shape[:-3] + (2 * chan_width, part_rows))

    def branch_of_rows(values):
        return jnp.moveaxis(values.reshape(values.shape[:-2] + (2, chan_width, part_rows)), -1, -3)

    branch_new, branch_copy = map(
        branch_of_rows,
        adam_matrix(
            rows_of_branch(branch_state), rows_of_branch(branch_grad), factor, rate_matrix,
            weight_decay,
        ),
    )
    gate_rows_state = gate_state.reshape(4, -1, block_size)
    gate_new, gate_copy = adam_matrix(
        gate_rows_state, gate_grad.reshape(-1, block_size), factor, rate_gate, weight_decay
    )
    gate_new, gate_copy = gate_new.reshape(gate_state.shape), gate_copy.reshape(gate_grad.shape)
    mixer_new, mixer_copy = adam_matrix(mixer_state, mixer_grad, factor, rate_matrix, weight_decay)
    expand_new, expand_copy = adam_matrix(
        expand_state, expand_grad, factor, rate_matrix, weight_decay
    )
    shrink_new, shrink_copy = adam_matrix(
        shrink_state, shrink_grad, factor, rate_matrix, weight_decay
    )
    channel_all, _ = adam(channel_state, channel_grad, factor, rate_channel, 0.0)
    gains_new, _ = adam(gains_state, gains_grad, factor, rate_gains, 0.0)
    channel_new = jnp.stack([channel_all[0], channel_all[3]])
    channel_moments = channel_all[1:3]
    return (
        output,
        residual_grad,
        branch_grad,
        gate_grad,
        mixer_grad,
        expand_grad,
        shrink_grad,
        channel_grad,
        gains_grad,
        grad_norm,
        branch_new,
        gate_new,
        mixer_new,
        expand_new,
        shrink_new,
        channel_new,
        channel_moments,
        gains_new,
        branch_copy,
        gate_copy,
        mixer_copy,
        expand_copy,
        shrink_copy,
    )


def solution(mesh):
    in_specs = (
        P(("seq", "chan"), None),
        P(("seq", "chan"), None),
        P("seq"),
        P(None, None, "chan"),
        P(None, "chan", None, None),
        P("chan", None),
        P(None, None, "chan"),
        P("chan", None),
        P(None, "seq", None, "chan"),
        P(None, None, "chan", "seq", None),
        P(None, "chan", "seq"),
        P(None, "seq", None, "chan"),
        P(None, "chan", "seq"),
        P(None, None, "chan"),
        P(),
    )
    out_specs = (
        P(("seq", "chan"), None),
        P(("seq", "chan"), None),
        P("seq", None, "chan"),
        P(None, "chan", "seq", None),
        P("chan", "seq"),
        P("seq", None, "chan"),
        P("chan", "seq"),
        P(None, "chan"),
        P(),
        P(),
        P(None, "seq", None, "chan"),
        P(None, None, "chan", "seq", None),
        P(None, "chan", "seq"),
        P(None, "seq", None, "chan"),
        P(None, "chan", "seq"),
        P(None, None, "chan"),
        P(None, None, "chan"),
        P(),
        P("seq", None, "chan"),
        P(None, "chan", "seq", None),
        P("chan", "seq"),
        P("seq", None, "chan"),
        P("chan", "seq"),
    )
    return jax.shard_map(local, mesh=mesh, in_specs=in_specs, out_specs=out_specs, check_vma=False)
```

```python
import math

import jax
import jax.numpy as jnp
from jax import lax
from jax.experimental import pallas as pl
from jax.experimental.pallas import tpu as pltpu
from jax.sharding import PartitionSpec as P

CONV = 4
SEQ_LEN = 2048
SEQS = 2
STEP = 10
PARAMS = 54321152


norm_eps = 1e-06
lru_scale = 8.0
clip_rms = 0.4
beta_one = 0.9
beta_two = 0.95
adam_eps = 1e-08
weight_decay = 0.1
ema_keep = 0.99
rate_matrix = 0.02
rate_gate = 0.1
rate_channel = 1.0
rate_gains = 0.5
SUB = 8
TILE = 64
PARTS = TILE // SUB
GELU_SCALE = math.sqrt(2.0 / math.pi)
GELU_CUBE = 0.044715


def contract_rows(left_mat, right_mat):
    return lax.dot_general(
        left_mat, right_mat, (((0,), (0,)), ((), ())), preferred_element_type=jnp.float32
    )


def contract_cols(left_mat, right_mat):
    return lax.dot_general(
        left_mat, right_mat, (((1,), (1,)), ((), ())), preferred_element_type=jnp.float32
    )


def contract(left_mat, right_mat):
    return jnp.dot(left_mat, right_mat, preferred_element_type=jnp.float32)


def norm_back(values, scale, gain, upstream):
    scaled = gain * upstream
    return scale * scaled - values * scale * scale * scale * jnp.mean(
        scaled * values, axis=-1, keepdims=True
    )


def adam(old_state, gradient, factor, step_rate, decay_use):
    clipped = gradient * factor
    moment_one = beta_one * old_state[1] + (1.0 - beta_one) * clipped
    moment_two = beta_two * old_state[2] + (1.0 - beta_two) * clipped * clipped
    first_hat = moment_one / (1.0 - beta_one**STEP)
    second_hat = moment_two / (1.0 - beta_two**STEP)
    master = old_state[0] - step_rate * (
        first_hat / (jnp.sqrt(second_hat) + adam_eps) + decay_use * old_state[0]
    )
    average = ema_keep * old_state[3] + (1.0 - ema_keep) * master
    return (jnp.stack([master, moment_one, moment_two, average]), master)


def gelu_parts(values):
    square = values * values
    turn = jnp.tanh(GELU_SCALE * values * (1.0 + GELU_CUBE * square))
    half = 0.5 * (1.0 + turn)
    slope = half + 0.5 * values * (1.0 - turn * turn) * (
        GELU_SCALE * (1.0 + 3.0 * GELU_CUBE * square)
    )
    return values * half, slope


def decay_parts(log_decay):
    decay = jnp.exp(log_decay)
    z = 2.0 * log_decay
    series = 1.0 + z * (1.0 / 7.0)
    for order in (6.0, 5.0, 4.0, 3.0, 2.0):
        series = 1.0 + z * (1.0 / order) * series
    return decay, jnp.where(z > -0.35, -z * series, 1.0 - decay * decay)


def roll_down(values, offset):
    return pltpu.roll(values, offset, 0)


def roll_up(values, offset):
    return pltpu.roll(values, SUB - offset, 0)


def lru_forward_kernel(
    place_ref,
    normed_ref,
    gate_w_ref,
    recur_w_ref,
    mask_ref,
    rate_w_ref,
    input_w_ref,
    par_ref,
    mixed_ref,
    gate_ref,
    recur_ref,
    hidden_ref,
    conv_ref,
    rate_ref,
    admit_ref,
    rate_pre,
    input_pre,
    tail,
    state,
):
    block, width = gate_ref.shape

    @pl.when(pl.program_id(0) == 0)
    def _():
        tail[...] = jnp.zeros_like(tail)
        state[...] = jnp.zeros_like(state)

    normed = normed_ref[...]
    recur_ref[...] = contract_cols(normed, recur_w_ref[...])
    gate_ref[...] = contract_cols(normed, gate_w_ref[...])
    row = lax.broadcasted_iota(jnp.int32, (SUB, width), 0)

    def convolve(step, before):
        base = pl.multiple_of(step * TILE, TILE)
        halves = []
        for half in range(PARTS):
            rows = pl.ds(base + half * SUB, SUB)
            now = recur_ref[rows, :]
            masks = mask_ref[rows, :]
            total = par_ref[CONV : CONV + 1, :] + par_ref[0:1, :] * now
            for offset in range(1, CONV):
                moved = jnp.where(
                    row < offset, roll_down(before, offset), roll_down(now, offset)
                )
                total = total + par_ref[offset : offset + 1, :] * (
                    moved * masks[:, offset - 1 : offset]
                )
            halves.append(total)
            before = now
        conv_ref[pl.ds(base, TILE), :] = jnp.concatenate(halves, axis=0).astype(jnp.bfloat16)
        return before

    tail[...] = lax.fori_loop(0, block // TILE, convolve, tail[...])
    low = conv_ref[...]
    rate_pre[...] = contract(low, rate_w_ref[...])
    input_pre[...] = contract(low, input_w_ref[...])

    def advance(step, carry):
        base = pl.multiple_of(step * TILE, TILE)
        conv = conv_ref[pl.ds(base, TILE), :].astype(jnp.float32)
        halves = []
        for half in range(PARTS):
            rows = pl.ds(base + half * SUB, SUB)
            rate = jax.nn.sigmoid(rate_pre[rows, :] + par_ref[CONV + 1 : CONV + 2, :])
            admit = jax.nn.sigmoid(input_pre[rows, :] + par_ref[CONV + 2 : CONV + 3, :])
            decay, rest = decay_parts(par_ref[CONV + 3 : CONV + 4, :] * rate)
            coeff = decay * mask_ref[rows, 0:1]
            drive = jnp.sqrt(rest) * admit * conv[half * SUB : (half + 1) * SUB, :]
            for offset in (1, 2, 4):
                inner = row >= offset
                drive = drive + coeff * jnp.where(inner, roll_down(drive, offset), 0.0)
                coeff = coeff * jnp.where(inner, roll_down(coeff, offset), 1.0)
            hidden = drive + coeff * carry
            carry = jnp.broadcast_to(hidden[SUB - 1 : SUB, :], hidden.shape)
            hidden_ref[rows, :] = hidden
            rate_ref[rows, :] = rate
            admit_ref[rows, :] = admit
            branch = gate_ref[rows, :]
            turn = jnp.tanh(GELU_SCALE * branch * (1.0 + GELU_CUBE * branch * branch))
            halves.append(0.5 * branch * (1.0 + turn) * hidden)
        mixed_ref[pl.ds(base, TILE), :] = jnp.concatenate(halves, axis=0).astype(jnp.bfloat16)
        return carry

    state[...] = lax.fori_loop(0, block // TILE, advance, state[...])


def lru_backward_kernel(
    place_ref,
    back_ref,
    mixer_ref,
    gate_ref,
    recur_ref,
    hidden_ref,
    before_ref,
    conv_ref,
    rate_ref,
    admit_ref,
    mask_ref,
    rate_w_ref,
    input_w_ref,
    par_ref,
    gate_back_ref,
    recur_back_ref,
    rate_grad_ref,
    input_grad_ref,
    sums_ref,
    upstream_ref,
    rate_low,
    input_low,
    conv_back,
    state,
    ahead,
):
    block, width = gate_ref.shape
    steps = block // TILE

    @pl.when(pl.program_id(0) == 0)
    def _():
        state[...] = jnp.zeros_like(state)
        ahead[...] = jnp.zeros_like(ahead)
        sums_ref[...] = jnp.zeros_like(sums_ref)
        rate_grad_ref[...] = jnp.zeros_like(rate_grad_ref)
        input_grad_ref[...] = jnp.zeros_like(input_grad_ref)

    upstream_ref[...] = contract_cols(back_ref[...], mixer_ref[...])
    row = lax.broadcasted_iota(jnp.int32, (SUB, width), 0)

    def retreat(step, carry):
        carried_next, coeff_next = carry
        index = steps - 1 - step
        base = pl.multiple_of(index * TILE, TILE)
        conv_tile = conv_ref[pl.ds(base, TILE), :].astype(jnp.float32)
        lows = [[None] * PARTS for _ in range(3)]
        edge = pl.multiple_of(jnp.maximum(base - SUB, 0), SUB)
        earlier = jnp.where(index == 0, before_ref[...], hidden_ref[pl.ds(edge, SUB), :])
        for half in reversed(range(PARTS)):
            rows = pl.ds(base + half * SUB, SUB)
            conv = conv_tile[half * SUB : (half + 1) * SUB, :]
            rate = rate_ref[rows, :]
            admit = admit_ref[rows, :]
            speed = par_ref[CONV + 3 : CONV + 4, :]
            decay, rest = decay_parts(speed * rate)
            inverse = lax.rsqrt(rest)
            norm = rest * inverse
            coeff = decay * mask_ref[rows, 0:1]
            act, slope = gelu_parts(gate_ref[rows, :])
            upstream = upstream_ref[rows, :]
            hidden = hidden_ref[rows, :]
            carried = upstream * act
            chain = jnp.where(row == SUB - 1, coeff_next, roll_up(coeff, 1))
            for offset in (1, 2, 4):
                inner = row < SUB - offset
                carried = carried + chain * jnp.where(inner, roll_up(carried, offset), 0.0)
                chain = chain * jnp.where(inner, roll_up(chain, offset), 1.0)
            carried = carried + chain * carried_next
            carried_next = jnp.broadcast_to(carried[0:1, :], carried.shape)
            coeff_next = jnp.broadcast_to(coeff[0:1, :], coeff.shape)
            if half:
                last = hidden_ref[pl.ds(base + (half - 1) * SUB, SUB), :]
            else:
                last = earlier
            previous = jnp.where(row == 0, roll_down(last, 1), roll_down(hidden, 1))
            log_grad = carried * (
                previous * coeff - admit * conv * (decay * decay) * inverse
            )
            rate_back = log_grad * speed * rate * (1.0 - rate)
            drive = carried * norm
            direct = drive * admit
            input_back = drive * conv * admit * (1.0 - admit)
            conv_back[rows, :] = direct
            lows[0][half] = upstream * hidden * slope
            lows[1][half] = rate_back
            lows[2][half] = input_back
            sums_ref[5] += rate_back
            sums_ref[6] += input_back
            sums_ref[7] += log_grad * rate
        tile = pl.ds(base, TILE)
        gate_back_ref[tile, :] = jnp.concatenate(lows[0], axis=0).astype(jnp.bfloat16)
        rate_low[tile, :] = jnp.concatenate(lows[1], axis=0).astype(jnp.bfloat16)
        input_low[tile, :] = jnp.concatenate(lows[2], axis=0).astype(jnp.bfloat16)
        return carried_next, coeff_next

    carried_next, coeff_next = lax.fori_loop(0, steps, retreat, (state[0], state[1]))
    state[0] = carried_next
    state[1] = coeff_next
    low = conv_ref[...]
    rate_back_low = rate_low[...]
    input_back_low = input_low[...]
    rate_grad_ref[...] += contract_rows(low, rate_back_low)
    input_grad_ref[...] += contract_rows(low, input_back_low)
    conv_back[...] += contract_cols(rate_back_low, rate_w_ref[...]) + contract_cols(
        input_back_low, input_w_ref[...]
    )

    def unconvolve(step, carry):
        base = pl.multiple_of((steps - 1 - step) * TILE, TILE)
        halves = [None] * PARTS
        nexts = list(carry)
        for half in reversed(range(PARTS)):
            rows = pl.ds(base + half * SUB, SUB)
            grad = conv_back[rows, :]
            now = recur_ref[rows, :]
            masks = mask_ref[rows, :]
            sums_ref[0] += grad * now
            sums_ref[CONV] += grad
            total = par_ref[0:1, :] * grad
            for offset in range(1, CONV):
                kept = grad * masks[:, offset - 1 : offset]
                moved = jnp.where(
                    row < SUB - offset, roll_up(kept, offset), roll_up(nexts[offset - 1], offset)
                )
                nexts[offset - 1] = kept
                sums_ref[offset] += moved * now
                total = total + par_ref[offset : offset + 1, :] * moved
            halves[half] = total
        recur_back_ref[pl.ds(base, TILE), :] = jnp.concatenate(halves, axis=0).astype(jnp.bfloat16)
        return tuple(nexts)

    nexts = lax.fori_loop(0, steps, unconvolve, tuple(ahead[k] for k in range(CONV - 1)))
    for k in range(CONV - 1):
        ahead[k] = nexts[k]


def lru_sizes(rows, width, piece):
    block = min(256, piece)
    return block, rows // block, piece // block


def lru_forward(place, normed, gate_w, recur_w, masks, rate_w, input_w, params, piece):
    rows, depth = normed.shape
    width = gate_w.shape[0]
    block, count, per = lru_sizes(rows, width, piece)

    def there(i, place_ref):
        return (((i // per) ^ place_ref[0]) * per + i % per, 0)

    def here(i, place_ref):
        return (i, 0)

    def fixed(i, place_ref):
        return (0, 0)

    tall = lambda where: pl.BlockSpec((block, width), where)
    square = pl.BlockSpec((width, width), fixed)
    flat = pl.BlockSpec((width, depth), fixed)
    floats = jax.ShapeDtypeStruct((rows, width), jnp.float32)
    lows = jax.ShapeDtypeStruct((rows, width), jnp.bfloat16)
    return pl.pallas_call(
        lru_forward_kernel,
        grid_spec=pltpu.PrefetchScalarGridSpec(
            num_scalar_prefetch=1,
            grid=(count,),
            in_specs=[
                pl.BlockSpec((block, depth), there),
                flat,
                flat,
                pl.BlockSpec((block, SUB), here),
                square,
                square,
                pl.BlockSpec((2 * CONV, width), fixed),
            ],
            out_specs=[tall(there)] + [tall(here)] * 6,
            scratch_shapes=[
                pltpu.VMEM((block, width), jnp.float32),
                pltpu.VMEM((block, width), jnp.float32),
                pltpu.VMEM((SUB, width), jnp.float32),
                pltpu.VMEM((SUB, width), jnp.float32),
            ],
        ),
        out_shape=[lows, floats, floats, floats, lows, floats, floats],
        compiler_params=pltpu.CompilerParams(
            dimension_semantics=("arbitrary",), vmem_limit_bytes=48 * 2**20
        ),
        cost_estimate=pl.CostEstimate(
            flops=4 * rows * width * (width + depth),
            bytes_accessed=26 * rows * width + 2 * rows * depth,
            transcendentals=6 * rows * width,
        ),
        name="lru_forward",
    )(place, normed, gate_w, recur_w, masks, rate_w, input_w, params)


def lru_backward(
    place, back, mixer, gate_branch, recur_input, hidden, conv, rate, admit, masks, rate_w,
    input_w, params, piece,
):
    rows, depth = back.shape
    width = gate_branch.shape[1]
    block, count, per = lru_sizes(rows, width, piece)

    def there(i, place_ref):
        t = count - 1 - i
        return (((t // per) ^ place_ref[0]) * per + t % per, 0)

    def here(i, place_ref):
        return (count - 1 - i, 0)

    def before(i, place_ref):
        return (jnp.maximum((count - 1 - i) * (block // SUB) - 1, 0), 0)

    def fixed(i, place_ref):
        return (0, 0)

    tall = lambda where: pl.BlockSpec((block, width), where)
    square = pl.BlockSpec((width, width), fixed)
    return pl.pallas_call(
        lru_backward_kernel,
        grid_spec=pltpu.PrefetchScalarGridSpec(
            num_scalar_prefetch=1,
            grid=(count,),
            in_specs=[
                pl.BlockSpec((block, depth), there),
                pl.BlockSpec((width, depth), fixed),
                tall(here),
                tall(here),
                tall(here),
                pl.BlockSpec((SUB, width), before),
                tall(here),
                tall(here),
                tall(here),
                pl.BlockSpec((block, SUB), here),
                square,
                square,
                pl.BlockSpec((2 * CONV, width), fixed),
            ],
            out_specs=[
                tall(there),
                tall(there),
                square,
                square,
                pl.BlockSpec((2 * CONV, SUB, width), lambda i, place_ref: (0, 0, 0)),
            ],
            scratch_shapes=[
                pltpu.VMEM((block, width), jnp.float32),
                pltpu.VMEM((block, width), jnp.bfloat16),
                pltpu.VMEM((block, width), jnp.bfloat16),
                pltpu.VMEM((block, width), jnp.float32),
                pltpu.VMEM((2, SUB, width), jnp.float32),
                pltpu.VMEM((CONV - 1, SUB, width), jnp.float32),
            ],
        ),
        out_shape=[
            jax.ShapeDtypeStruct((rows, width), jnp.bfloat16),
            jax.ShapeDtypeStruct((rows, width), jnp.bfloat16),
            jax.ShapeDtypeStruct((width, width), jnp.float32),
            jax.ShapeDtypeStruct((width, width), jnp.float32),
            jax.ShapeDtypeStruct((2 * CONV, SUB, width), jnp.float32),
        ],
        compiler_params=pltpu.CompilerParams(
            dimension_semantics=("arbitrary",), vmem_limit_bytes=48 * 2**20
        ),
        cost_estimate=pl.CostEstimate(
            flops=8 * rows * width * width + 2 * rows * width * depth,
            bytes_accessed=30 * rows * width + 2 * rows * depth,
            transcendentals=6 * rows * width,
        ),
        name="lru_backward",
    )(
        place, back, mixer, gate_branch, recur_input, hidden, hidden, conv, rate, admit, masks,
        rate_w, input_w, params,
    )


def adam_kernel(step_rate, decay_use, factor_ref, state_ref, grad_ref, new_ref, copy_ref):
    clipped = grad_ref[...] * factor_ref[0, 0]
    master = state_ref[0]
    moment_one = beta_one * state_ref[1] + (1.0 - beta_one) * clipped
    moment_two = beta_two * state_ref[2] + (1.0 - beta_two) * clipped * clipped
    first_hat = moment_one * (1.0 / (1.0 - beta_one**STEP))
    second_hat = moment_two * (1.0 / (1.0 - beta_two**STEP))
    master = master - step_rate * (
        first_hat / (jnp.sqrt(second_hat) + adam_eps) + decay_use * master
    )
    new_ref[0] = master
    new_ref[1] = moment_one
    new_ref[2] = moment_two
    new_ref[3] = ema_keep * state_ref[3] + (1.0 - ema_keep) * master
    copy_ref[...] = master.astype(jnp.bfloat16)


def adam_matrix(state, gradient, factor, step_rate, decay_use):
    rows, rest = gradient.shape[0], gradient.shape[1:]
    goal = max(16, 2**17 // math.prod(rest))
    fits = [b for b in range(16, rows + 1, 16) if rows % b == 0 and (b <= goal or b == 16)]
    block = max(fits, default=rows)
    zeros = (0,) * len(rest)
    wide = pl.BlockSpec((4, block) + rest, lambda i: (0, i) + zeros)
    narrow = pl.BlockSpec((block,) + rest, lambda i: (i,) + zeros)
    return pl.pallas_call(
        lambda *refs: adam_kernel(step_rate, decay_use, *refs),
        grid=(rows // block,),
        in_specs=[pl.BlockSpec(memory_space=pltpu.SMEM), wide, narrow],
        out_specs=[wide, narrow],
        out_shape=[
            jax.ShapeDtypeStruct(state.shape, jnp.float32),
            jax.ShapeDtypeStruct(gradient.shape, jnp.bfloat16),
        ],
        compiler_params=pltpu.CompilerParams(
            dimension_semantics=("arbitrary",), vmem_limit_bytes=48 * 2**20
        ),
        cost_estimate=pl.CostEstimate(
            flops=20 * gradient.size, bytes_accessed=38 * gradient.size, transcendentals=0
        ),
        name="adam",
    )(factor.reshape(1, 1), state, gradient)


def swap(values, axis, bit):
    return lax.ppermute(
        values, axis, [(i, i ^ bit) for i in range(lax.axis_size(axis))]
    )


def bits_of(size):
    return [1 << k for k in reversed(range(size.bit_length() - 1))]


def later(values, *others):
    return lax.optimization_barrier((values,) + others)[0]


def tree_sum(terms):
    while len(terms) > 1:
        terms = [left + right for left, right in zip(terms[::2], terms[1::2])]
    return terms[0]


def sum_over(values, axis, step=1):
    others = range(step, lax.axis_size(axis), step)
    return tree_sum([values] + [swap(values, axis, other) for other in others])


def both(*values):
    return lax.optimization_barrier(values)


def gather_blocks(own, size):
    blocks = {0: own}
    for bit in bits_of(size):
        blocks.update({m | bit: swap(block, "chan", bit) for m, block in list(blocks.items())})
    return [blocks[m] for m in range(size)]


def lay_rows(blocks, room=1):
    rows = room * sum(block.shape[0] for block in blocks)
    return lay_more(jnp.zeros((rows,) + blocks[0].shape[1:], blocks[0].dtype), blocks, 0)


def lay_more(whole, blocks, start=None):
    if start is None:
        start = whole.shape[0] - sum(block.shape[0] for block in blocks)
    for block in blocks:
        whole = lax.dynamic_update_slice_in_dim(whole, block, start, axis=0)
        start += block.shape[0]
    return whole


def split_rows(mat, piece):
    return [mat[k * piece : (k + 1) * piece] for k in range(mat.shape[0] // piece)]


def scatter_near(partial, piece):
    blocks = dict(enumerate(split_rows(partial, piece)))
    came = []
    for bit in reversed(bits_of(len(blocks))):
        inward = {m: swap(blocks[m | bit], "chan", bit) for m in blocks if not m & bit}
        came += inward.values()
        blocks = {
            m: (blocks[m].astype(jnp.float32) + block.astype(jnp.float32)).astype(jnp.bfloat16)
            for m, block in inward.items()
        }
    return blocks[0], came


def rows_far(parts):
    return [part[part.shape[0] // 2 :] for part in parts]


def rows_near(parts):
    return [part[: part.shape[0] // 2] for part in parts]


def scatter_start(product, parts, size, piece, first=0):
    far = product(*parts).astype(jnp.bfloat16)
    total, came = scatter_near(far, piece)
    if first:
        sent = [swap(rows, "chan", size // 2) for rows in (total[:first], total[first:])]
    else:
        sent = swap(total, "chan", size // 2)
    return sent, came, far


def scatter_end(arrived, near, piece):
    total, _ = scatter_near(near, piece)
    return total.astype(jnp.float32) + arrived.astype(jnp.float32)


def block_diagonal(blocks):
    count, size, _ = blocks.shape
    return jnp.concatenate(
        [jnp.pad(blocks[k], ((0, 0), (k * size, (count - 1 - k) * size))) for k in range(count)],
        axis=0,
    )


def diagonal_blocks(matrix, count):
    size = matrix.shape[0] // count
    return jnp.stack(
        [matrix[k * size : (k + 1) * size, k * size : (k + 1) * size] for k in range(count)]
    )


def local(
    residual,
    cotangent,
    resets,
    branch_weights,
    gate_blocks,
    mixer_weights,
    expand_weights,
    shrink_weights,
    branch_state,
    gate_state,
    mixer_state,
    expand_state,
    shrink_state,
    channel_state,
    gains_state,
):
    seq_count = lax.axis_size("seq")
    group = lax.axis_size("chan") // SEQS
    seq_place = lax.axis_index("seq")
    chan_place = lax.axis_index("chan")
    place = (chan_place % group).astype(jnp.int32).reshape(1)
    width = residual.shape[1]
    piece = residual.shape[0]
    chan_width = branch_weights.shape[2]
    hidden_width = expand_weights.shape[2]
    block_count = gate_blocks.shape[1]

    def partner(values):
        return swap(values, "chan", group)

    def fetch_part(matrix):
        rows = matrix.shape[0] // seq_count
        return partner(lax.dynamic_slice_in_dim(matrix, seq_place * rows, rows, axis=0))

    def share(part):
        return lax.all_gather(part, "seq", axis=0, tiled=True)

    gains = gains_state[0]
    gain_first = 1.0 + gains[0]
    gain_second = 1.0 + gains[1]
    rows_float = residual.astype(jnp.float32)
    scale_one = lax.rsqrt(jnp.mean(rows_float * rows_float, axis=-1, keepdims=True) + norm_eps)
    normed_one = (rows_float * scale_one * gain_first).astype(jnp.bfloat16)
    side = group // 2
    own_branch = branch_weights.transpose(1, 2, 0)
    first_part = fetch_part(
        later(
            jnp.concatenate([own_branch.reshape(2 * chan_width, width), mixer_weights], axis=0),
            normed_one,
        )
    )
    half = piece // 2
    own_expand = expand_weights.reshape(width, 2 * hidden_width)
    normed_near = lay_rows(gather_blocks(normed_one, side), 2)
    normed_top, first_part, own_expand, normed_near = both(
        swap(normed_one[:half], "chan", side), first_part, own_expand, normed_near
    )
    others = share(first_part)
    other_branch = others[: 2 * chan_width].reshape(own_branch.shape)
    other_mixer = others[2 * chan_width :]
    branch_full = jnp.concatenate([own_branch, other_branch], axis=1)
    normed_end = swap(later(normed_one, normed_top)[half:], "chan", side)
    normed_far = gather_blocks(jnp.concatenate([normed_top, normed_end], axis=0), side)
    normed_all = lay_more(normed_near, normed_far)
    back_far = swap(later(cotangent, normed_end), "chan", side)
    expand_part = fetch_part(later(own_expand, normed_end))
    shrink_part = fetch_part(later(shrink_weights, normed_end))
    pair_width = 2 * hidden_width

    gate_full = jnp.concatenate([gate_blocks, partner(gate_blocks)], axis=1)
    rate_w = block_diagonal(gate_full[0])
    input_w = block_diagonal(gate_full[1])
    channel = channel_state[0]
    channel_full = jnp.concatenate([channel, partner(channel)], axis=1)
    speed = -lru_scale * jax.nn.softplus(channel_full[CONV + 3 :])
    params = jnp.concatenate([channel_full[: CONV + 3], speed], axis=0)

    flags = lax.dynamic_index_in_dim(
        resets.reshape(SEQS, SEQ_LEN), chan_place // group, axis=0, keepdims=False
    )
    stays = jnp.where(jnp.arange(SEQ_LEN) == 0, 0.0, 1.0 - (flags == 1).astype(jnp.float32))
    within = [stays]
    for offset in range(1, CONV - 1):
        within.append(within[-1] * jnp.pad(stays, (offset, 0))[:SEQ_LEN])
    masks = jnp.stack(within + [stays] * (SUB - len(within)), axis=1)

    mixed, gate_branch, recur_input, hidden, conv_low, rate, admit = lru_forward(
        place, normed_all, branch_full[0], branch_full[1], masks, rate_w, input_w, params, piece
    )
    mixed, back_far, expand_part = both(mixed, back_far, expand_part)
    mixer_full = jnp.concatenate([mixer_weights, other_mixer], axis=0)
    back_halves = [lay_rows(gather_blocks(half_of, side)) for half_of in (cotangent, back_far)]
    other_expand = share(expand_part)
    expand_full = jnp.concatenate(
        [
            own_expand[:, :hidden_width],
            other_expand[:, :hidden_width],
            own_expand[:, hidden_width:],
            other_expand[:, hidden_width:],
        ],
        axis=1,
    )
    through_mixer = lambda left: contract(left, mixer_full)
    arrived, came, _ = scatter_start(through_mixer, rows_far([mixed]), group, piece)
    near = through_mixer(*rows_near([later(mixed, *came)])).astype(jnp.bfloat16)
    arrived, shrink_part = both(arrived, shrink_part)
    middle = rows_float + scatter_end(arrived, near, piece)
    scale_two = lax.rsqrt(jnp.mean(middle * middle, axis=-1, keepdims=True) + norm_eps)
    normed_two = (middle * scale_two * gain_second).astype(jnp.bfloat16)
    shrink_full = lay_rows([shrink_weights, share(later(shrink_part, other_expand))])
    mlp_near = lay_rows(gather_blocks(normed_two, side))
    mlp_far = swap(normed_two, "chan", side)

    def mlp(rows, backs):
        expanded = contract(rows, expand_full)
        up_part = expanded[:, pair_width:]
        act_part, slope_part = gelu_parts(expanded[:, :pair_width])
        product_grad = contract_cols(backs, shrink_full)
        return (
            (act_part * up_part).astype(jnp.bfloat16),
            (product_grad * up_part * slope_part).astype(jnp.bfloat16),
            (product_grad * act_part).astype(jnp.bfloat16),
        )

    product_near, gate_near, up_near = mlp(mlp_near, back_halves[0])
    mlp_far, product_near, gate_near, up_near = both(mlp_far, product_near, gate_near, up_near)
    mlp_far = lay_rows(gather_blocks(mlp_far, side))
    product_far, gate_far, up_far = mlp(mlp_far, back_halves[1])

    def reduce_seq(matrix):
        return lax.psum_scatter(
            matrix.astype(jnp.bfloat16), "seq", scatter_dimension=0, tiled=True
        )

    def through_expand(*grads):
        return contract_cols(jnp.concatenate(grads, axis=1), expand_full)

    def through_shrink(left):
        return contract(left, shrink_full)

    arrived, came, _ = scatter_start(through_expand, [gate_far, up_far], group, piece)
    gate_far, up_far, product_far, *_ = both(gate_far, up_far, product_far, *came)
    expand_back = jnp.concatenate(
        [
            jnp.concatenate([gate_near, up_near], axis=1),
            jnp.concatenate([gate_far, up_far], axis=1),
        ],
        axis=0,
    )
    normed_mlp = lay_rows([mlp_near, mlp_far])
    expand_local = contract_rows(normed_mlp, expand_back).astype(jnp.bfloat16)
    arrived, expand_local, gate_near, up_near = both(arrived, expand_local, gate_near, up_near)
    near = through_expand(gate_near, up_near).astype(jnp.bfloat16)
    expand_sum = reduce_seq(expand_local)
    normed_two_grad = scatter_end(arrived, near, piece)
    back_float = cotangent.astype(jnp.float32)
    middle_grad = back_float + norm_back(middle, scale_two, gain_second, normed_two_grad)
    middle_low = middle_grad.astype(jnp.bfloat16)
    product_near, product_far = later(product_near, middle_low), later(product_far, middle_low)
    back_all = lay_rows(back_halves)
    product_low = lay_rows([product_near, product_far])
    shrink_local = contract_rows(back_all, product_low).astype(jnp.bfloat16)
    middle_near = lay_rows(gather_blocks(middle_low, side), 2)
    product_far = later(product_far, shrink_local)
    out_arrived, _, out_far = scatter_start(through_shrink, [product_far], group, piece)
    out_near = through_shrink(later(product_near, out_far)).astype(jnp.bfloat16)
    middle_far, shrink_local, middle_near, out_near, mixer_full = both(
        swap(middle_low, "chan", side), shrink_local, middle_near, out_near, mixer_full
    )
    branch_back = lay_more(middle_near, gather_blocks(middle_far, side))
    gain_two = jnp.sum(normed_two_grad * middle * scale_two, axis=0)

    def settle(part, pieces, each):
        mine = [part[:, 2 * k * each : (2 * k + 1) * each] for k in range(pieces)]
        theirs = [part[:, (2 * k + 1) * each : (2 * k + 2) * each] for k in range(pieces)]
        return jnp.concatenate(mine, axis=1), partner(jnp.concatenate(theirs, axis=1))

    def total(pair):
        return pair[0].astype(jnp.float32) + pair[1].astype(jnp.float32)

    mixer_local = contract_rows(branch_back, mixed).astype(jnp.bfloat16)
    units_sum = reduce_seq(jnp.concatenate([shrink_local, mixer_local], axis=1))
    expand_pair = settle(expand_sum, 2, hidden_width)
    gate_back, recur_back, rate_w_grad, input_w_grad, sums = lru_backward(
        place, later(branch_back, mixer_local), mixer_full, gate_branch, recur_input, hidden,
        conv_low, rate, admit, masks, rate_w, input_w, params, piece,
    )
    gate_back, out_arrived, expand_theirs = both(gate_back, out_arrived, expand_pair[1])
    expand_pair = (expand_pair[0], expand_theirs)
    branch_back_low = jnp.concatenate([gate_back, recur_back], axis=1)
    through_branch = lambda left: contract(left, branch_full.reshape(4 * chan_width, width))
    branch_local = contract_rows(normed_all, branch_back_low).astype(jnp.bfloat16)
    branch_back_low = later(branch_back_low, branch_local)
    arrived, _, far = scatter_start(
        through_branch, rows_far([branch_back_low]), group, piece, TILE
    )
    branch_back_low, arrived[0] = both(branch_back_low, arrived[0])
    arrived = jnp.concatenate(arrived, axis=0)
    block_size = gate_blocks.shape[2]
    part_rows = width // seq_count
    gate_pair = jnp.stack(
        [
            diagonal_blocks(rate_w_grad, 2 * block_count),
            diagonal_blocks(input_w_grad, 2 * block_count),
        ]
    ).astype(jnp.bfloat16)
    gate_parts = (2, 2, block_count, seq_count, block_size // seq_count, block_size)
    gate_pair = gate_pair.reshape(gate_parts).transpose(3, 1, 0, 2, 4, 5)
    gate_shape = gate_pair.shape[1:]
    gate_count = math.prod(gate_shape[:-1])
    gate_rows = jnp.pad(
        gate_pair.reshape(seq_count, gate_count, block_size),
        ((0, 0), (0, part_rows - gate_count), (0, 0)),
    ).reshape(width, block_size)
    branch_sum = reduce_seq(jnp.concatenate([branch_local, gate_rows], axis=1))
    units_sum = later(units_sum, branch_local)
    shrink_pair = settle(units_sum[:, :pair_width], 1, hidden_width)
    near = through_branch(*rows_near([branch_back_low])).astype(jnp.bfloat16)
    mixer_pair = settle(units_sum[:, pair_width:], 1, chan_width)
    sums = later(sums, branch_local)
    expand_grad = total(expand_pair).reshape(-1, 2, hidden_width)
    channel_pair = jnp.sum(sums, axis=1)
    channel_pair = jnp.concatenate(
        [
            channel_pair[: CONV + 3],
            channel_pair[CONV + 3 :] * -lru_scale * jax.nn.sigmoid(channel_full[CONV + 3 :]),
        ],
        axis=0,
    )
    channel_own = channel_pair[:, :chan_width] + partner(channel_pair[:, chan_width:])
    output = (middle + scatter_end(out_arrived, out_near, piece)).astype(jnp.bfloat16)
    normed_one_grad = scatter_end(arrived, near, piece)
    gain_one = jnp.sum(normed_one_grad * rows_float * scale_one, axis=0)
    residual_grad = middle_grad + norm_back(rows_float, scale_one, gain_first, normed_one_grad)
    (
        branch_sum, residual_grad, gain_one, gain_two, output, channel_own, shrink_theirs,
        mixer_theirs, expand_grad,
    ) = both(
        branch_sum, residual_grad, gain_one, gain_two, output, channel_own, shrink_pair[1],
        mixer_pair[1], expand_grad,
    )
    mixer_pair = (mixer_pair[0], mixer_theirs)
    shrink_pair = (shrink_pair[0], shrink_theirs)
    gate_part = branch_sum[:gate_count, 4 * chan_width :].reshape(gate_shape)
    gate_pair = (gate_part[0], partner(gate_part[1]))
    branch_pair = settle(branch_sum[:, : 4 * chan_width], 2, chan_width)
    shrink_grad = total(shrink_pair).T
    mixer_grad = total(mixer_pair).T
    branch_grad = total(branch_pair).reshape(-1, 2, chan_width)
    gate_grad = total(gate_pair)
    grad_shards = (branch_grad, gate_grad, mixer_grad, expand_grad, shrink_grad)
    own_squares = sum((jnp.sum(shard_grad * shard_grad) for shard_grad in grad_shards))
    lanes = 128
    packed = sum_over(
        jnp.concatenate(
            [
                gain_one,
                gain_two,
                jnp.full((lanes,), own_squares),
                channel_own.reshape(-1),
            ]
        ),
        "seq",
    )
    channel_grad = packed[2 * width + lanes :].reshape(channel_own.shape)
    packed = jnp.concatenate(
        [
            packed[: 2 * width],
            packed[2 * width : 2 * width + lanes] + jnp.sum(channel_grad * channel_grad),
        ]
    )
    packed = packed + swap(packed, "chan", 1)
    packed = sum_over(packed, "chan", 2)
    gains_grad = packed[: 2 * width].reshape(2, width)
    grad_norm = jnp.sqrt(packed[2 * width] + jnp.sum(gains_grad * gains_grad))
    clip_limit = clip_rms * math.sqrt(PARAMS)
    factor = jnp.minimum(1.0, clip_limit / (grad_norm + 1e-06))

    def rows_of_branch(values):
        return jnp.moveaxis(values, -3, -1).reshape(values.shape[:-3] + (2 * chan_width, part_rows))

    def branch_of_rows(values):
        return jnp.moveaxis(values.reshape(values.shape[:-2] + (2, chan_width, part_rows)), -1, -3)

    branch_new, branch_copy = map(
        branch_of_rows,
        adam_matrix(
            rows_of_branch(branch_state), rows_of_branch(branch_grad), factor, rate_matrix,
            weight_decay,
        ),
    )
    gate_rows_state = gate_state.reshape(4, -1, block_size)
    gate_new, gate_copy = adam_matrix(
        gate_rows_state, gate_grad.reshape(-1, block_size), factor, rate_gate, weight_decay
    )
    gate_new, gate_copy = gate_new.reshape(gate_state.shape), gate_copy.reshape(gate_grad.shape)
    mixer_new, mixer_copy = adam_matrix(mixer_state, mixer_grad, factor, rate_matrix, weight_decay)
    expand_new, expand_copy = adam_matrix(
        expand_state, expand_grad, factor, rate_matrix, weight_decay
    )
    shrink_new, shrink_copy = adam_matrix(
        shrink_state, shrink_grad, factor, rate_matrix, weight_decay
    )
    channel_all, _ = adam(channel_state, channel_grad, factor, rate_channel, 0.0)
    gains_new, _ = adam(gains_state, gains_grad, factor, rate_gains, 0.0)
    channel_new = jnp.stack([channel_all[0], channel_all[3]])
    channel_moments = channel_all[1:3]
    return (
        output,
        residual_grad,
        branch_grad,
        gate_grad,
        mixer_grad,
        expand_grad,
        shrink_grad,
        channel_grad,
        gains_grad,
        grad_norm,
        branch_new,
        gate_new,
        mixer_new,
        expand_new,
        shrink_new,
        channel_new,
        channel_moments,
        gains_new,
        branch_copy,
        gate_copy,
        mixer_copy,
        expand_copy,
        shrink_copy,
    )


def solution(mesh):
    in_specs = (
        P(("seq", "chan"), None),
        P(("seq", "chan"), None),
        P("seq"),
        P(None, None, "chan"),
        P(None, "chan", None, None),
        P("chan", None),
        P(None, None, "chan"),
        P("chan", None),
        P(None, "seq", None, "chan"),
        P(None, None, "chan", "seq", None),
        P(None, "chan", "seq"),
        P(None, "seq", None, "chan"),
        P(None, "chan", "seq"),
        P(None, None, "chan"),
        P(),
    )
    out_specs = (
        P(("seq", "chan"), None),
        P(("seq", "chan"), None),
        P("seq", None, "chan"),
        P(None, "chan", "seq", None),
        P("chan", "seq"),
        P("seq", None, "chan"),
        P("chan", "seq"),
        P(None, "chan"),
        P(),
        P(),
        P(None, "seq", None, "chan"),
        P(None, None, "chan", "seq", None),
        P(None, "chan", "seq"),
        P(None, "seq", None, "chan"),
        P(None, "chan", "seq"),
        P(None, None, "chan"),
        P(None, None, "chan"),
        P(),
        P("seq", None, "chan"),
        P(None, "chan", "seq", None),
        P("chan", "seq"),
        P("seq", None, "chan"),
        P("chan", "seq"),
    )
    return jax.shard_map(local, mesh=mesh, in_specs=in_specs, out_specs=out_specs, check_vma=False)
```
